32 devices in a mesh: segment: 2 (over core), dp: 4 (over y, x), space: 4 (over z).
Axes of the slice: x: 2, y: 2, z: 4, core: 2. Of those that a mesh axis runs over, the one named last changes fastest.
Arguments:
- inputs: bfloat16 [4, 8, 8, 8, 16, 528], P(None, 'dp', None, 'space'), may hold values from -6 to 6
- crop_group: int32 [4], replicated, may hold values from 0 to 2, as said below
- in_proj_4f: bfloat16 [528, 576], replicated, may hold values from -0.25 to 0.25
- conv_a_4f: bfloat16 [3, 3, 3, 160, 320], replicated, may hold values from -0.09375 to 0.09375
- conv_b_4f: bfloat16 [3, 3, 3, 32, 128], replicated, may hold values from -0.21875 to 0.21875
- gain_4f: float32 [1024], replicated, may hold values from 0.1 to 1.9
- bias_4f: float32 [1024], replicated, may hold values from -3 to 3
- in_proj_5b: bfloat16 [832, 576], replicated, may hold values from -0.21875 to 0.21875
- conv_a_5b: bfloat16 [3, 3, 3, 160, 320], replicated, may hold values from -0.09375 to 0.09375
- conv_b_5b: bfloat16 [3, 3, 3, 32, 128], replicated, may hold values from -0.21875 to 0.21875
- gain_5b: float32 [1024], replicated, may hold values from 0.1 to 1.9
- bias_5b: float32 [1024], replicated, may hold values from -3 to 3
- out_grad: bfloat16 [4, 8, 4, 4, 8, 832], P(None, 'dp', None, 'space'), may hold values from -6 to 6
Outputs:
- block_out: bfloat16 [4, 8, 4, 4, 8, 832], P('segment', 'dp', None, 'space')
- input_grad: float32 [4, 8, 8, 8, 16, 528], P('segment', 'dp', None, 'space')
- grad_in_proj_4f: float32 [528, 576], replicated
- grad_conv_a_4f: float32 [3, 3, 3, 160, 320], replicated
- grad_conv_b_4f: float32 [3, 3, 3, 32, 128], replicated
- grad_gain_4f: float32 [1024], replicated
- grad_bias_4f: float32 [1024], replicated
- grad_in_proj_5b: float32 [832, 576], replicated
- grad_conv_a_5b: float32 [3, 3, 3, 160, 320], replicated
- grad_conv_b_5b: float32 [3, 3, 3, 32, 128], replicated
- grad_gain_5b: float32 [1024], replicated
- grad_bias_5b: float32 [1024], replicated
The draws below stay inside these ranges and needn't reach their ends.
Inputs may be any that keep to these rules, and one draw needn't show every extreme that they name: `crop_group`: some micro-batch has group 0 and some has group 2.
All inputs are finite; a program needn't handle non-finite values.
Results may differ from the reference program's by a relative error of at most 0.022.
Values may be sent and summed in bfloat16 or wider, within the bound.
No kernel may reach another device: no remote copies, remote signals or barrier semaphores. Data moves between devices by JAX's collectives and lax.ppermute only.
A program may use at most 128 MiB of HBM per device.

```python
import jax
import jax.numpy as jnp
from jax import lax

C_IN = 528
B0 = 256
B1R = 160
B1 = 320
B2R = 32
B2 = 128
BP = 128
FRAMES = 8
COLUMNS = 16
MICRO = 4
CROPS = 3
C_MID = 832
FIRST = 576
NORM = 1024
CLIPS = 8
ROWS = 8


def draw_crop_group(key, part):
    key = jax.random.fold_in(key, 11)
    group_key, order_key = jax.random.split(key)
    groups = jax.random.randint(group_key, (MICRO,), 0, CROPS)
    order = jax.random.permutation(order_key, MICRO)
    groups = groups.at[order[0]].set(0)
    groups = groups.at[order[1]].set(CROPS - 1)
    return groups.astype(jnp.int32)


def block_levels(stream_key, extent, shards, smallest, largest):
    loudness, own = 1.0, jax.random.fold_in(stream_key, 6)
    for dim, shards_of in shards:
        heights = jnp.exp(jax.random.uniform(jax.random.fold_in(own, dim), (shards_of,), jnp.float32, smallest / len(shards), largest / len(shards)))
        loudness = loudness * jnp.repeat(heights, extent[dim] // shards_of).reshape([-1 if axis == dim else 1 for axis in range(len(extent))])
    return loudness


def noise(own_key, shape, scale, most, cuts=(), dtype=jnp.bfloat16):
    level = block_levels(own_key, shape, cuts, -0.22, 0.18) if cuts else 1.0
    drawn = jax.random.normal(own_key, shape, jnp.float32) * scale * level
    return jnp.minimum(jnp.maximum(drawn, -most), most).astype(dtype)


def setup_inputs(seed: int = 0) -> dict:
    arg_keys = jax.random.split(jax.random.key(seed), 14)
    inputs = noise(arg_keys[0], (MICRO, CLIPS, FRAMES, ROWS, COLUMNS, C_IN), 1.0, 6.0, ((1, 4), (3, 4)))
    crop_group = draw_crop_group(jax.random.fold_in(arg_keys[13], 71), 0)
    in_proj_4f = noise(arg_keys[2], (C_IN, FIRST), C_IN ** -0.5, 0.25)
    conv_a_4f = noise(arg_keys[3], (3, 3, 3, B1R, B1), (27 * B1R) ** -0.5, 0.09375)
    conv_b_4f = noise(arg_keys[4], (3, 3, 3, B2R, B2), (27 * B2R) ** -0.5, 0.21875)
    gain_4f = jnp.clip(1.0 + 0.18 * jax.random.normal(arg_keys[5], (NORM,), jnp.float32), 0.1, 1.9)
    bias_4f = noise(arg_keys[6], (NORM,), 0.5, 3.0, (), jnp.float32)
    in_proj_5b = noise(arg_keys[7], (C_MID, FIRST), C_MID ** -0.5, 0.21875)
    conv_a_5b = noise(arg_keys[8], (3, 3, 3, B1R, B1), (27 * B1R) ** -0.5, 0.09375)
    conv_b_5b = noise(arg_keys[9], (3, 3, 3, B2R, B2), (27 * B2R) ** -0.5, 0.21875)
    gain_5b = jnp.clip(1.0 + 0.18 * jax.random.normal(arg_keys[10], (NORM,), jnp.float32), 0.1, 1.9)
    bias_5b = noise(arg_keys[11], (NORM,), 0.5, 3.0, (), jnp.float32)
    out_grad = noise(arg_keys[12], (MICRO, CLIPS, FRAMES // 2, ROWS // 2, COLUMNS // 2, C_MID), 1.0, 6.0, ((1, 4), (3, 4)))
    return dict(inputs=inputs, crop_group=crop_group, in_proj_4f=in_proj_4f, conv_a_4f=conv_a_4f, conv_b_4f=conv_b_4f, gain_4f=gain_4f, bias_4f=bias_4f, in_proj_5b=in_proj_5b, conv_a_5b=conv_a_5b, conv_b_5b=conv_b_5b, gain_5b=gain_5b, bias_5b=bias_5b, out_grad=out_grad)


@jax.custom_vjp
def low(v):
    return lax.optimization_barrier(v.astype(jnp.bfloat16)).astype(jnp.float32)

@jax.custom_vjp
def low_back(v):
    return v

def low_keep(v):
    return (low(v), None)

def low_pass(kept, grad):
    return (grad,)

def back_keep(v):
    return (v, None)

def back_low(kept, grad):
    return (low(grad),)
low.defvjp(low_keep, low_pass)
low_back.defvjp(back_keep, back_low)
epsilon = 0.001

def neighbour_sum(values, axis):
    size = values.shape[axis]
    widths = [(1, 1) if position == axis else (0, 0) for position in range(values.ndim)]
    padded = jnp.pad(values, widths)
    return lax.slice_in_dim(padded, 0, size, axis=axis) + lax.slice_in_dim(padded, 1, size + 1, axis=axis) + lax.slice_in_dim(padded, 2, size + 2, axis=axis)

def box_mean(values):
    return neighbour_sum(neighbour_sum(neighbour_sum(values, 1), 2), 3) / 27.0

def conv_cube(values, kernel):
    return lax.conv_general_dilated(values, kernel, (1, 1, 1), 'SAME', dimension_numbers=('NDHWC', 'DHWIO', 'NDHWC'), precision=lax.Precision.HIGHEST)

def crop_mask(group, full_rows, full_width, clips, frames):
    height = full_rows - group * (full_rows // 4)
    across = full_width - group * (full_width // 4)
    keep = (jnp.arange(full_rows)[:, None] < height) & (jnp.arange(full_width)[None, :] < across)
    mask = keep.astype(jnp.float32)[None, None, :, :, None]
    count = (clips * frames * height * across).astype(jnp.float32)
    return (mask, count)

def norm_act(values, mask, count, gain, bias):
    mean = lax.optimization_barrier(jnp.sum(values * mask, axis=(0, 1, 2, 3))) / count
    variance = lax.optimization_barrier(jnp.sum(values * values * mask, axis=(0, 1, 2, 3))) / count - mean * mean
    scale = lax.rsqrt(variance + epsilon)
    return jax.nn.silu((values - mean) * scale * gain + bias) * mask

def pool_pairs(values):
    clips, frames, rows, width, channels = values.shape
    grouped = values.reshape(clips, frames // 2, 2, rows // 2, 2, width // 2, 2, channels)
    return lax.optimization_barrier(jnp.mean(grouped, axis=(2, 4, 6)))

def layer(values, mask, count, weights):
    in_proj, conv_first, conv_second, gain, bias = weights
    stem_end = FIRST - BP
    projected = low_back(jnp.einsum('nfrwc,cd->nfrwd', values, in_proj, precision=lax.Precision.HIGHEST))
    project = low(projected[..., stem_end:])
    pooled_branch = low_back(box_mean(project))
    first = jnp.concatenate([projected[..., :stem_end], pooled_branch], axis=-1)
    first_act = norm_act(first, mask, count, gain[:FIRST], bias[:FIRST])
    stems = low(first_act[..., B0:stem_end])
    second = low_back(jnp.concatenate([conv_cube(stems[..., :B1R], conv_first), conv_cube(stems[..., B1R:], conv_second)], axis=-1))
    second_act = norm_act(second, mask, count, gain[FIRST:], bias[FIRST:])
    return low(jnp.concatenate([first_act[..., :B0], second_act, first_act[..., stem_end:]], axis=-1))

def reference(inputs, crop_group, in_proj_4f, conv_a_4f, conv_b_4f, gain_4f, bias_4f, in_proj_5b, conv_a_5b, conv_b_5b, gain_5b, bias_5b, out_grad):
    micro, clips, frames, full_rows, full_width, channels = inputs.shape
    weights = (in_proj_4f.astype(jnp.float32), conv_a_4f.astype(jnp.float32), conv_b_4f.astype(jnp.float32), gain_4f.astype(jnp.float32), bias_4f.astype(jnp.float32), in_proj_5b.astype(jnp.float32), conv_a_5b.astype(jnp.float32), conv_b_5b.astype(jnp.float32), gain_5b.astype(jnp.float32), bias_5b.astype(jnp.float32))

    def network(values, params):
        outputs = []
        for step in range(micro):
            group = crop_group[step]
            mask_full, count_full = crop_mask(group, full_rows, full_width, clips, frames)
            mask_half, count_half = crop_mask(group, full_rows // 2, full_width // 2, clips, frames // 2)
            middle = layer(values[step] * mask_full, mask_full, count_full, params[0:5])
            pooled = low(low_back(pool_pairs(middle)))
            outputs.append(layer(pooled, mask_half, count_half, params[5:10]))
        return jnp.stack(outputs)
    result, pullback = jax.vjp(network, inputs.astype(jnp.float32), weights)
    grad_inputs, grad_weights = pullback(out_grad.astype(jnp.float32))
    return (result.astype(jnp.bfloat16), grad_inputs, grad_weights[0], grad_weights[1], grad_weights[2], grad_weights[3], grad_weights[4], grad_weights[5], grad_weights[6], grad_weights[7], grad_weights[8], grad_weights[9])
```

```python
import jax
import jax.numpy as jnp
from jax import lax
from jax.sharding import PartitionSpec as P

B0 = 256
B1R = 160
B2R = 32
B1 = 320
B2 = 128
BP = 128
FIRST = 576
STEMS = B1R + B2R
STEM_END = B0 + STEMS
SECOND = B1 + B2
BELOW = B2 + B1 + BP
GRANULE = 16

epsilon = 0.001
bf16 = jnp.bfloat16
f32 = jnp.float32


def matching(edges):
    by_sender = {}
    for edge in edges:
        by_sender.setdefault(edge[0], []).append(edge)
    taken = {}

    def place(sender, seen):
        for edge in by_sender[sender]:
            receiver = edge[1]
            if receiver in seen:
                continue
            seen.add(receiver)
            if receiver not in taken or place(taken[receiver][0], seen):
                taken[receiver] = edge
                return True
        return False

    for sender in sorted(by_sender):
        place(sender, set())
    return sorted(taken.values())


def rounds_of(edges):
    left, rounds = list(edges), []
    while left:
        chosen = matching(left)
        for edge in chosen:
            left.remove(edge)
        rounds.append(chosen)
    return rounds


def route(blocks, edges, slots):
    axes = ("segment", "space")
    me = lax.axis_index(axes)
    devices = lax.axis_size("segment") * lax.axis_size("space")
    received, place = [], [[0] * slots for _ in range(devices)]
    for turn, chosen in enumerate(rounds_of(edges)):
        block_of = [0] * devices
        for sender, receiver, block, slot in chosen:
            block_of[sender] = block
            place[receiver][slot] = turn
        own = lax.dynamic_index_in_dim(blocks, jnp.array(block_of)[me], 0, keepdims=False)
        if all(edge[0] == edge[1] for edge in chosen):
            received.append(own)
        else:
            received.append(lax.ppermute(own, axes, [(edge[0], edge[1]) for edge in chosen]))
    stack = jnp.stack(received)
    order = jnp.array(place)[me]
    return [lax.dynamic_index_in_dim(stack, order[slot], 0, keepdims=False) for slot in range(slots)]


def exchange(parts, axis):
    peers = lax.axis_size(axis)
    me = lax.axis_index(axis)
    got = [lax.dynamic_index_in_dim(parts, me, 0, keepdims=False)]
    for step in range(1, peers):
        part = lax.dynamic_index_in_dim(parts, (me + step) % peers, 0, keepdims=False)
        got.append(lax.ppermute(part, axis, [(i, (i + step) % peers) for i in range(peers)]))
    return got


def gathered(part, axis):
    peers = lax.axis_size(axis)
    me = lax.axis_index(axis)
    whole = jnp.zeros((peers,) + part.shape, part.dtype)
    for step in range(peers):
        got = part
        if step:
            got = lax.ppermute(part, axis, [(i, (i + step) % peers) for i in range(peers)])
        whole = lax.dynamic_update_index_in_dim(whole, got, (me - step) % peers, 0)
    return whole


def sum_over(x, axis):
    peers = lax.axis_size(axis)
    if peers > 4:
        return lax.psum(x, axis)
    total = x
    for step in range(1, peers):
        total = total + lax.ppermute(x, axis, [(i, (i + step) % peers) for i in range(peers)])
    return total


def reduce_scattered(x, axis):
    peers = lax.axis_size(axis)
    parts = x.reshape((peers, -1) + x.shape[1:])
    got = exchange(parts, axis)
    return sum(part.astype(f32) for part in got).astype(bf16)


def gradients_summed(grads):
    flat = [grad.reshape(-1) for grad in grads]
    sizes = [part.shape[0] for part in flat]
    n_all = lax.axis_size("segment") * lax.axis_size("dp") * lax.axis_size("space")
    block = n_all * GRANULE * 128
    length = sum(sizes)
    padded = -(-length // block) * block
    x = jnp.concatenate([part.astype(bf16) for part in flat] + [jnp.zeros((padded - length,), bf16)])
    x = x.reshape(-1, 128)
    for axis in ("segment", "dp", "space"):
        x = reduce_scattered(x, axis)
    for axis in ("space", "dp", "segment"):
        x = gathered(x, axis).reshape(-1, 128)
    x = x.reshape(-1)
    outs, start = [], 0
    for grad, size in zip(grads, sizes):
        outs.append(x[start : start + size].astype(f32).reshape(grad.shape))
        start += size
    return outs


def neighbour_sum(values, axis):
    size = values.shape[axis]
    widths = [(1, 1) if position == axis else (0, 0) for position in range(values.ndim)]
    padded = jnp.pad(values, widths)
    return (
        lax.slice_in_dim(padded, 0, size, axis=axis)
        + lax.slice_in_dim(padded, 1, size + 1, axis=axis)
        + lax.slice_in_dim(padded, 2, size + 2, axis=axis)
    )


def box_mean(values):
    wide = values.astype(f32)
    return neighbour_sum(neighbour_sum(neighbour_sum(wide, 0), 1), 2) / 27.0


def conv_cube(values, kernel):
    return lax.conv_general_dilated(
        values[None],
        kernel,
        (1, 1, 1),
        "SAME",
        dimension_numbers=("NDHWC", "DHWIO", "NDHWC"),
        preferred_element_type=f32,
    )[0]


def conv_back(grad, kernel):
    return conv_cube(grad, jnp.swapaxes(jnp.flip(kernel, (0, 1, 2)), 3, 4))


def kernel_grad(values, grad):
    frames, rows, width, channels = values.shape
    padded = jnp.pad(values, ((1, 1), (1, 1), (1, 1), (0, 0)))
    beside = jnp.concatenate([padded[:, :, k : k + width] for k in range(3)], axis=-1)
    taps = []
    for f in range(3):
        for r in range(3):
            window = beside[f : f + frames, r : r + rows]
            taps.append(jnp.einsum("frwc,frwd->cd", window, grad, preferred_element_type=f32))
    return jnp.stack(taps).reshape(3, 3, 3, channels, grad.shape[-1])


def box_mask(height, across, row_start, rows, width):
    row_place = row_start + jnp.arange(rows, dtype=jnp.int32)
    column_place = jnp.arange(width, dtype=jnp.int32)
    keep = (row_place[:, None] < height) & (column_place[None, :] < across)
    return keep.astype(f32)[..., None]


def moments(totals, count):
    mean = totals[0] / count
    variance = totals[1] / count - mean * mean
    return (mean, lax.rsqrt(variance + epsilon))


def sums(values, other, axes):
    return jnp.stack([jnp.sum(values, axis=axes), jnp.sum(values * other, axis=axes)])


def slope(active, upstream):
    sig = jax.nn.sigmoid(active)
    return upstream * sig * (1.0 + active * (1.0 - sig))


def pool_pairs(values):
    frames, rows, width, channels = values.shape[-4:]
    grouped = values.astype(f32).reshape(
        values.shape[:-4] + (frames // 2, 2, rows // 2, 2, width // 2, 2, channels)
    )
    return jnp.mean(grouped, axis=(-6, -4, -2)).astype(bf16)


def spread_pairs(values):
    for axis in (-4, -3, -2):
        values = jnp.repeat(values, 2, axis=axis)
    return values.astype(f32) * 0.125


def shards(
    inputs,
    crop_group,
    in_proj_4f,
    conv_a_4f,
    conv_b_4f,
    gain_4f,
    bias_4f,
    in_proj_5b,
    conv_a_5b,
    conv_b_5b,
    gain_5b,
    bias_5b,
    out_grad,
):
    segs, dps, bands = (lax.axis_size(axis) for axis in ("segment", "dp", "space"))
    seg, band = lax.axis_index("segment"), lax.axis_index("space")
    micro, clips, frames, rows, width, channels = inputs.shape
    full_rows, all_clips = rows * bands, clips * dps
    halves = micro // segs
    items = micro * clips
    spread = segs if items == segs * bands else 1
    assert items == spread * bands and clips % spread == 0
    each = clips // spread
    first_clip = seg * each if spread > 1 else 0
    my_micro = band // each
    counted = 1.0 if spread > 1 else (seg == 0).astype(f32)

    inward, pooled_in, outward = [], [], []
    for s in range(segs):
        for z in range(bands):
            for item in range(bands):
                inward.append((s * bands + z, s * bands + item, item, z))
    for m in range(micro):
        for c in range(clips):
            if spread > 1:
                holders = [((c // each) * bands + m * each + c % each)]
            else:
                holders = [s * bands + m * clips + c for s in range(segs)]
            home, local = m // halves, (m % halves) * clips + c
            for z in range(bands):
                for holder in holders:
                    pooled_in.append((home * bands + z, holder, local, z))
                outward.append((holders[z % len(holders)], home * bands + z, z, local))

    def group_sum(x):
        x = sum_over(x, "dp")
        if spread > 1:
            x = sum_over(x, "segment")
        if each > 1:
            pairs = [[z * each + k for k in range(each)] for z in range(micro)]
            x = lax.psum(x, "space", axis_index_groups=pairs)
        return x

    def to_rows(parts):
        return jnp.concatenate(parts, axis=1)

    def by_band(values):
        return jnp.stack(jnp.split(values, bands, axis=1))

    def crop(group, scale):
        height = full_rows // scale - group * (full_rows // scale // 4)
        across = width // scale - group * (width // scale // 4)
        count = (all_clips * (frames // scale) * height * across).astype(f32)
        return (height, across, count)

    band_clips = lax.dynamic_slice_in_dim(inputs, first_clip, each, axis=1) if spread > 1 else inputs
    heights, acrosses, counts = crop(crop_group, 1)
    band_masks = jnp.stack(
        [box_mask(heights[m], acrosses[m], band * rows, rows, width) for m in range(micro)]
    )
    cut = (band_clips * band_masks[:, None, None].astype(bf16)).reshape(
        items // spread, frames, rows, width, channels
    )
    narrow = jnp.einsum("nfrwc,cd->nfrwd", cut, in_proj_4f[:, B0:], preferred_element_type=f32)
    stems_part, project_part = narrow[..., :STEMS], narrow[..., STEMS:]
    stem_local = jnp.stack(
        [jnp.sum(stems_part, axis=(1, 2, 3)), jnp.sum(stems_part * stems_part, axis=(1, 2, 3))], 1
    )
    stem_totals = group_sum(sum(exchange(stem_local, "space")))
    stems_in = to_rows(route(stems_part.astype(bf16), inward, bands))
    project = to_rows(route(project_part.astype(bf16), inward, bands))
    grads_in = lax.dynamic_slice_in_dim(out_grad, first_clip, each, axis=1) if spread > 1 else out_grad
    upper = to_rows(route(grads_in.reshape((items // spread,) + out_grad.shape[2:]), inward, bands))

    mine = lax.dynamic_slice_in_dim(inputs, seg * halves, halves, axis=0)
    mine_masks = lax.dynamic_slice_in_dim(band_masks, seg * halves, halves, axis=0)[:, None, None]
    mine_counts = lax.dynamic_slice_in_dim(counts, seg * halves, halves, axis=0)
    mine = mine * mine_masks.astype(bf16)
    lead = jnp.einsum("mnfrwc,cd->mnfrwd", mine, in_proj_4f[:, :B0], preferred_element_type=f32)
    lead_local = jnp.stack(
        [jnp.sum(lead, axis=(1, 2, 3, 4)), jnp.sum(lead * lead, axis=(1, 2, 3, 4))], 1
    )
    lead_totals = sum_over(sum_over(lead_local, "dp"), "space")

    def per_micro(v):
        return v[:, None, None, None, None]

    lead_mean, lead_scale = moments((lead_totals[:, 0], lead_totals[:, 1]), mine_counts[:, None])
    lead_norm = (lead - per_micro(lead_mean)) * per_micro(lead_scale)
    lead_active = lead_norm * gain_4f[:B0] + bias_4f[:B0]
    lead_out = (jax.nn.silu(lead_active) * mine_masks).astype(bf16)
    lead_pooled = pool_pairs(lead_out).reshape(
        (halves * clips, frames // 2, rows // 2, width // 2, B0)
    )
    pooled_lead = to_rows(route(lead_pooled, pooled_in, bands))

    height, across, count = crop(crop_group[my_micro], 1)
    mask = box_mask(height, across, 0, full_rows, width)
    cells = (0, 1, 2)
    stem_mean, stem_scale = moments(stem_totals, count)
    stem_gain, stem_bias = gain_4f[B0:STEM_END], bias_4f[B0:STEM_END]
    stem_norm = (stems_in.astype(f32) - stem_mean) * stem_scale
    stem_active = stem_norm * stem_gain + stem_bias
    stems = (jax.nn.silu(stem_active) * mask).astype(bf16)
    rest = jnp.concatenate(
        [
            conv_cube(stems[..., :B1R], conv_a_4f),
            conv_cube(stems[..., B1R:], conv_b_4f),
            box_mean(project),
        ],
        axis=-1,
    )
    rest_totals = group_sum(sums(rest * mask, rest, cells))
    rest_mean, rest_scale = moments(rest_totals, count)
    rest_gain = jnp.concatenate([gain_4f[FIRST:], gain_4f[STEM_END:FIRST]])
    rest_bias = jnp.concatenate([bias_4f[FIRST:], bias_4f[STEM_END:FIRST]])
    rest_norm = (rest - rest_mean) * rest_scale
    rest_active = rest_norm * rest_gain + rest_bias
    rest_out = (jax.nn.silu(rest_active) * mask).astype(bf16)
    pooled = jnp.concatenate([pooled_lead, pool_pairs(rest_out)], axis=-1)

    height5, across5, count5 = crop(crop_group[my_micro], 2)
    mask5 = box_mask(height5, across5, 0, full_rows // 2, width // 2)
    projected5 = jnp.einsum("frwc,cd->frwd", pooled, in_proj_5b, preferred_element_type=f32)
    first5 = jnp.concatenate(
        [projected5[..., :STEM_END], box_mean(projected5[..., STEM_END:].astype(bf16))], axis=-1
    )
    first5_mean, first5_scale = moments(group_sum(sums(first5 * mask5, first5, cells)), count5)
    norm5 = (first5 - first5_mean) * first5_scale
    active5 = norm5 * gain_5b[:FIRST] + bias_5b[:FIRST]
    act5 = jax.nn.silu(active5) * mask5
    stems5 = act5[..., B0:STEM_END].astype(bf16)
    second5 = jnp.concatenate(
        [conv_cube(stems5[..., :B1R], conv_a_5b), conv_cube(stems5[..., B1R:], conv_b_5b)], axis=-1
    )
    second5_mean, second5_scale = moments(group_sum(sums(second5 * mask5, second5, cells)), count5)
    second5_norm = (second5 - second5_mean) * second5_scale
    second5_active = second5_norm * gain_5b[FIRST:] + bias_5b[FIRST:]
    second5_act = jax.nn.silu(second5_active) * mask5
    output = jnp.concatenate([act5[..., :B0], second5_act, act5[..., STEM_END:]], -1).astype(bf16)
    block_out = jnp.stack(route(by_band(output), outward, halves * clips))
    block_out = block_out.reshape((halves, clips) + block_out.shape[1:])

    def arranged(first, second):
        return jnp.concatenate([first[..., :B0], second, first[..., STEM_END:]], axis=-1)

    outer5_norm = arranged(norm5, second5_norm)
    outer5_gain = arranged(gain_5b[:FIRST], gain_5b[FIRST:])
    outer5_scale = arranged(first5_scale, second5_scale)
    outer5_slope = slope(arranged(active5, second5_active), upper.astype(f32) * mask5)
    outer5_local = sums(outer5_slope, outer5_norm, cells)
    outer5_total = group_sum(outer5_local) / count5
    outer5_grad = (
        mask5
        * (outer5_gain * outer5_scale)
        * (outer5_slope - outer5_total[0] - outer5_norm * outer5_total[1])
    )
    lead5_grad = outer5_grad[..., :B0]
    branch5_grad = outer5_grad[..., B0:].astype(bf16)
    wide5_grad, thin5_grad = branch5_grad[..., :B1], branch5_grad[..., B1:SECOND]
    stems5_upper = jnp.concatenate(
        [conv_back(wide5_grad, conv_a_5b), conv_back(thin5_grad, conv_b_5b)], axis=-1
    )
    stem5_slope = slope(active5[..., B0:STEM_END], stems5_upper * mask5)
    stem5_norm = norm5[..., B0:STEM_END]
    stem5_local = sums(stem5_slope, stem5_norm, cells)
    stem5_total = group_sum(stem5_local) / count5
    stem5_grad = (
        mask5
        * (gain_5b[B0:STEM_END] * first5_scale[B0:STEM_END])
        * (stem5_slope - stem5_total[0] - stem5_norm * stem5_total[1])
    )
    projected5_grad = jnp.concatenate(
        [lead5_grad, stem5_grad, box_mean(branch5_grad[..., SECOND:])], axis=-1
    ).astype(bf16)
    pooled_grad = jnp.einsum(
        "frwd,cd->frwc", projected5_grad, in_proj_5b, preferred_element_type=f32
    ).astype(bf16)
    grads5 = [
        jnp.einsum("frwc,frwd->cd", pooled, projected5_grad, preferred_element_type=f32),
        kernel_grad(stems5[..., :B1R], wide5_grad),
        kernel_grad(stems5[..., B1R:], thin5_grad),
    ]
    middle = B0 + SECOND

    def norm_grads(outer, stem):
        return jnp.concatenate([outer[:B0], stem, outer[middle:], outer[B0:middle]])

    grads5.append(norm_grads(outer5_local[1], stem5_local[1]))
    grads5.append(norm_grads(outer5_local[0], stem5_local[0]))

    lead_upper = jnp.stack(route(by_band(pooled_grad[..., :B0]), outward, halves * clips))
    rest_upper = spread_pairs(pooled_grad[..., B0:]) * mask
    rest_slope = slope(rest_active, rest_upper)
    rest_local = sums(rest_slope, rest_norm, cells)
    rest_total = group_sum(rest_local) / count
    rest_grad = (
        mask * (rest_gain * rest_scale) * (rest_slope - rest_total[0] - rest_norm * rest_total[1])
    ).astype(bf16)
    wide_grad, thin_grad = rest_grad[..., :B1], rest_grad[..., B1:SECOND]
    stems_upper = jnp.concatenate(
        [conv_back(wide_grad, conv_a_4f), conv_back(thin_grad, conv_b_4f)], axis=-1
    )
    stem_slope = slope(stem_active, stems_upper * mask)
    stem_grad_local = sums(stem_slope, stem_norm, cells)
    stem_grad_total = group_sum(stem_grad_local)
    project_grad = box_mean(rest_grad[..., SECOND:])
    late = jnp.concatenate([stem_slope, project_grad], axis=-1).astype(bf16)
    late = jnp.stack(route(by_band(late), outward, halves * clips))
    late = late.reshape((halves, clips) + late.shape[1:])
    all_totals = gathered(stem_grad_total, "space")[::each]
    all_stats = gathered(stem_totals, "space")[::each]
    grad_wide = kernel_grad(stems[..., :B1R], wide_grad)
    grad_thin = kernel_grad(stems[..., B1R:], thin_grad)

    lead_upper = lead_upper.reshape((halves, clips) + lead_upper.shape[1:])
    lead_slope = slope(lead_active, spread_pairs(lead_upper) * mine_masks)
    lead_grad_local = jnp.stack(
        [
            jnp.sum(lead_slope, axis=(1, 2, 3, 4)),
            jnp.sum(lead_slope * lead_norm, axis=(1, 2, 3, 4)),
        ],
        1,
    )
    lead_total = sum_over(sum_over(lead_grad_local, "dp"), "space") / mine_counts[:, None, None]
    lead_grad = (
        mine_masks
        * (gain_4f[:B0] * per_micro(lead_scale))
        * (lead_slope - per_micro(lead_total[:, 0]) - lead_norm * per_micro(lead_total[:, 1]))
    )

    mine_stats = lax.dynamic_slice_in_dim(all_stats, seg * halves, halves, axis=0)
    mine_total = lax.dynamic_slice_in_dim(all_totals, seg * halves, halves, axis=0)
    mine_total = mine_total / mine_counts[:, None, None]
    mine_mean, mine_scale = moments((mine_stats[:, 0], mine_stats[:, 1]), mine_counts[:, None])
    mine_stem = jnp.einsum(
        "mnfrwc,cd->mnfrwd", mine, in_proj_4f[:, B0:STEM_END], preferred_element_type=f32
    )
    mine_norm = (mine_stem - per_micro(mine_mean)) * per_micro(mine_scale)
    stem_grad = (
        mine_masks
        * (stem_gain * per_micro(mine_scale))
        * (
            late[..., :STEMS].astype(f32)
            - per_micro(mine_total[:, 0])
            - mine_norm * per_micro(mine_total[:, 1])
        )
    )
    projected_grad = jnp.concatenate(
        [lead_grad.astype(bf16), stem_grad.astype(bf16), late[..., STEMS:]], axis=-1
    )
    input_grad = (
        jnp.einsum("mnfrwd,cd->mnfrwc", projected_grad, in_proj_4f, preferred_element_type=f32)
        * mine_masks
    )
    grad_proj = jnp.einsum("mnfrwc,mnfrwd->cd", mine, projected_grad, preferred_element_type=f32)

    def norm_grads_4f(place):
        return jnp.concatenate(
            [
                jnp.sum(lead_grad_local[:, place], axis=0),
                stem_grad_local[place] * counted,
                rest_local[place, SECOND:] * counted,
                rest_local[place, :SECOND] * counted,
            ]
        )

    grads = [grad_proj, grad_wide * counted, grad_thin * counted, norm_grads_4f(1), norm_grads_4f(0)]
    grads = grads + [grad * counted for grad in grads5]
    return (block_out, input_grad, *gradients_summed(grads))


def solution(mesh):
    banded = P(None, "dp", None, "space", None, None)
    halved = P("segment", "dp", None, "space", None, None)
    in_specs = (banded,) + (P(),) * 11 + (banded,)
    out_specs = (halved, halved) + (P(),) * 10
    return jax.shard_map(shards, mesh=mesh, in_specs=in_specs, out_specs=out_specs, check_vma=False)
```

```python
import functools

import jax
import jax.numpy as jnp
from jax import lax
from jax.experimental import pallas as pl
from jax.experimental.pallas import tpu as pltpu
from jax.sharding import PartitionSpec as P

B0 = 256
B1R = 160
B2R = 32
B1 = 320
B2 = 128
BP = 128
FIRST = 576
STEMS = B1R + B2R
STEM_END = B0 + STEMS
SECOND = B1 + B2
REST = SECOND + BP
C_MID = B0 + REST
BESIDE = 640
GRANULE = 16

SEG, DP, BAND, FIRST_CLIP, MY_MICRO, COUNTED, TABLES = range(7)

epsilon = 0.001
bf16 = jnp.bfloat16
f32 = jnp.float32
i32 = jnp.int32


def matching(edges):
    by_sender = {}
    for edge in edges:
        by_sender.setdefault(edge[0], []).append(edge)
    taken = {}

    def place(sender, seen):
        for edge in by_sender[sender]:
            receiver = edge[1]
            if receiver in seen:
                continue
            seen.add(receiver)
            if receiver not in taken or place(taken[receiver][0], seen):
                taken[receiver] = edge
                return True
        return False

    for sender in sorted(by_sender):
        place(sender, set())
    return sorted(taken.values())


class Route:
    def __init__(self, edges, devices):
        left, self.rounds = list(edges), []
        while left:
            chosen = matching(left)
            for edge in chosen:
                left.remove(edge)
            self.rounds.append(chosen)
        self.blocks = [[0] * len(self.rounds) for _ in range(devices)]
        self.slots = [[0] * len(self.rounds) for _ in range(devices)]
        for turn, chosen in enumerate(self.rounds):
            for sender, receiver, block, slot in chosen:
                self.blocks[sender][turn] = block
                self.slots[receiver][turn] = slot

    def send(self, parts):
        got = []
        for part, chosen in zip(parts, self.rounds):
            if all(edge[0] == edge[1] for edge in chosen):
                got.append(part)
            else:
                pairs = [(edge[0], edge[1]) for edge in chosen]
                got.append(lax.ppermute(part, ("segment", "space"), pairs))
        return got


def rotation(peers, step):
    return [(i, (i + step) % peers) for i in range(peers)]


def rotated(parts, axis):
    peers = lax.axis_size(axis)
    return [parts[0]] + [
        lax.ppermute(parts[k], axis, rotation(peers, k)) for k in range(1, peers)
    ]


def copies(x, axis):
    return rotated([x] * lax.axis_size(axis), axis)


def sum_over(x, axis):
    if lax.axis_size(axis) > 4:
        return lax.psum(x, axis)
    got = copies(x, axis)
    return functools.reduce(jnp.add, got)


def call(body, outs, ins, numbers=(), scratch=(), cost=None, limit=40):
    vmem = pl.BlockSpec(memory_space=pltpu.VMEM)
    smem = pl.BlockSpec(memory_space=pltpu.SMEM)
    flops, traffic = cost or (10**7, 10**6)
    return pl.pallas_call(
        body,
        out_shape=[jax.ShapeDtypeStruct(shape, dtype) for shape, dtype in outs],
        in_specs=[smem] * len(numbers) + [vmem] * len(ins),
        out_specs=[vmem] * len(outs),
        scratch_shapes=[pltpu.VMEM(shape, dtype) for shape, dtype in scratch],
        cost_estimate=pl.CostEstimate(flops=flops, bytes_accessed=traffic, transcendentals=0),
        compiler_params=pltpu.CompilerParams(vmem_limit_bytes=limit * 2**20),
    )(*numbers, *ins)


def dot(a, b):
    return jnp.dot(a, b, preferred_element_type=f32)


def dot_nt(a, b):
    return lax.dot_general(a, b, (((1,), (1,)), ((), ())), preferred_element_type=f32)


def dot_tn(a, b):
    return lax.dot_general(a, b, (((0,), (0,)), ((), ())), preferred_element_type=f32)


def mask_of(cells, rows, width, height, across, first_row=0):
    place = lax.broadcasted_iota(i32, (cells, 1), 0)
    column = lax.rem(place, width)
    row = lax.rem(lax.div(place, width), rows) + first_row
    return jnp.where((row < height) & (column < across), 1.0, 0.0).astype(f32)


def pool_matrix(frames, rows, width, up):
    cells, pooled = frames * rows * width, frames * rows * width // 8
    shape = (cells, pooled) if up else (pooled, cells)
    place = lax.broadcasted_iota(i32, shape, 0 if up else 1)
    target = lax.broadcasted_iota(i32, shape, 1 if up else 0)
    column = lax.rem(place, width) // 2
    row = lax.rem(lax.div(place, width), rows) // 2
    frame = lax.div(place, width * rows) // 2
    home = (frame * (rows // 2) + row) * (width // 2) + column
    return jnp.where(home == target, 0.125, 0.0).astype(bf16)


def moments(totals, inverse):
    mean = totals[0:1] * inverse
    variance = totals[1:2] * inverse - mean * mean
    return mean, lax.rsqrt(variance + epsilon)


def column_shift(x, width, by):
    cells = x.shape[0]
    column = lax.rem(lax.broadcasted_iota(i32, (cells, 1), 0), width)
    edge = 0 if by == 1 else width - 1
    return jnp.where(column == edge, 0.0, pltpu.roll(x, by % cells, 0))


def silu(active):
    return active * jax.nn.sigmoid(active)


def slope(active, upstream):
    sig = jax.nn.sigmoid(active)
    return upstream * sig * (1.0 + active * (1.0 - sig))


def sums(a, b):
    return jnp.concatenate(
        [jnp.sum(a, axis=0, keepdims=True), jnp.sum(a * b, axis=0, keepdims=True)], axis=0
    )


def box_mean(x, frames, rows, width):
    cells, channels = x.shape
    x = x + column_shift(x, width, 1) + column_shift(x, width, -1)
    x = x.reshape(frames, rows, width, channels)
    edge = jnp.zeros((frames, 1, width, channels), f32)
    x = (
        x
        + jnp.concatenate([edge, x[:, : rows - 1]], axis=1)
        + jnp.concatenate([x[:, 1:], edge], axis=1)
    )
    edge = jnp.zeros((1, rows, width, channels), f32)
    x = (
        x
        + jnp.concatenate([edge, x[: frames - 1]], axis=0)
        + jnp.concatenate([x[1:], edge], axis=0)
    )
    return x.reshape(cells, channels) * (1.0 / 27.0)


def place_bands(dst, blocks, slots, frames, rows, width):
    for turn, block in enumerate(blocks):
        part = block[...].astype(dst.dtype).reshape(frames, rows, width, dst.shape[-1])
        dst[:, pl.ds(slots[turn] * rows, rows)] = part


def fill_beside(beside, stems, frames, rows, width):
    beside[...] = jnp.zeros_like(beside)
    three = jnp.concatenate(
        [column_shift(stems, width, 1), stems, column_shift(stems, width, -1)], axis=1
    )
    three = three.astype(beside.dtype).reshape(frames, rows, width, 3 * STEMS)
    beside[1 : frames + 1, 1 : rows + 1, :, : 3 * STEMS] = three


def fill_conv_weights(flat, wide, thin):
    flat[...] = jnp.zeros_like(flat)
    for tap in range(27):
        row = (tap // 3) * BESIDE + (tap % 3) * STEMS
        flat[row : row + B1R, B2:] = wide[tap]
        flat[row + B1R : row + STEMS, :B2] = thin[tap]


def fill_back_weights(flat, wide, thin):
    flat[...] = jnp.zeros_like(flat)
    for tap in range(27):
        start = tap * 512
        flat[:B1R, start + B2 : start + SECOND] = wide[26 - tap]
        flat[B1R:, start : start + B2] = thin[26 - tap]


def fill_shifted(shifted, grad, frames, rows, width):
    shifted[...] = jnp.zeros_like(shifted)
    for dc in range(3):
        moved = grad if dc == 1 else column_shift(grad, width, 1 - dc)
        moved = moved.astype(shifted.dtype).reshape(frames, rows, width, SECOND)
        shifted[dc, 1 : frames + 1, 1 : rows + 1, :, :SECOND] = moved


def window(padded, f, r, frames, rows):
    part = padded[f : f + frames, r : r + rows]
    return part.reshape(frames * rows * part.shape[2], part.shape[3]).astype(bf16)


def conv_chunk(beside, flat, start, step, rows):
    taps = [window(beside, start + f, r, step, rows) for f in range(3) for r in range(3)]
    return dot(jnp.concatenate(taps, axis=1), flat[...])


def back_chunk(shifted, flat, start, step, rows):
    taps = [
        window(shifted.at[dc], start + f, r, step, rows)
        for f in range(3)
        for r in range(3)
        for dc in range(3)
    ]
    return dot_nt(jnp.concatenate(taps, axis=1), flat[...])


def pack_conv(slab, beside, dz, frames, rows, width, scale):
    cells = frames * rows * width
    wide_dz, thin_dz = dz[:, B2:], dz[:, :B2]
    half = 27 * B1R // 2
    for f in range(3):
        for r in range(3):
            part = window(beside, f, r, frames, rows)
            wide = dot_tn(part, wide_dz) * scale
            thin = dot_tn(part, thin_dz) * scale
            for c in range(3):
                tap = (f * 3 + r) * 3 + c
                rows_wide = wide[c * STEMS : c * STEMS + B1R].astype(bf16)
                slab[tap * B1R : (tap + 1) * B1R] = rows_wide[:, :128]
                at = 27 * B1R + tap * B1R
                slab[at : at + B1R] = rows_wide[:, 128:256]
                for piece in range(2):
                    row = tap * B1R + piece * 80
                    side = row >= half
                    at = 2 * 27 * B1R + row - (half if side else 0)
                    lanes = slice(64, 128) if side else slice(0, 64)
                    slab[at : at + 80, lanes] = rows_wide[piece * 80 : piece * 80 + 80, 256:]
                at = 2 * 27 * B1R + half + tap * B2R
                slab[at : at + B2R] = thin[c * STEMS + B1R : (c + 1) * STEMS].astype(bf16)


CONV_ROWS = 2 * 27 * B1R + 27 * B1R // 2 + 27 * B2R


def halved(n):
    return -(-n // (2 * GRANULE)) * GRANULE


def pack_matrix(slab, at, matrix):
    n, lanes = matrix.shape
    blocks, half = lanes // 128, halved(n)
    matrix = matrix.astype(bf16)
    for j in range(blocks):
        slab[at + j * n : at + (j + 1) * n] = matrix[:, j * 128 : (j + 1) * 128]
    at = at + blocks * n
    left, right = matrix[:half, blocks * 128 :], matrix[half:, blocks * 128 :]
    if n < 2 * half:
        right = jnp.concatenate([right, jnp.zeros((2 * half - n, 64), bf16)], axis=0)
    slab[at : at + half] = jnp.concatenate([left, right], axis=1)
    return at + half


def pack_norms(slab, at, gain, bias):
    rows = [row[:, j * 128 : (j + 1) * 128] for row in (gain, bias) for j in range(8)]
    slab[at : at + 16] = jnp.concatenate(rows, axis=0).astype(bf16)


def give_halves(slab, seg, mine, other):
    half = mine.shape[0]
    mine[...] = slab[pl.ds(seg * half, half)]
    other[...] = slab[pl.ds((1 - seg) * half, half)]


def unpack_conv(slab, wide_out, thin_out):
    half = 27 * B1R // 2
    for tap in range(27):
        at = tap * B1R
        wide_out[tap, :, :128] = slab[at : at + B1R].astype(f32)
        wide_out[tap, :, 128:256] = slab[27 * B1R + at : 27 * B1R + at + B1R].astype(f32)
        for piece in range(2):
            row = at + piece * 80
            side = row >= half
            start = 2 * 27 * B1R + row - (half if side else 0)
            part = slab[start : start + 80].astype(f32)
            part = part[:, 64:] if side else part[:, :64]
            wide_out[tap, piece * 80 : piece * 80 + 80, 256:] = part
        at = 2 * 27 * B1R + half + tap * B2R
        thin_out[tap] = slab[at : at + B2R].astype(f32)


def unpack_matrix(slab, at, n, lanes):
    blocks, half = lanes // 128, halved(n)
    parts = [slab[at + j * n : at + (j + 1) * n].astype(f32) for j in range(blocks)]
    at = at + blocks * n
    tail = slab[at : at + half].astype(f32)
    parts.append(jnp.concatenate([tail[:, :64], tail[: n - half, 64:]], axis=0))
    return parts, at + half


def matrix_rows(n, lanes):
    return lanes // 128 * n + halved(n)


def padded_rows(rows):
    unit = GRANULE * lax.axis_size("segment") * lax.axis_size("dp") * lax.axis_size("space")
    return -(-rows // unit) * unit


def split_sum(parts, pieces, row, at):
    rows = parts[0].shape[0] // pieces

    def body(row_ref, *refs):
        ins, outs = refs[: len(parts)], refs[len(parts) :]
        for k, out in enumerate(outs):
            start = lax.rem(row_ref[at] + k, pieces) * rows if pieces > 1 else 0
            if pieces > 1:
                start = pl.multiple_of(start, GRANULE)
            total = ins[0][pl.ds(start, rows)].astype(f32)
            for ref in ins[1:]:
                total = total + ref[pl.ds(start, rows)].astype(f32)
            out[...] = total.astype(bf16)

    return call(body, [((rows, 128), bf16)] * pieces, parts, [row], limit=32)


def joined(parts, row, at):
    rows, pieces = parts[0].shape[0], len(parts)

    def body(row_ref, *refs):
        for k, ref in enumerate(refs[:-1]):
            start = lax.rem(row_ref[at] + pieces - k, pieces) * rows
            refs[-1][pl.ds(pl.multiple_of(start, GRANULE), rows)] = ref[...]

    return call(body, [((rows * pieces, 128), bf16)], parts, [row], limit=32)[0]


def swapped(x):
    return lax.ppermute(x, "segment", [(0, 1), (1, 0)])


def reduce_slab(mine, other, row):
    parts = split_sum([mine, swapped(other)], lax.axis_size("dp"), row, DP)
    parts = split_sum(rotated(parts, "dp"), lax.axis_size("space"), row, BAND)
    return split_sum(rotated(parts, "space"), 1, row, BAND)[0]


def gather_slab(shard, row):
    quarter = joined(copies(shard, "space"), row, BAND)
    held = copies(quarter, "dp")
    return held + [swapped(part) for part in held]


def place_slab(slab, pieces, seg, dp, peers):
    rows = pieces[0].shape[0]
    for k, piece in enumerate(pieces):
        side = seg if k < peers else 1 - seg
        at = (side * peers + lax.rem(dp + peers - k % peers, peers)) * rows
        slab[pl.ds(pl.multiple_of(at, GRANULE), rows)] = piece[...]


def shards(
    inputs,
    crop_group,
    in_proj_4f,
    conv_a_4f,
    conv_b_4f,
    gain_4f,
    bias_4f,
    in_proj_5b,
    conv_a_5b,
    conv_b_5b,
    gain_5b,
    bias_5b,
    out_grad,
):
    segs, dps, bands = (lax.axis_size(axis) for axis in ("segment", "dp", "space"))
    micro, clips, frames, rows, width, channels = inputs.shape
    full_rows, all_clips = rows * bands, clips * dps
    halves = micro // segs
    held = halves * clips
    items = micro * clips
    spread = segs if items == segs * bands else 1
    assert segs == 2 and items == spread * bands and clips % spread == 0
    each = clips // spread
    cells, part_cells = frames * full_rows * width, frames * rows * width
    frames5, rows5, width5 = frames // 2, full_rows // 2, width // 2
    cells5, part_cells5 = cells // 8, part_cells // 8
    band_rows5 = rows // 2

    inward, pooled_in, outward = [], [], []
    for s in range(segs):
        for z in range(bands):
            for item in range(bands):
                inward.append((s * bands + z, s * bands + item, item, z))
    for m in range(micro):
        for c in range(clips):
            if spread > 1:
                holders = [(c // each) * bands + m * each + c % each]
            else:
                holders = [s * bands + m * clips + c for s in range(segs)]
            home, local = m // halves, (m % halves) * clips + c
            for z in range(bands):
                for holder in holders:
                    pooled_in.append((home * bands + z, holder, local, z))
                outward.append((holders[z % len(holders)], home * bands + z, z, local))
    inward, pooled_in, outward = (
        Route(edges, segs * bands) for edges in (inward, pooled_in, outward)
    )
    IN_BLOCK = TABLES
    IN_SLOT = IN_BLOCK + len(inward.rounds)
    POOLED_BLOCK = IN_SLOT + len(inward.rounds)
    POOLED_SLOT = POOLED_BLOCK + len(pooled_in.rounds)
    OUT_BLOCK = POOLED_SLOT + len(pooled_in.rounds)
    OUT_SLOT = OUT_BLOCK + len(outward.rounds)
    table = []
    for s in range(segs):
        for d in range(dps):
            for z in range(bands):
                me = s * bands + z
                first = s * each if spread > 1 else 0
                counted = 1 if spread > 1 or s == 0 else 0
                line = [s, d, z, first, z // each, counted]
                for route in (inward, pooled_in, outward):
                    line = line + route.blocks[me] + route.slots[me]
                table.append(line)
    row = jnp.array(table, i32)[lax.axis_index(("segment", "dp", "space"))]
    numbers = [row, crop_group]

    def group_parts(x):
        if each > 1:
            pairs = [[z * each + k for k in range(each)] for z in range(micro)]
            x = lax.psum(x, "space", axis_index_groups=pairs)
        if spread > 1:
            x = x + swapped(x)
        if dps > 4:
            return [lax.psum(x, "dp")]
        return copies(x, "dp")

    def total_of(refs):
        return functools.reduce(jnp.add, [ref[...] for ref in refs])

    def crop(row_ref, group_ref, scale=1, m=None):
        group = group_ref[row_ref[MY_MICRO] if m is None else m]
        tall, wide = full_rows // scale, width // scale
        height, across = tall - group * (tall // 4), wide - group * (wide // 4)
        count = all_clips * (frames // scale) * height * across
        return height, across, 1.0 / jnp.full((1, 1), count, i32).astype(f32)

    def line(*parts):
        return jnp.concatenate(parts).reshape(1, -1)

    def affine(gain, bias):
        def parts(v):
            return (v[:B0], v[B0:STEM_END], v[STEM_END:FIRST], v[FIRST : FIRST + B1], v[FIRST + B1 :])

        def ordered(v):
            lead, stem, pool, wide, thin = parts(v)
            return jnp.concatenate([lead, pool, thin, wide, stem])

        return jnp.stack([ordered(gain), ordered(bias)])

    LEAD, POOL, OUTER, STEM = slice(0, B0), slice(B0, B0 + BP), slice(0, C_MID), slice(C_MID, None)
    RESTS, SECONDS = slice(B0, C_MID), slice(B0 + BP, C_MID)
    affine4, affine5 = affine(gain_4f, bias_4f), affine(gain_5b, bias_5b)
    wide4, thin4 = conv_a_4f.reshape(27, B1R, B1), conv_b_4f.reshape(27, B2R, B2)
    wide5, thin5 = conv_a_5b.reshape(27, B1R, B1), conv_b_5b.reshape(27, B2R, B2)

    def first_order(x, axis):
        lead, stem, pool = jnp.split(x, [B0, STEM_END], axis=axis)
        return jnp.concatenate([lead, pool, stem], axis=axis)

    proj4 = first_order(in_proj_4f, 1)
    proj5 = first_order(in_proj_5b.T, 0)
    lead, wide, thin, pool = jnp.split(proj5, [B0, B0 + B1, B0 + SECOND], axis=1)
    proj5 = jnp.concatenate([lead, pool, thin, wide], axis=1)

    def project_body(row_ref, group_ref, x_ref, p_ref, stat, *outs):
        for k in range(bands):
            item = row_ref[IN_BLOCK + k]
            m, c = lax.div(item, each), row_ref[FIRST_CLIP] + lax.rem(item, each)
            x = x_ref[m, c].reshape(part_cells, channels)
            height, across, _ = crop(row_ref, group_ref, 1, m)
            mask = mask_of(part_cells, rows, width, height, across, row_ref[BAND] * rows)
            z = dot(x, p_ref[:, B0:]) * mask
            stem = z[:, :STEMS]
            outs[k][...] = stem.astype(bf16)
            outs[bands + k][...] = z[:, STEMS:].astype(bf16)
            stat[item] = sums(stem, stem)

    got = call(
        project_body,
        [((bands, 2, STEMS), f32)]
        + [((part_cells, STEMS), bf16)] * bands
        + [((part_cells, BP), bf16)] * bands,
        [inputs, in_proj_4f],
        numbers,
    )
    stem_stat, stem_parts, pool_parts = got[0], got[1 : 1 + bands], got[1 + bands :]
    if spread > 1:
        stem_stat = stem_stat + swapped(stem_stat)
    stem_stat = sum_over(stem_stat, "dp")
    band = lax.axis_index("space")
    if each > 1:
        stem_stat = jnp.repeat(
            stem_stat.reshape(micro, each, 2, STEMS).sum(1), each, axis=0
        )
    stem_stat = jnp.roll(stem_stat, -band, axis=0)
    stem_totals = rotated([stem_stat[k] for k in range(bands)], "space")
    stem_blocks = inward.send(stem_parts)
    pool_blocks = inward.send(pool_parts)
    grads = lax.dynamic_slice_in_dim(out_grad, row[FIRST_CLIP], each, axis=1)
    grads = grads.reshape(bands, part_cells5, C_MID)
    upper_blocks = inward.send(
        [
            lax.dynamic_index_in_dim(grads, row[IN_BLOCK + k], 0, keepdims=False)
            for k in range(bands)
        ]
    )

    def home_crop(row_ref, group_ref, i):
        m = row_ref[SEG] * halves + i // clips
        height, across, inverse = crop(row_ref, group_ref, 1, m)
        first = row_ref[BAND] * rows
        return m, mask_of(part_cells, rows, width, height, across, first), inverse

    def lead_body(row_ref, group_ref, x_ref, p_ref, lead_out, stem_out, stat):
        for i in range(held):
            m, mask, _ = home_crop(row_ref, group_ref, i)
            x = x_ref[m, i % clips].reshape(part_cells, channels)
            z = dot(x, p_ref[:, :STEM_END]) * mask
            lead = z[:, :B0]
            lead_out[i] = lead
            stem_out[i] = z[:, B0:]
            total = sums(lead, lead)
            j = i // clips
            stat[j] = total if i % clips == 0 else stat[j] + total

    lead, home_stem, lead_stat = call(
        lead_body,
        [
            ((held, part_cells, B0), f32),
            ((held, part_cells, STEMS), f32),
            ((halves, 2, B0), f32),
        ],
        [inputs, in_proj_4f],
        numbers,
    )
    lead_stat = sum_over(sum_over(lead_stat, "dp"), "space")

    def lead_act(i, lead_ref, stat_ref, affine_ref, inverse):
        mean, scale = moments(stat_ref[i // clips], inverse)
        norm = (lead_ref[i] - mean) * scale
        return norm, scale, norm * affine_ref[0:1, LEAD] + affine_ref[1:2, LEAD]

    def lead_out_body(row_ref, group_ref, lead_ref, stat_ref, affine_ref, *refs):
        outs, kept = refs[:-1], refs[-1]
        matrix = pool_matrix(frames, rows, width, False)
        for i in range(held):
            _, mask, inverse = home_crop(row_ref, group_ref, i)
            _, _, active = lead_act(i, lead_ref, stat_ref, affine_ref, inverse)
            kept[i] = dot(matrix, (silu(active) * mask).astype(bf16)).astype(bf16)
        for turn, out in enumerate(outs):
            out[...] = kept[row_ref[POOLED_BLOCK + turn]]

    lead_pooled = pooled_in.send(
        call(
            lead_out_body,
            [((part_cells5, B0), bf16)] * len(pooled_in.rounds),
            [lead, lead_stat, affine4],
            numbers,
            [((held, part_cells5, B0), bf16)],
        )
    )

    step = 2 if full_rows * width <= 128 else 1

    def conv_body(row_ref, group_ref, affine_ref, wide_ref, thin_ref, *refs):
        stats, blocks = refs[:bands], refs[bands : 2 * bands]
        second_out, sums_out, norm_out, stat_out, beside, stage, flat = refs[2 * bands :]
        height, across, inverse = crop(row_ref, group_ref)
        totals = total_of(stats)
        mean, scale = moments(totals, inverse)
        stat_out[...] = totals
        fill_conv_weights(flat, wide_ref, thin_ref)
        slots = [row_ref[IN_SLOT + k] for k in range(bands)]
        place_bands(stage, blocks, slots, frames, rows, width)
        mask = mask_of(cells, full_rows, width, height, across)
        norm = (stage[...].reshape(cells, STEMS) - mean) * scale
        norm_out[...] = norm
        active = norm * affine_ref[0:1, STEM] + affine_ref[1:2, STEM]
        fill_beside(beside, silu(active) * mask, frames, full_rows, width)
        chunk = step * full_rows * width
        total = jnp.zeros((2, SECOND), f32)
        for start in range(0, frames, step):
            got = conv_chunk(beside, flat, start, step, full_rows)
            second_out[start * full_rows * width : start * full_rows * width + chunk] = got
            total = total + sums(got * mask[:chunk], got)
        sums_out[...] = total

    second, second_sums, stem_norm, stem_total, beside = call(
        conv_body,
        [
            ((cells, SECOND), f32),
            ((2, SECOND), f32),
            ((cells, STEMS), f32),
            ((2, STEMS), f32),
            ((frames + 2, full_rows + 2, width, BESIDE), bf16),
        ],
        [affine4, wide4, thin4] + stem_totals + stem_blocks,
        numbers,
        [
            ((frames, full_rows, width, STEMS), f32),
            ((9 * BESIDE, SECOND), bf16),
        ],
        cost=(2 * cells * 27 * (B1R * B1 + B2R * B2), 10**7),
    )

    def pool_body(row_ref, group_ref, second_sums, *refs):
        blocks, (zp_out, sums_out, stage) = refs[:bands], refs[bands:]
        height, across, _ = crop(row_ref, group_ref)
        slots = [row_ref[IN_SLOT + k] for k in range(bands)]
        place_bands(stage, blocks, slots, frames, rows, width)
        zp = box_mean(stage[...].reshape(cells, BP), frames, full_rows, width)
        zp_out[...] = zp
        mask = mask_of(cells, full_rows, width, height, across)
        sums_out[...] = jnp.concatenate([sums(zp * mask, zp), second_sums[...]], axis=1)

    zp, rest_sums = call(
        pool_body,
        [((cells, BP), f32), ((2, REST), f32)],
        [second_sums] + pool_blocks,
        numbers,
        [((frames, full_rows, width, BP), f32)],
    )
    rest_parts = group_parts(rest_sums)
    n_parts = len(rest_parts)

    span = 2 * full_rows * width

    def rest_of(zp_ref, second_ref, start, affine_ref, mean, scale):
        z = jnp.concatenate(
            [zp_ref[start : start + span], second_ref[start : start + span]], axis=1
        )
        norm = (z - mean) * scale
        return norm, norm * affine_ref[0:1, RESTS] + affine_ref[1:2, RESTS]

    def middle_body(row_ref, group_ref, affine_ref, p_ref, zp_ref, second_ref, *refs):
        parts, leads = refs[:n_parts], refs[n_parts:-6]
        stat_out, pooled, first_out, sums_out, stage, kept = refs[-6:]
        height, across, inverse = crop(row_ref, group_ref)
        mean, scale = moments(total_of(parts), inverse)
        stat_out[...] = jnp.concatenate([mean, scale], axis=0)
        mask = mask_of(span, full_rows, width, height, across)
        matrix = pool_matrix(2, full_rows, width, False)
        slots = [row_ref[POOLED_SLOT + k] for k in range(len(leads))]
        place_bands(stage, leads, slots, frames5, band_rows5, width5)
        pooled[:, :B0] = stage[...].reshape(cells5, B0).astype(bf16)
        for f in range(frames5):
            _, active = rest_of(zp_ref, second_ref, f * span, affine_ref, mean, scale)
            out = dot(matrix, (silu(active) * mask).astype(bf16))
            pooled[f * span // 8 : (f + 1) * span // 8, B0:] = out.astype(bf16)
        z = dot_nt(pooled[...], p_ref[...])
        kept[...] = z
        project = z[:, LEAD.stop : LEAD.stop + BP].astype(bf16).astype(f32)
        kept[:, B0 : B0 + BP] = box_mean(project, frames5, rows5, width5)
        z = kept[...]
        first_out[...] = z
        height, across, _ = crop(row_ref, group_ref, 2)
        sums_out[...] = sums(z * mask_of(cells5, rows5, width5, height, across), z)

    rest_stat, pooled, first5, first5_sums = call(
        middle_body,
        [((2, REST), f32), ((cells5, C_MID), bf16), ((cells5, FIRST), f32), ((2, FIRST), f32)],
        [affine4, proj5, zp, second] + rest_parts + lead_pooled,
        numbers,
        [((frames5, rows5, width5, B0), f32), ((cells5, FIRST), f32)],
    )
    first5_parts = group_parts(first5_sums)

    def conv5_body(row_ref, group_ref, affine_ref, wide_ref, thin_ref, first_ref, *refs):
        parts = refs[:n_parts]
        second_out, sums_out, stat_out, beside, flat = refs[n_parts:]
        height, across, inverse = crop(row_ref, group_ref, 2)
        mean, scale = moments(total_of(parts), inverse)
        stat_out[...] = jnp.concatenate([mean, scale], axis=0)
        fill_conv_weights(flat, wide_ref, thin_ref)
        mask = mask_of(cells5, rows5, width5, height, across)
        stem = slice(B0 + BP, FIRST)
        norm = (first_ref[:, stem] - mean[:, stem]) * scale[:, stem]
        active = norm * affine_ref[0:1, STEM] + affine_ref[1:2, STEM]
        fill_beside(beside, silu(active) * mask, frames5, rows5, width5)
        got = conv_chunk(beside, flat, 0, frames5, rows5)
        second_out[...] = got
        sums_out[...] = sums(got * mask, got)

    second5, second5_sums, first5_stat, beside5 = call(
        conv5_body,
        [
            ((cells5, SECOND), f32),
            ((2, SECOND), f32),
            ((2, FIRST), f32),
            ((frames5 + 2, rows5 + 2, width5, BESIDE), f32),
        ],
        [affine5, wide5, thin5, first5] + first5_parts,
        numbers,
        [((9 * BESIDE, SECOND), bf16)],
    )
    second5_parts = group_parts(second5_sums)

    def out5_body(row_ref, group_ref, affine_ref, first_ref, stat_ref, second_ref, *refs):
        parts, uppers = refs[:n_parts], refs[n_parts : n_parts + bands]
        refs = refs[n_parts + bands :]
        outs = refs[: len(outward.rounds)]
        norm_out, slope_out, scale_out, sums_out, stage, kept = refs[len(outward.rounds) :]
        height, across, inverse = crop(row_ref, group_ref, 2)
        mean2, scale2 = moments(total_of(parts), inverse)
        mask = mask_of(cells5, rows5, width5, height, across)
        outer = slice(0, B0 + BP)
        mean = jnp.concatenate([stat_ref[0:1, outer], mean2], axis=1)
        scale = jnp.concatenate([stat_ref[1:2, outer], scale2], axis=1)
        z = jnp.concatenate([first_ref[:, outer], second_ref[...]], axis=1)
        norm = (z - mean) * scale
        active = norm * affine_ref[0:1, OUTER] + affine_ref[1:2, OUTER]
        act = silu(active) * mask
        natural = [act[:, :B0], act[:, B0 + BP + B2 :], act[:, B0 + BP : B0 + BP + B2]]
        natural = jnp.concatenate(natural + [act[:, B0 : B0 + BP]], axis=1)
        kept[...] = natural.reshape(frames5, rows5, width5, C_MID)
        for turn, out in enumerate(outs):
            part = kept[:, pl.ds(row_ref[OUT_BLOCK + turn] * band_rows5, band_rows5)]
            out[...] = part.reshape(part_cells5, C_MID).astype(bf16)
        slots = [row_ref[IN_SLOT + k] for k in range(bands)]
        place_bands(stage, uppers, slots, frames5, band_rows5, width5)
        upper = stage[...].reshape(cells5, C_MID)
        upper = jnp.concatenate(
            [
                upper[:, :B0],
                upper[:, B0 + SECOND :],
                upper[:, B0 + B1 : B0 + SECOND],
                upper[:, B0 : B0 + B1],
            ],
            axis=1,
        )
        slopes = slope(active, upper * mask)
        norm_out[...] = norm
        slope_out[...] = slopes
        scale_out[...] = scale
        sums_out[...] = sums(slopes, norm)

    got = call(
        out5_body,
        [((part_cells5, C_MID), bf16)] * len(outward.rounds)
        + [
            ((cells5, C_MID), f32),
            ((cells5, C_MID), f32),
            ((1, C_MID), f32),
            ((2, C_MID), f32),
        ],
        [affine5, first5, first5_stat, second5] + second5_parts + upper_blocks,
        numbers,
        [((frames5, rows5, width5, C_MID), f32)] * 2,
    )
    out_blocks = outward.send(got[: len(outward.rounds)])
    outer5_norm, outer5_slope, outer5_scale, outer5_sums = got[len(outward.rounds) :]
    block_out = jnp.stack(out_blocks)
    block_out = jnp.stack(
        [
            lax.dynamic_index_in_dim(block_out, place, 0, keepdims=False)
            for place in jnp.argsort(row[OUT_SLOT : OUT_SLOT + held])
        ]
    ).reshape(halves, clips, frames5, band_rows5, width5, C_MID)
    outer5_parts = group_parts(outer5_sums)

    def back5_body(row_ref, group_ref, affine_ref, wide_ref, thin_ref, *refs):
        norm_ref, slope_ref, scale_ref, first_ref, stat_ref = refs[:5]
        parts, refs = refs[5 : 5 + n_parts], refs[5 + n_parts :]
        dz_out, lead_out, project_out, slope_out, sums_out, shifted, flat = refs
        height, across, inverse = crop(row_ref, group_ref, 2)
        mask = mask_of(cells5, rows5, width5, height, across)
        fill_back_weights(flat, wide_ref, thin_ref)
        total = total_of(parts) * inverse
        grad = (mask * (affine_ref[0:1, OUTER] * scale_ref[...])) * (
            slope_ref[...] - total[0:1] - norm_ref[...] * total[1:2]
        )
        lead_out[...] = grad[:, :B0]
        low = grad[:, B0:].astype(bf16)
        dz = low[:, BP:]
        dz_out[...] = dz
        project_out[...] = box_mean(low[:, :BP].astype(f32), frames5, rows5, width5)
        fill_shifted(shifted, dz.astype(f32), frames5, rows5, width5)
        upper = back_chunk(shifted, flat, 0, frames5, rows5)
        stem = slice(B0 + BP, FIRST)
        norm = (first_ref[:, stem] - stat_ref[0:1, stem]) * stat_ref[1:2, stem]
        active = norm * affine_ref[0:1, STEM] + affine_ref[1:2, STEM]
        slopes = slope(active, upper * mask)
        slope_out[...] = slopes
        sums_out[...] = sums(slopes, norm)

    dz5, lead5_grad, project5_grad, stem5_slope, stem5_sums = call(
        back5_body,
        [
            ((cells5, SECOND), bf16),
            ((cells5, B0), f32),
            ((cells5, BP), f32),
            ((cells5, STEMS), f32),
            ((2, STEMS), f32),
        ],
        [affine5, wide5, thin5, outer5_norm, outer5_slope, outer5_scale, first5, first5_stat]
        + outer5_parts,
        numbers,
        [
            ((3, frames5 + 2, rows5 + 2, width5, 512), f32),
            ((STEMS, 27 * 512), bf16),
        ],
    )
    stem5_parts = group_parts(stem5_sums)

    def rest_slope(f, pooled_grad, matrix, mask, zp_ref, second_ref, affine_ref, stat_ref):
        norm, active = rest_of(
            zp_ref, second_ref, f * span, affine_ref, stat_ref[0:1], stat_ref[1:2]
        )
        upper = dot(matrix, pooled_grad[f * span // 8 : (f + 1) * span // 8])
        return norm, slope(active, upper * mask)

    def first5_body(row_ref, group_ref, affine_ref, affine4_ref, p_ref, *refs):
        lead_ref, project_ref, slope_ref, first_ref, stat_ref = refs[:5]
        zp_ref, second_ref, rest_stat = refs[5:8]
        parts, refs = refs[8 : 8 + n_parts], refs[8 + n_parts :]
        outs, refs = refs[: len(outward.rounds)], refs[len(outward.rounds) :]
        projected_out, rest_out, sums_out, kept = refs
        height, across, inverse = crop(row_ref, group_ref, 2)
        mask = mask_of(cells5, rows5, width5, height, across)
        total = total_of(parts) * inverse
        stem = slice(B0 + BP, FIRST)
        norm = (first_ref[:, stem] - stat_ref[0:1, stem]) * stat_ref[1:2, stem]
        stem_grad = (mask * (affine_ref[0:1, STEM] * stat_ref[1:2, stem])) * (
            slope_ref[...] - total[0:1] - norm * total[1:2]
        )
        projected = jnp.concatenate([lead_ref[...], project_ref[...], stem_grad], axis=1)
        projected = projected.astype(bf16)
        projected_out[...] = projected
        pooled_grad = dot(projected, p_ref[...]).astype(bf16)
        kept[...] = pooled_grad[:, :B0].astype(f32).reshape(frames5, rows5, width5, B0)
        for turn, out in enumerate(outs):
            part = kept[:, pl.ds(row_ref[OUT_BLOCK + turn] * band_rows5, band_rows5)]
            out[...] = part.reshape(part_cells5, B0).astype(bf16)
        rest_grad = pooled_grad[:, B0:]
        rest_out[...] = rest_grad
        height, across, _ = crop(row_ref, group_ref)
        mask = mask_of(span, full_rows, width, height, across)
        matrix = pool_matrix(2, full_rows, width, True)
        total = jnp.zeros((2, REST), f32)
        for f in range(frames5):
            norm, slopes = rest_slope(
                f, rest_grad, matrix, mask, zp_ref, second_ref, affine4_ref, rest_stat
            )
            total = total + sums(slopes, norm)
        sums_out[...] = total

    got = call(
        first5_body,
        [((part_cells5, B0), bf16)] * len(outward.rounds)
        + [((cells5, FIRST), bf16), ((cells5, REST), bf16), ((2, REST), f32)],
        [affine5, affine4, proj5, lead5_grad, project5_grad, stem5_slope, first5, first5_stat]
        + [zp, second, rest_stat]
        + stem5_parts,
        numbers,
        [((frames5, rows5, width5, B0), f32)],
    )
    lead_upper = outward.send(got[: len(outward.rounds)])
    projected5_grad, rest_upper, rest_grad_sums = got[len(outward.rounds) :]
    rest_grad_parts = group_parts(rest_grad_sums)

    rows_5b = padded_rows(CONV_ROWS + matrix_rows(FIRST, C_MID) + 16)

    def natural(outer, stem):
        pool, thin, wide = (
            outer[:, B0 : B0 + BP],
            outer[:, B0 + BP : B0 + BP + B2],
            outer[:, B0 + BP + B2 :],
        )
        return jnp.concatenate([outer[:, :B0], stem, pool, wide, thin], axis=1)

    def weights5_body(row_ref, beside, dz_ref, pooled_ref, projected_ref, *refs):
        outer_ref, stem_ref, mine, other, slab = refs
        scale = jnp.full((1, 1), row_ref[COUNTED], i32).astype(f32)
        pack_conv(slab, beside, dz_ref[...], frames5, rows5, width5, scale)
        grad = dot_tn(projected_ref[...], pooled_ref[...]) * scale
        at = pack_matrix(slab, CONV_ROWS, grad)
        norms = natural(outer_ref[...], stem_ref[...]) * scale
        pack_norms(slab, at, norms[1:2], norms[0:1])
        slab[at + 16 :] = jnp.zeros((rows_5b - at - 16, 128), bf16)
        give_halves(slab, row_ref[SEG], mine, other)

    mine5, other5 = call(
        weights5_body,
        [((rows_5b // 2, 128), bf16)] * 2,
        [beside5, dz5, pooled, projected5_grad, outer5_sums, stem5_sums],
        [row],
        [((rows_5b, 128), bf16)],
    )
    shard5 = reduce_slab(mine5, other5, row)
    pieces5 = gather_slab(shard5, row)

    def back4_body(row_ref, group_ref, affine_ref, zp_ref, second_ref, stat_ref, grad_ref, *refs):
        parts, refs = refs[:n_parts], refs[n_parts:]
        outs, (dz_out, kept) = refs[: len(outward.rounds)], refs[len(outward.rounds) :]
        height, across, inverse = crop(row_ref, group_ref)
        mask = mask_of(span, full_rows, width, height, across)
        total = total_of(parts) * inverse
        matrix = pool_matrix(2, full_rows, width, True)
        factor = affine_ref[0:1, RESTS] * stat_ref[1:2]
        for f in range(frames5):
            norm, slopes = rest_slope(
                f, grad_ref, matrix, mask, zp_ref, second_ref, affine_ref, stat_ref
            )
            grad = (mask * factor) * (slopes - total[0:1] - norm * total[1:2])
            low = grad.astype(bf16)
            dz_out[f * span : (f + 1) * span] = low[:, BP:]
            kept[2 * f : 2 * f + 2] = low[:, :BP].astype(f32).reshape(2, full_rows, width, BP)
        pool = box_mean(kept[...].reshape(cells, BP), frames, full_rows, width)
        kept[...] = pool.reshape(frames, full_rows, width, BP)
        for turn, out in enumerate(outs):
            part = kept[:, pl.ds(row_ref[OUT_BLOCK + turn] * rows, rows)]
            out[...] = part.reshape(part_cells, BP).astype(bf16)

    got = call(
        back4_body,
        [((part_cells, BP), bf16)] * len(outward.rounds) + [((cells, SECOND), bf16)],
        [affine4, zp, second, rest_stat, rest_upper] + rest_grad_parts,
        numbers,
        [((frames, full_rows, width, BP), f32)],
    )
    project_grads = outward.send(got[: len(outward.rounds)])
    dz = got[-1]

    rows_4f = padded_rows(CONV_ROWS)

    def weights4_body(row_ref, beside, dz_ref, mine, other, slab):
        scale = jnp.full((1, 1), row_ref[COUNTED], i32).astype(f32)
        pack_conv(slab, beside, dz_ref[...], frames, full_rows, width, scale)
        slab[CONV_ROWS:] = jnp.zeros((rows_4f - CONV_ROWS, 128), bf16)
        give_halves(slab, row_ref[SEG], mine, other)

    mine4, other4 = call(
        weights4_body,
        [((rows_4f // 2, 128), bf16)] * 2,
        [beside, dz],
        [row],
        [((rows_4f, 128), bf16)],
        cost=(2 * cells * 27 * (B1R * B1 + B2R * B2), 10**7),
    )
    shard4 = reduce_slab(mine4, other4, row)

    def stems4_body(row_ref, group_ref, affine_ref, wide_ref, thin_ref, dz_ref, norm_ref, *refs):
        outs, refs = refs[: len(outward.rounds)], refs[len(outward.rounds) :]
        sums_out, shifted, flat, kept = refs
        height, across, _ = crop(row_ref, group_ref)
        fill_back_weights(flat, wide_ref, thin_ref)
        fill_shifted(shifted, dz_ref[...].astype(f32), frames, full_rows, width)
        chunk = step * full_rows * width
        mask = mask_of(chunk, full_rows, width, height, across)
        total = jnp.zeros((2, STEMS), f32)
        for start in range(0, frames, step):
            upper = back_chunk(shifted, flat, start, step, full_rows)
            at = start * full_rows * width
            norm = norm_ref[at : at + chunk]
            active = norm * affine_ref[0:1, STEM] + affine_ref[1:2, STEM]
            slopes = slope(active, upper * mask)
            kept[start : start + step] = slopes.reshape(step, full_rows, width, STEMS)
            total = total + sums(slopes, norm)
        sums_out[...] = total
        for turn, out in enumerate(outs):
            part = kept[:, pl.ds(row_ref[OUT_BLOCK + turn] * rows, rows)]
            out[...] = part.reshape(part_cells, STEMS).astype(bf16)

    got = call(
        stems4_body,
        [((part_cells, STEMS), bf16)] * len(outward.rounds) + [((2, STEMS), f32)],
        [affine4, wide4, thin4, dz, stem_norm],
        numbers,
        [
            ((3, frames + 2, full_rows + 2, width, 512), bf16),
            ((STEMS, 27 * 512), bf16),
            ((frames, full_rows, width, STEMS), f32),
        ],
        cost=(2 * cells * 27 * (B1R * B1 + B2R * B2), 10**7),
    )
    stem_slopes = outward.send(got[: len(outward.rounds)])
    stem_sums = got[-1]
    stem_grad_total = functools.reduce(jnp.add, group_parts(stem_sums))
    stem_grad_totals = copies(stem_grad_total, "space")
    stem_stats = copies(stem_total, "space")

    def lead_slopes(i, row_ref, group_ref, lead_ref, stat_ref, affine_ref, matrix, kept):
        _, mask, inverse = home_crop(row_ref, group_ref, i)
        norm, scale, active = lead_act(i, lead_ref, stat_ref, affine_ref, inverse)
        upper = dot(matrix, kept[i])
        return mask, inverse, scale, norm, slope(active, upper * mask)

    def lead_back_body(row_ref, group_ref, lead_ref, stat_ref, affine_ref, *refs):
        uppers, (sums_out, kept) = refs[:held], refs[held:]
        matrix = pool_matrix(frames, rows, width, True)
        for turn, ref in enumerate(uppers):
            kept[row_ref[OUT_SLOT + turn]] = ref[...]
        for i in range(held):
            _, _, _, norm, slopes = lead_slopes(
                i, row_ref, group_ref, lead_ref, stat_ref, affine_ref, matrix, kept
            )
            total = sums(slopes, norm)
            j = i // clips
            sums_out[j] = total if i % clips == 0 else sums_out[j] + total

    lead_sums, lead_upper = call(
        lead_back_body,
        [((halves, 2, B0), f32), ((held, part_cells5, B0), bf16)],
        [lead, lead_stat, affine4] + lead_upper,
        numbers,
    )
    lead_total = sum_over(sum_over(lead_sums, "dp"), "space")

    rows_proj = padded_rows(matrix_rows(channels, FIRST) + 16)

    def first4_body(row_ref, group_ref, x_ref, affine_ref, lead_ref, stat_ref, *refs):
        upper_ref, total_ref, stem_ref, lead_sums, rest_sums, stem_sums = refs[:6]
        refs = refs[6:]
        stats, totals, refs = refs[:bands], refs[bands : 2 * bands], refs[2 * bands :]
        slopes_in, pools_in, refs = refs[:held], refs[held : 2 * held], refs[2 * held :]
        projected, mine, other, x_all, slab, late, stat_all, total_all = refs
        matrix = pool_matrix(frames, rows, width, True)
        for turn in range(held):
            place = row_ref[OUT_SLOT + turn]
            late[place, :, :BP] = pools_in[turn][...].astype(f32)
            late[place, :, BP:] = slopes_in[turn][...].astype(f32)
        for k in range(bands):
            stat_all[k] = stats[k][...]
            total_all[k] = totals[k][...]
        for i in range(held):
            mask, inverse, scale, norm, slopes = lead_slopes(
                i, row_ref, group_ref, lead_ref, stat_ref, affine_ref, matrix, upper_ref
            )
            total = total_ref[i // clips] * inverse
            lead_grad = (affine_ref[0:1, LEAD] * scale) * (
                slopes - total[0:1] - norm * total[1:2]
            )
            m = row_ref[SEG] * halves + i // clips
            turn = lax.rem(row_ref[BAND] + bands - m * each, bands)
            mean, scale = moments(stat_all[turn], inverse)
            total = total_all[turn] * inverse
            norm = (stem_ref[i] - mean) * scale
            stem_grad = (affine_ref[0:1, STEM] * scale) * (
                late[i, :, BP:] - total[0:1] - norm * total[1:2]
            )
            grad = jnp.concatenate([lead_grad, late[i, :, :BP], stem_grad], axis=1) * mask
            at = i * part_cells
            projected[at : at + part_cells] = grad.astype(bf16)
            x_all[at : at + part_cells] = x_ref[m, i % clips].reshape(part_cells, channels)
        at = pack_matrix(slab, 0, dot_tn(x_all[...], projected[...]))
        counted = jnp.full((1, 1), row_ref[COUNTED], i32).astype(f32)
        own = jnp.sum(lead_sums[...], axis=0)
        rest = rest_sums[...] * counted
        norms = natural(jnp.concatenate([own, rest], axis=1), stem_sums[...] * counted)
        pack_norms(slab, at, norms[1:2], norms[0:1])
        slab[at + 16 :] = jnp.zeros((rows_proj - at - 16, 128), bf16)
        give_halves(slab, row_ref[SEG], mine, other)

    projected_grad, mine_proj, other_proj = call(
        first4_body,
        [((held * part_cells, FIRST), bf16)] + [((rows_proj // 2, 128), bf16)] * 2,
        [inputs, affine4, lead, lead_stat, lead_upper, lead_total, home_stem]
        + [lead_sums, rest_grad_sums, stem_sums]
        + stem_stats
        + stem_grad_totals
        + stem_slopes
        + project_grads,
        numbers,
        [
            ((held * part_cells, channels), bf16),
            ((rows_proj, 128), bf16),
            ((held, part_cells, BP + STEMS), f32),
            ((bands, 2, STEMS), f32),
            ((bands, 2, STEMS), f32),
        ],
    )
    shard_proj = reduce_slab(mine_proj, other_proj, row)

    def input_body(projected_ref, p_ref, out):
        for i in range(held):
            at = i * part_cells
            got = dot_nt(projected_ref[at : at + part_cells], p_ref[...])
            out[i // clips, i % clips] = got.reshape(frames, rows, width, channels)

    (input_grad,) = call(
        input_body,
        [((halves, clips, frames, rows, width, channels), f32)],
        [projected_grad, proj4],
    )

    def unpacked(pieces, n_rows, body, outs):
        def whole(row_ref, *refs):
            slab = refs[-1]
            place_slab(slab, refs[: len(pieces)], row_ref[SEG], row_ref[DP], dps)
            body(slab, *refs[len(pieces) : -1])

        return call(whole, outs, pieces, [row], [((n_rows, 128), bf16)], limit=48)

    conv_outs = [((27, B1R, B1), f32), ((27, B2R, B2), f32)]

    def unpack5(slab, wide_out, thin_out, proj_out, norm_out):
        unpack_conv(slab, wide_out, thin_out)
        parts, at = unpack_matrix(slab, CONV_ROWS, FIRST, C_MID)
        lead = parts[:2]
        tail = jnp.concatenate([parts[6], parts[3], parts[2]], axis=1)
        for first, last, place in ((0, B0, 0), (B0, B0 + BP, STEM_END), (B0 + BP, FIRST, B0)):
            to = slice(place, place + last - first)
            proj_out[to, 0:128] = lead[0][first:last]
            proj_out[to, 128:256] = lead[1][first:last]
            proj_out[to, 256:384] = parts[4][first:last]
            proj_out[to, 384:512] = parts[5][first:last]
            proj_out[to, 512:] = tail[first:last]
        norm_out[...] = slab[at : at + 16].astype(f32)

    wide5_grad, thin5_grad, proj5_grad, norms5 = unpacked(
        pieces5, rows_5b, unpack5, conv_outs + [((FIRST, C_MID), f32), ((16, 128), f32)]
    )
    wide4_grad, thin4_grad = unpacked(
        gather_slab(shard4, row), rows_4f, unpack_conv, conv_outs
    )

    def unpack_proj(slab, proj_out, norm_out):
        parts, at = unpack_matrix(slab, 0, channels, FIRST)
        proj_out[:, :128] = parts[0]
        proj_out[:, 128:256] = parts[1]
        proj_out[:, 256:] = jnp.concatenate([parts[3], parts[4], parts[2]], axis=1)
        norm_out[...] = slab[at : at + 16].astype(f32)

    proj4_grad, norms4 = unpacked(
        gather_slab(shard_proj, row),
        rows_proj,
        unpack_proj,
        [((channels, FIRST), f32), ((16, 128), f32)],
    )
    return (
        block_out,
        input_grad,
        proj4_grad,
        wide4_grad.reshape(conv_a_4f.shape),
        thin4_grad.reshape(conv_b_4f.shape),
        norms4[:8].reshape(-1),
        norms4[8:].reshape(-1),
        proj5_grad.T,
        wide5_grad.reshape(conv_a_5b.shape),
        thin5_grad.reshape(conv_b_5b.shape),
        norms5[:8].reshape(-1),
        norms5[8:].reshape(-1),
    )


def solution(mesh):
    banded = P(None, "dp", None, "space", None, None)
    halved_specs = P("segment", "dp", None, "space", None, None)
    in_specs = (banded,) + (P(),) * 11 + (banded,)
    out_specs = (halved_specs, halved_specs) + (P(),) * 10
    return jax.shard_map(shards, mesh=mesh, in_specs=in_specs, out_specs=out_specs, check_vma=False)
```

```python
import functools

import jax
import jax.numpy as jnp
from jax import lax
from jax.experimental import pallas as pl
from jax.experimental.pallas import tpu as pltpu
from jax.sharding import PartitionSpec as P

B0 = 256
B1R = 160
B2R = 32
B1 = 320
B2 = 128
BP = 128
FIRST = 576
STEMS = B1R + B2R
STEM_END = B0 + STEMS
SECOND = B1 + B2
REST = SECOND + BP
C_MID = B0 + REST
BESIDE = 640
GRANULE = 16
SCALE = 3.0
PADDED = 256

SEG, DP, BAND, FIRST_CLIP, MY_MICRO, COUNTED, TABLES = range(7)

epsilon = 0.001
bf16 = jnp.bfloat16
f32 = jnp.float32
i32 = jnp.int32


def matching(edges):
    by_sender = {}
    for edge in edges:
        by_sender.setdefault(edge[0], []).append(edge)
    taken = {}

    def place(sender, seen):
        for edge in by_sender[sender]:
            receiver = edge[1]
            if receiver in seen:
                continue
            seen.add(receiver)
            if receiver not in taken or place(taken[receiver][0], seen):
                taken[receiver] = edge
                return True
        return False

    for sender in sorted(by_sender):
        place(sender, set())
    return sorted(taken.values())


class Route:
    def __init__(self, edges, devices):
        left, self.rounds = list(edges), []
        while left:
            chosen = matching(left)
            for edge in chosen:
                left.remove(edge)
            self.rounds.append(chosen)
        self.blocks = [[0] * len(self.rounds) for _ in range(devices)]
        self.slots = [[0] * len(self.rounds) for _ in range(devices)]
        for turn, chosen in enumerate(self.rounds):
            for sender, receiver, block, slot in chosen:
                self.blocks[sender][turn] = block
                self.slots[receiver][turn] = slot

    def send(self, parts):
        got = []
        for part, chosen in zip(parts, self.rounds):
            if all(edge[0] == edge[1] for edge in chosen):
                got.append(part)
            else:
                pairs = [(edge[0], edge[1]) for edge in chosen]
                got.append(lax.ppermute(part, ("segment", "space"), pairs))
        return got


def pairing(peers, step):
    return [(i, i ^ step) for i in range(peers)]


def exchanged(parts, axis):
    peers = lax.axis_size(axis)
    assert peers & (peers - 1) == 0
    return [parts[0]] + [lax.ppermute(parts[k], axis, pairing(peers, k)) for k in range(1, peers)]


def copies(x, axis):
    return exchanged([x] * lax.axis_size(axis), axis)


def sum_over(x, axis):
    if lax.axis_size(axis) > 4:
        return lax.psum(x, axis)
    got = copies(x, axis)
    return functools.reduce(jnp.add, got)


class Order:
    def __init__(self):
        self.last = []


order = Order()


def call(body, outs, ins, numbers=(), scratch=(), us=2.0, limit=40):
    vmem = pl.BlockSpec(memory_space=pltpu.VMEM)
    smem = pl.BlockSpec(memory_space=pltpu.SMEM)
    skipped, after = len(numbers) + len(ins), order.last

    def waited(*refs):
        body(*refs[:skipped], *refs[skipped + len(after) :])

    got = pl.pallas_call(
        waited,
        out_shape=[jax.ShapeDtypeStruct(shape, dtype) for shape, dtype in outs],
        in_specs=[smem] * len(numbers)
        + [vmem] * len(ins)
        + [pl.BlockSpec(memory_space=pl.ANY)] * len(after),
        out_specs=[vmem] * len(outs),
        scratch_shapes=[pltpu.VMEM(shape, dtype) for shape, dtype in scratch],
        cost_estimate=pl.CostEstimate(
            flops=int(us * SCALE * 1.1e9), bytes_accessed=10**6, transcendentals=0
        ),
        compiler_params=pltpu.CompilerParams(vmem_limit_bytes=limit * 2**20),
    )(*numbers, *ins, *after)
    order.last = [got[-1]]
    return got


def dot(a, b):
    return jnp.dot(a, b, preferred_element_type=f32)


def dot_nt(a, b):
    return lax.dot_general(a, b, (((1,), (1,)), ((), ())), preferred_element_type=f32)


def dot_tn(a, b):
    return lax.dot_general(a, b, (((0,), (0,)), ((), ())), preferred_element_type=f32)


def mask_of(cells, rows, width, height, across, first_row=0):
    place = lax.broadcasted_iota(i32, (cells, 1), 0)
    column = lax.rem(place, width)
    row = lax.rem(lax.div(place, width), rows) + first_row
    return jnp.where((row < height) & (column < across), 1.0, 0.0).astype(f32)


def pool_matrix(frames, rows, width, up):
    cells, pooled = frames * rows * width, frames * rows * width // 8
    shape = (cells, pooled) if up else (pooled, cells)
    place = lax.broadcasted_iota(i32, shape, 0 if up else 1)
    target = lax.broadcasted_iota(i32, shape, 1 if up else 0)
    column = lax.rem(place, width) // 2
    row = lax.rem(lax.div(place, width), rows) // 2
    frame = lax.div(place, width * rows) // 2
    home = (frame * (rows // 2) + row) * (width // 2) + column
    return jnp.where(home == target, 0.125, 0.0).astype(bf16)


def moments(totals, inverse):
    mean = totals[0:1] * inverse
    variance = totals[1:2] * inverse - mean * mean
    return mean, lax.rsqrt(variance + epsilon)


def column_shift(x, width, by):
    cells = x.shape[0]
    column = lax.rem(lax.broadcasted_iota(i32, (cells, 1), 0), width)
    edge = 0 if by == 1 else width - 1
    return jnp.where(column == edge, 0.0, pltpu.roll(x, by % cells, 0))


def silu(active):
    return active * jax.nn.sigmoid(active)


def slope(active, upstream):
    sig = jax.nn.sigmoid(active)
    return upstream * sig * (1.0 + active * (1.0 - sig))


def sums(a, b):
    return jnp.concatenate(
        [jnp.sum(a, axis=0, keepdims=True), jnp.sum(a * b, axis=0, keepdims=True)], axis=0
    )


def box_mean(x, frames, rows, width):
    cells, channels = x.shape
    x = x + column_shift(x, width, 1) + column_shift(x, width, -1)
    x = x.reshape(frames, rows, width, channels)
    edge = jnp.zeros((frames, 1, width, channels), f32)
    x = (
        x
        + jnp.concatenate([edge, x[:, : rows - 1]], axis=1)
        + jnp.concatenate([x[:, 1:], edge], axis=1)
    )
    edge = jnp.zeros((1, rows, width, channels), f32)
    x = (
        x
        + jnp.concatenate([edge, x[: frames - 1]], axis=0)
        + jnp.concatenate([x[1:], edge], axis=0)
    )
    return x.reshape(cells, channels) * (1.0 / 27.0)


def place_bands(dst, blocks, slots, frames, rows, width):
    for turn, block in enumerate(blocks):
        part = block[...].astype(dst.dtype).reshape(frames, rows, width, dst.shape[-1])
        dst[:, pl.ds(slots[turn] * rows, rows)] = part


def fill_beside(beside, stems, frames, rows, width):
    beside[...] = jnp.zeros_like(beside)
    three = jnp.concatenate(
        [column_shift(stems, width, 1), stems, column_shift(stems, width, -1)], axis=1
    )
    three = three.astype(beside.dtype).reshape(frames, rows, width, 3 * STEMS)
    beside[1 : frames + 1, 1 : rows + 1, :, : 3 * STEMS] = three


def fill_conv_weights(flat, wide, thin):
    flat[...] = jnp.zeros_like(flat)
    for tap in range(27):
        row = (tap // 3) * BESIDE + (tap % 3) * STEMS
        flat[row : row + B1R, B2:] = wide[tap]
        flat[row + B1R : row + STEMS, :B2] = thin[tap]


def fill_back_weights(flat, wide, thin):
    flat[...] = jnp.zeros_like(flat)
    for tap in range(27):
        start = tap * 512
        flat[:B1R, start + B2 : start + SECOND] = wide[26 - tap]
        flat[B1R:, start : start + B2] = thin[26 - tap]


def fill_shifted(shifted, grad, frames, rows, width):
    shifted[...] = jnp.zeros_like(shifted)
    for dc in range(3):
        moved = grad if dc == 1 else column_shift(grad, width, 1 - dc)
        moved = moved.astype(shifted.dtype).reshape(frames, rows, width, SECOND)
        shifted[dc, 1 : frames + 1, 1 : rows + 1, :, :SECOND] = moved


def window(padded, f, r, frames, rows):
    part = padded[f : f + frames, r : r + rows]
    return part.reshape(frames * rows * part.shape[2], part.shape[3]).astype(bf16)


def conv_chunk(beside, flat, start, step, rows):
    taps = [window(beside, start + f, r, step, rows) for f in range(3) for r in range(3)]
    return dot(jnp.concatenate(taps, axis=1), flat[...])


def back_chunk(shifted, flat, start, step, rows):
    taps = [
        window(shifted.at[dc], start + f, r, step, rows)
        for f in range(3)
        for r in range(3)
        for dc in range(3)
    ]
    return dot_nt(jnp.concatenate(taps, axis=1), flat[...])


def pack_conv(slab, beside, dz, frames, rows, width, scale):
    cells = frames * rows * width
    wide_dz, thin_dz = dz[:, B2:], dz[:, :B2]
    half = 27 * B1R // 2
    for f in range(3):
        for r in range(3):
            part = window(beside, f, r, frames, rows)
            wide = dot_tn(part, wide_dz) * scale
            thin = dot_tn(part, thin_dz) * scale
            for c in range(3):
                tap = (f * 3 + r) * 3 + c
                rows_wide = wide[c * STEMS : c * STEMS + B1R].astype(bf16)
                slab[tap * B1R : (tap + 1) * B1R] = rows_wide[:, :128]
                at = 27 * B1R + tap * B1R
                slab[at : at + B1R] = rows_wide[:, 128:256]
                for piece in range(2):
                    row = tap * B1R + piece * 80
                    side = row >= half
                    at = 2 * 27 * B1R + row - (half if side else 0)
                    lanes = slice(64, 128) if side else slice(0, 64)
                    slab[at : at + 80, lanes] = rows_wide[piece * 80 : piece * 80 + 80, 256:]
                at = 2 * 27 * B1R + half + tap * B2R
                slab[at : at + B2R] = thin[c * STEMS + B1R : (c + 1) * STEMS].astype(bf16)


CONV_ROWS = 2 * 27 * B1R + 27 * B1R // 2 + 27 * B2R


def halved(n):
    return -(-n // (2 * GRANULE)) * GRANULE


def pack_matrix(slab, at, matrix):
    n, lanes = matrix.shape
    blocks, half = lanes // 128, halved(n)
    matrix = matrix.astype(bf16)
    for j in range(blocks):
        slab[at + j * n : at + (j + 1) * n] = matrix[:, j * 128 : (j + 1) * 128]
    at = at + blocks * n
    left, right = matrix[:half, blocks * 128 :], matrix[half:, blocks * 128 :]
    if n < 2 * half:
        right = jnp.concatenate([right, jnp.zeros((2 * half - n, 64), bf16)], axis=0)
    slab[at : at + half] = jnp.concatenate([left, right], axis=1)
    return at + half


def pack_norms(slab, at, gain, bias):
    rows = [row[:, j * 128 : (j + 1) * 128] for row in (gain, bias) for j in range(8)]
    slab[at : at + 16] = jnp.concatenate(rows, axis=0).astype(bf16)


def give_halves(slab, seg, mine, other):
    half = mine.shape[0]
    mine[...] = slab[pl.ds(seg * half, half)]
    other[...] = slab[pl.ds((1 - seg) * half, half)]


def unpack_conv(slab, wide_out, thin_out):
    half = 27 * B1R // 2
    for tap in range(27):
        at = tap * B1R
        wide_out[tap, :, :128] = slab[at : at + B1R].astype(f32)
        wide_out[tap, :, 128:256] = slab[27 * B1R + at : 27 * B1R + at + B1R].astype(f32)
        for piece in range(2):
            row = at + piece * 80
            side = row >= half
            start = 2 * 27 * B1R + row - (half if side else 0)
            part = slab[start : start + 80].astype(f32)
            part = part[:, 64:] if side else part[:, :64]
            wide_out[tap, piece * 80 : piece * 80 + 80, 256:] = part
        at = 2 * 27 * B1R + half + tap * B2R
        thin_out[tap] = slab[at : at + B2R].astype(f32)


def unpack_matrix(slab, at, n, lanes):
    blocks, half = lanes // 128, halved(n)
    parts = [slab[at + j * n : at + (j + 1) * n].astype(f32) for j in range(blocks)]
    at = at + blocks * n
    tail = slab[at : at + half].astype(f32)
    parts.append(jnp.concatenate([tail[:, :64], tail[: n - half, 64:]], axis=0))
    return parts, at + half


def matrix_rows(n, lanes):
    return lanes // 128 * n + halved(n)


def padded_rows(rows):
    unit = GRANULE * lax.axis_size("segment") * lax.axis_size("dp") * lax.axis_size("space")
    return -(-rows // unit) * unit


def split_sum(parts, pieces, row, at):
    rows = parts[0].shape[0] // pieces

    def body(row_ref, *refs):
        ins, outs = refs[: len(parts)], refs[len(parts) :]
        for k, out in enumerate(outs):
            start = (row_ref[at] ^ k) * rows if pieces > 1 else 0
            if pieces > 1:
                start = pl.multiple_of(start, GRANULE)
            total = ins[0][pl.ds(start, rows)].astype(f32)
            for ref in ins[1:]:
                total = total + ref[pl.ds(start, rows)].astype(f32)
            out[...] = total.astype(bf16)

    outs = [((rows, 128), bf16)] * pieces
    return call(body, outs, parts, [row], us=1.0, limit=32)


def joined(parts, row, at):
    rows, pieces = parts[0].shape[0], len(parts)

    def body(row_ref, *refs):
        for k, ref in enumerate(refs[:-1]):
            start = (row_ref[at] ^ k) * rows
            refs[-1][pl.ds(pl.multiple_of(start, GRANULE), rows)] = ref[...]

    outs = [((rows * pieces, 128), bf16)]
    return call(body, outs, parts, [row], us=1.0, limit=32)[0]


def swapped(x):
    return lax.ppermute(x, "segment", [(0, 1), (1, 0)])


class Slab:
    def __init__(self, mine, other, row):
        self.row, self.parts = row, [mine, swapped(other)]

    def to_dp(self):
        self.marks = split_sum(self.parts, lax.axis_size("dp"), self.row, DP)
        self.parts = exchanged(self.marks, "dp")
        return self.marks[:1]

    def to_space(self):
        self.marks = split_sum(self.parts, lax.axis_size("space"), self.row, BAND)
        self.parts = exchanged(self.marks, "space")
        return self.marks[:1]

    def back_space(self):
        self.shard = split_sum(self.parts, 1, self.row, BAND)[0]
        self.parts = copies(self.shard, "space")
        return [self.shard]

    def back_dp(self):
        self.quarter = joined(self.parts, self.row, BAND)
        self.parts = copies(self.quarter, "dp")
        self.parts = self.parts + [swapped(part) for part in self.parts]
        return [self.quarter]


def widened(x):
    more = PADDED - x.shape[1]
    return jnp.concatenate([x, jnp.zeros((2, more), f32)], axis=1) if more else x


def pack_lanes(out, at, x):
    cells, channels = x.shape
    for start in range(0, channels, 128):
        part = x[:, start : start + 128]
        if part.shape[1] < 128:
            part = jnp.concatenate([part, jnp.zeros((cells, 128 - part.shape[1]), f32)], axis=1)
        out[at : at + cells] = part.astype(bf16)
        at += cells
    return at


def unpacked_lanes(ref, at, cells, channels):
    parts = []
    for start in range(0, channels, 128):
        parts.append(ref[at : at + cells, : min(128, channels - start)].astype(f32))
        at += cells
    return jnp.concatenate(parts, axis=1)


def place_slab(slab, pieces, seg, dp, peers):
    rows = pieces[0].shape[0]
    for k, piece in enumerate(pieces):
        side = seg if k < peers else 1 - seg
        at = (side * peers + (dp ^ (k % peers))) * rows
        slab[pl.ds(pl.multiple_of(at, GRANULE), rows)] = piece[...]


def shards(
    inputs,
    crop_group,
    in_proj_4f,
    conv_a_4f,
    conv_b_4f,
    gain_4f,
    bias_4f,
    in_proj_5b,
    conv_a_5b,
    conv_b_5b,
    gain_5b,
    bias_5b,
    out_grad,
):
    order.last = []
    segs, dps, bands = (lax.axis_size(axis) for axis in ("segment", "dp", "space"))
    micro, clips, frames, rows, width, channels = inputs.shape
    full_rows, all_clips = rows * bands, clips * dps
    halves = micro // segs
    held = halves * clips
    items = micro * clips
    spread = segs if items == segs * bands else 1
    assert segs == 2 and items == spread * bands and clips % spread == 0
    each = clips // spread
    cells, part_cells = frames * full_rows * width, frames * rows * width
    frames5, rows5, width5 = frames // 2, full_rows // 2, width // 2
    cells5, part_cells5 = cells // 8, part_cells // 8
    band_rows5 = rows // 2

    inward, pooled_in, outward = [], [], []
    for s in range(segs):
        for z in range(bands):
            for item in range(bands):
                inward.append((s * bands + z, s * bands + item, item, z))
    for m in range(micro):
        for c in range(clips):
            if spread > 1:
                holders = [(c // each) * bands + m * each + c % each]
            else:
                holders = [s * bands + m * clips + c for s in range(segs)]
            home, local = m // halves, (m % halves) * clips + c
            for z in range(bands):
                for holder in holders:
                    pooled_in.append((home * bands + z, holder, local, z))
                outward.append((holders[z % len(holders)], home * bands + z, z, local))
    inward, pooled_in, outward = (
        Route(edges, segs * bands) for edges in (inward, pooled_in, outward)
    )
    IN_BLOCK = TABLES
    IN_SLOT = IN_BLOCK + len(inward.rounds)
    POOLED_BLOCK = IN_SLOT + len(inward.rounds)
    POOLED_SLOT = POOLED_BLOCK + len(pooled_in.rounds)
    OUT_BLOCK = POOLED_SLOT + len(pooled_in.rounds)
    OUT_SLOT = OUT_BLOCK + len(outward.rounds)
    table = []
    for s in range(segs):
        for d in range(dps):
            for z in range(bands):
                me = s * bands + z
                first = s * each if spread > 1 else 0
                counted = 1 if spread > 1 or s == 0 else 0
                line = [s, d, z, first, z // each, counted]
                for route in (inward, pooled_in, outward):
                    line = line + route.blocks[me] + route.slots[me]
                table.append(line)
    row = jnp.array(table, i32)[lax.axis_index(("segment", "dp", "space"))]
    numbers = [row, crop_group]

    def group_parts(x):
        if each > 1:
            pairs = [[z * each + k for k in range(each)] for z in range(micro)]
            x = lax.psum(x, "space", axis_index_groups=pairs)
        if spread > 1:
            x = x + swapped(x)
        if dps > 4:
            return [lax.psum(x, "dp")]
        return copies(x, "dp")

    def total_of(refs):
        return functools.reduce(jnp.add, [ref[...] for ref in refs])

    def crop(row_ref, group_ref, scale=1, m=None):
        group = group_ref[row_ref[MY_MICRO] if m is None else m]
        tall, wide = full_rows // scale, width // scale
        height, across = tall - group * (tall // 4), wide - group * (wide // 4)
        count = all_clips * (frames // scale) * height * across
        return height, across, 1.0 / jnp.full((1, 1), count, i32).astype(f32)

    LEAD, OUTER, STEM = slice(0, B0), slice(0, C_MID), slice(C_MID, None)
    RESTS = slice(B0, C_MID)
    wide4, thin4 = conv_a_4f.reshape(27, B1R, B1), conv_b_4f.reshape(27, B2R, B2)
    wide5, thin5 = conv_a_5b.reshape(27, B1R, B1), conv_b_5b.reshape(27, B2R, B2)

    def project_body(row_ref, group_ref, x_ref, p_ref, stat, pool, *outs):
        for k in range(bands):
            item = row_ref[IN_BLOCK + k]
            m, c = lax.div(item, each), row_ref[FIRST_CLIP] + lax.rem(item, each)
            x = x_ref[m, c].reshape(part_cells, channels)
            height, across, _ = crop(row_ref, group_ref, 1, m)
            mask = mask_of(part_cells, rows, width, height, across, row_ref[BAND] * rows)
            z = dot(x, p_ref[:, B0:]) * mask
            stem = z[:, :STEMS]
            outs[k][...] = stem.astype(bf16)
            pool[k] = z[:, STEMS:].astype(bf16)
            stat[item] = sums(stem, stem)

    got = call(
        project_body,
        [((bands, 2, STEMS), f32), ((bands, part_cells, BP), bf16)]
        + [((part_cells, STEMS), bf16)] * bands,
        [inputs, in_proj_4f],
        numbers,
        us=1.5,
    )
    stem_stat, pool_parts, stem_parts = got[0], got[1], got[2:]
    stem_blocks = inward.send(stem_parts)

    def home_crop(row_ref, group_ref, i):
        m = row_ref[SEG] * halves + i // clips
        height, across, inverse = crop(row_ref, group_ref, 1, m)
        first = row_ref[BAND] * rows
        return m, mask_of(part_cells, rows, width, height, across, first), inverse

    lanes5 = -(-C_MID // 128)
    carried = part_cells + lanes5 * part_cells5

    def lead_body(row_ref, group_ref, x_ref, p_ref, stem_stat, pool, upper, *refs):
        lead_out, stem_out, stat, outs = refs[0], refs[1], refs[2], refs[3:]
        for i in range(held):
            m, mask, _ = home_crop(row_ref, group_ref, i)
            x = x_ref[m, i % clips].reshape(part_cells, channels)
            z = dot(x, p_ref[:, :STEM_END]) * mask
            lead = z[:, :B0]
            lead_out[i] = lead
            stem_out[i] = z[:, B0:]
            total = sums(lead, lead)
            j = bands + i // clips
            stat[j] = total if i % clips == 0 else stat[j] + total
        for k in range(bands):
            stat[k] = widened(stem_stat[k])
            item = row_ref[IN_BLOCK + k]
            m, c = lax.div(item, each), row_ref[FIRST_CLIP] + lax.rem(item, each)
            outs[k][:part_cells] = pool[k]
            pack_lanes(outs[k], part_cells, upper[m, c].astype(f32).reshape(part_cells5, C_MID))

    got = call(
        lead_body,
        [
            ((held, part_cells, B0), f32),
            ((held, part_cells, STEMS), f32),
            ((bands + halves, 2, PADDED), f32),
        ]
        + [((carried, 128), bf16)] * bands,
        [inputs, in_proj_4f, stem_stat, pool_parts, out_grad],
        numbers,
        us=2.5,
    )
    lead, home_stem, stat = got[:3]

    def all_parts(x, axis):
        return [lax.psum(x, axis)] if lax.axis_size(axis) > 4 else copies(x, axis)

    def whole_body(*refs):
        refs[-1][...] = total_of(refs[:-1])

    def summed_dp(x):
        parts = all_parts(x, "dp")
        return call(whole_body, [(x.shape, f32)], parts, us=0.8)[0]

    def share_body(row_ref, own, other, *outs):
        for k, out in enumerate(outs):
            item = row_ref[BAND] ^ k
            first = lax.div(item, each) * each
            total = jnp.zeros((2, PADDED), f32)
            for c in range(each):
                total = total + own[first + c]
                if spread > 1:
                    total = total + other[first + c]
            out[0] = total
            for j in range(halves):
                out[1 + j] = own[bands + j]

    stat = summed_dp(stat)
    stat_parts = call(
        share_body,
        [((1 + halves, 2, PADDED), f32)] * bands,
        [stat, swapped(stat)],
        [row],
        us=0.8,
    )
    stat_parts = exchanged(stat_parts, "space")
    carried_blocks = inward.send(got[3:])

    def arrange_body(gain4, bias4, gain5, bias5, p4, p5, affine4, affine5, proj4, proj5):
        for gain, bias, out in ((gain4, bias4, affine4), (gain5, bias5, affine5)):
            for k, ref in enumerate((gain, bias)):
                v = ref[...]
                out[k : k + 1] = jnp.concatenate(
                    [
                        v[:, :B0],
                        v[:, STEM_END:FIRST],
                        v[:, FIRST + B1 :],
                        v[:, FIRST : FIRST + B1],
                        v[:, B0:STEM_END],
                    ],
                    axis=1,
                )
        proj4[:, :B0] = p4[:, :B0]
        proj4[:, B0:] = jnp.concatenate([p4[:, STEM_END:], p4[:, B0:STEM_END]], axis=1)
        for first, last, to in ((0, B0, 0), (STEM_END, FIRST, B0), (B0, STEM_END, B0 + BP)):
            rows_in = p5[first:last]
            proj5[to : to + last - first, :B0] = rows_in[:, :B0]
            proj5[to : to + last - first, B0:] = jnp.concatenate(
                [
                    rows_in[:, B0 + SECOND :],
                    rows_in[:, B0 + B1 : B0 + SECOND],
                    rows_in[:, B0 : B0 + B1],
                ],
                axis=1,
            )

    affine4, affine5, proj4, proj5 = call(
        arrange_body,
        [((2, 1024), f32)] * 2 + [((channels, FIRST), bf16), ((FIRST, C_MID), bf16)],
        [v.reshape(1, -1) for v in (gain_4f, bias_4f, gain_5b, bias_5b)]
        + [in_proj_4f, in_proj_5b.T],
        us=2.0,
    )

    def lead_act(i, lead_ref, stat_ref, affine_ref, inverse):
        mean, scale = moments(stat_ref[i // clips], inverse)
        norm = (lead_ref[i] - mean) * scale
        return norm, scale, norm * affine_ref[0:1, LEAD] + affine_ref[1:2, LEAD]

    def lead_out_body(row_ref, group_ref, lead_ref, affine_ref, *refs):
        parts, stat_ref, outs, kept = refs[:bands], refs[bands], refs[bands + 1 : -1], refs[-1]
        stat_ref[...] = total_of(parts)[1:]
        matrix = pool_matrix(frames, rows, width, False)
        for i in range(held):
            _, mask, inverse = home_crop(row_ref, group_ref, i)
            _, _, active = lead_act(i, lead_ref, stat_ref, affine_ref, inverse)
            kept[i] = dot(matrix, (silu(active) * mask).astype(bf16)).astype(bf16)
        for turn, out in enumerate(outs):
            out[...] = kept[row_ref[POOLED_BLOCK + turn]]

    got = call(
        lead_out_body,
        [((halves, 2, B0), f32)] + [((part_cells5, B0), bf16)] * len(pooled_in.rounds),
        [lead, affine4] + stat_parts,
        numbers,
        [((held, part_cells5, B0), bf16)],
        us=1.8,
    )
    lead_stat = got[0]
    lead_pooled = pooled_in.send(got[1:])

    step = 2 if full_rows * width <= 128 else 1

    def conv_body(row_ref, group_ref, affine_ref, wide_ref, thin_ref, *refs):
        stats, blocks = refs[:bands], refs[bands : 2 * bands]
        second_out, sums_out, norm_out, stat_out, beside, stage, flat = refs[2 * bands :]
        height, across, inverse = crop(row_ref, group_ref)
        totals = functools.reduce(jnp.add, [ref[0] for ref in stats])[:, :STEMS]
        mean, scale = moments(totals, inverse)
        stat_out[...] = totals
        fill_conv_weights(flat, wide_ref, thin_ref)
        slots = [row_ref[IN_SLOT + k] for k in range(bands)]
        place_bands(stage, blocks, slots, frames, rows, width)
        mask = mask_of(cells, full_rows, width, height, across)
        norm = (stage[...].reshape(cells, STEMS) - mean) * scale
        norm_out[...] = norm
        active = norm * affine_ref[0:1, STEM] + affine_ref[1:2, STEM]
        fill_beside(beside, silu(active) * mask, frames, full_rows, width)
        chunk = step * full_rows * width
        total = jnp.zeros((2, SECOND), f32)
        for start in range(0, frames, step):
            got = conv_chunk(beside, flat, start, step, full_rows)
            second_out[start * full_rows * width : start * full_rows * width + chunk] = got
            total = total + sums(got * mask[:chunk], got)
        sums_out[...] = total

    second, second_sums, stem_norm, stem_total, beside = call(
        conv_body,
        [
            ((cells, SECOND), f32),
            ((2, SECOND), f32),
            ((cells, STEMS), f32),
            ((2, STEMS), f32),
            ((frames + 2, full_rows + 2, width, BESIDE), bf16),
        ],
        [affine4, wide4, thin4] + stat_parts + stem_blocks,
        numbers,
        [
            ((frames, full_rows, width, STEMS), f32),
            ((9 * BESIDE, SECOND), bf16),
        ],
        us=9.0,
    )

    def pool_body(row_ref, group_ref, second_sums, *refs):
        blocks, (zp_out, sums_out, stage) = refs[:bands], refs[bands:]
        height, across, _ = crop(row_ref, group_ref)
        slots = [row_ref[IN_SLOT + k] for k in range(bands)]
        place_bands(stage, [ref.at[:part_cells] for ref in blocks], slots, frames, rows, width)
        zp = box_mean(stage[...].reshape(cells, BP), frames, full_rows, width)
        zp_out[...] = zp
        mask = mask_of(cells, full_rows, width, height, across)
        sums_out[...] = jnp.concatenate([sums(zp * mask, zp), second_sums[...]], axis=1)

    zp, rest_sums = call(
        pool_body,
        [((cells, BP), f32), ((2, REST), f32)],
        [second_sums] + carried_blocks,
        numbers,
        [((frames, full_rows, width, BP), f32)],
        us=1.3,
    )
    rest_parts = group_parts(rest_sums)
    n_parts = len(rest_parts)

    span = 2 * full_rows * width

    def rest_of(zp_ref, second_ref, start, affine_ref, mean, scale):
        z = jnp.concatenate(
            [zp_ref[start : start + span], second_ref[start : start + span]], axis=1
        )
        norm = (z - mean) * scale
        return norm, norm * affine_ref[0:1, RESTS] + affine_ref[1:2, RESTS]

    def middle_body(row_ref, group_ref, affine_ref, p_ref, zp_ref, second_ref, *refs):
        parts, leads = refs[:n_parts], refs[n_parts:-6]
        stat_out, pooled, first_out, sums_out, stage, kept = refs[-6:]
        height, across, inverse = crop(row_ref, group_ref)
        mean, scale = moments(total_of(parts), inverse)
        stat_out[...] = jnp.concatenate([mean, scale], axis=0)
        mask = mask_of(span, full_rows, width, height, across)
        matrix = pool_matrix(2, full_rows, width, False)
        slots = [row_ref[POOLED_SLOT + k] for k in range(len(leads))]
        place_bands(stage, leads, slots, frames5, band_rows5, width5)
        pooled[:, :B0] = stage[...].reshape(cells5, B0).astype(bf16)
        for f in range(frames5):
            _, active = rest_of(zp_ref, second_ref, f * span, affine_ref, mean, scale)
            out = dot(matrix, (silu(active) * mask).astype(bf16))
            pooled[f * span // 8 : (f + 1) * span // 8, B0:] = out.astype(bf16)
        z = dot_nt(pooled[...], p_ref[...])
        kept[...] = z
        project = z[:, LEAD.stop : LEAD.stop + BP].astype(bf16).astype(f32)
        kept[:, B0 : B0 + BP] = box_mean(project, frames5, rows5, width5)
        z = kept[...]
        first_out[...] = z
        height, across, _ = crop(row_ref, group_ref, 2)
        sums_out[...] = sums(z * mask_of(cells5, rows5, width5, height, across), z)

    rest_stat, pooled, first5, first5_sums = call(
        middle_body,
        [((2, REST), f32), ((cells5, C_MID), bf16), ((cells5, FIRST), f32), ((2, FIRST), f32)],
        [affine4, proj5, zp, second] + rest_parts + lead_pooled,
        numbers,
        [((frames5, rows5, width5, B0), f32), ((cells5, FIRST), f32)],
    )
    first5_parts = group_parts(first5_sums)

    def conv5_body(row_ref, group_ref, affine_ref, wide_ref, thin_ref, first_ref, *refs):
        parts = refs[:n_parts]
        second_out, sums_out, stat_out, beside, flat = refs[n_parts:]
        height, across, inverse = crop(row_ref, group_ref, 2)
        mean, scale = moments(total_of(parts), inverse)
        stat_out[...] = jnp.concatenate([mean, scale], axis=0)
        fill_conv_weights(flat, wide_ref, thin_ref)
        mask = mask_of(cells5, rows5, width5, height, across)
        stem = slice(B0 + BP, FIRST)
        norm = (first_ref[:, stem] - mean[:, stem]) * scale[:, stem]
        active = norm * affine_ref[0:1, STEM] + affine_ref[1:2, STEM]
        fill_beside(beside, silu(active) * mask, frames5, rows5, width5)
        got = conv_chunk(beside, flat, 0, frames5, rows5)
        second_out[...] = got
        sums_out[...] = sums(got * mask, got)

    second5, second5_sums, first5_stat, beside5 = call(
        conv5_body,
        [
            ((cells5, SECOND), f32),
            ((2, SECOND), f32),
            ((2, FIRST), f32),
            ((frames5 + 2, rows5 + 2, width5, BESIDE), f32),
        ],
        [affine5, wide5, thin5, first5] + first5_parts,
        numbers,
        [((9 * BESIDE, SECOND), bf16)],
    )
    second5_parts = group_parts(second5_sums)

    def out5_body(row_ref, group_ref, affine_ref, first_ref, stat_ref, second_ref, *refs):
        parts, uppers = refs[:n_parts], refs[n_parts : n_parts + bands]
        out, norm_out, slope_out, scale_out, sums_out, stage = refs[n_parts + bands :]
        height, across, inverse = crop(row_ref, group_ref, 2)
        mean2, scale2 = moments(total_of(parts), inverse)
        mask = mask_of(cells5, rows5, width5, height, across)
        outer = slice(0, B0 + BP)
        mean = jnp.concatenate([stat_ref[0:1, outer], mean2], axis=1)
        scale = jnp.concatenate([stat_ref[1:2, outer], scale2], axis=1)
        z = jnp.concatenate([first_ref[:, outer], second_ref[...]], axis=1)
        norm = (z - mean) * scale
        active = norm * affine_ref[0:1, OUTER] + affine_ref[1:2, OUTER]
        act = silu(active) * mask
        natural = [act[:, :B0], act[:, B0 + BP + B2 :], act[:, B0 + BP : B0 + BP + B2]]
        natural = jnp.concatenate(natural + [act[:, B0 : B0 + BP]], axis=1)
        out[...] = natural.reshape(frames5, rows5, width5, C_MID)
        for k, ref in enumerate(uppers):
            part = unpacked_lanes(ref, part_cells, part_cells5, C_MID)
            part = part.reshape(frames5, band_rows5, width5, C_MID)
            stage[:, pl.ds(row_ref[IN_SLOT + k] * band_rows5, band_rows5)] = part
        upper = stage[...].reshape(cells5, C_MID)
        upper = jnp.concatenate(
            [
                upper[:, :B0],
                upper[:, B0 + SECOND :],
                upper[:, B0 + B1 : B0 + SECOND],
                upper[:, B0 : B0 + B1],
            ],
            axis=1,
        )
        slopes = slope(active, upper * mask)
        norm_out[...] = norm
        slope_out[...] = slopes
        scale_out[...] = scale
        sums_out[...] = sums(slopes, norm)

    out5, outer5_norm, outer5_slope, outer5_scale, outer5_sums = call(
        out5_body,
        [
            ((frames5, rows5, width5, C_MID), f32),
            ((cells5, C_MID), f32),
            ((cells5, C_MID), f32),
            ((1, C_MID), f32),
            ((2, C_MID), f32),
        ],
        [affine5, first5, first5_stat, second5] + second5_parts + carried_blocks,
        numbers,
        [((frames5, rows5, width5, C_MID), f32)],
        us=1.4,
    )
    outer5_parts = group_parts(outer5_sums)

    def back5_body(row_ref, group_ref, affine_ref, wide_ref, thin_ref, *refs):
        norm_ref, slope_ref, scale_ref, first_ref, stat_ref = refs[:5]
        parts, refs = refs[5 : 5 + n_parts], refs[5 + n_parts :]
        dz_out, lead_out, project_out, slope_out, sums_out, shifted, flat = refs
        height, across, inverse = crop(row_ref, group_ref, 2)
        mask = mask_of(cells5, rows5, width5, height, across)
        fill_back_weights(flat, wide_ref, thin_ref)
        total = total_of(parts) * inverse
        grad = (mask * (affine_ref[0:1, OUTER] * scale_ref[...])) * (
            slope_ref[...] - total[0:1] - norm_ref[...] * total[1:2]
        )
        lead_out[...] = grad[:, :B0]
        low = grad[:, B0:].astype(bf16)
        dz = low[:, BP:]
        dz_out[...] = dz
        project_out[...] = box_mean(low[:, :BP].astype(f32), frames5, rows5, width5)
        fill_shifted(shifted, dz.astype(f32), frames5, rows5, width5)
        upper = back_chunk(shifted, flat, 0, frames5, rows5)
        stem = slice(B0 + BP, FIRST)
        norm = (first_ref[:, stem] - stat_ref[0:1, stem]) * stat_ref[1:2, stem]
        active = norm * affine_ref[0:1, STEM] + affine_ref[1:2, STEM]
        slopes = slope(active, upper * mask)
        slope_out[...] = slopes
        sums_out[...] = sums(slopes, norm)

    dz5, lead5_grad, project5_grad, stem5_slope, stem5_sums = call(
        back5_body,
        [
            ((cells5, SECOND), bf16),
            ((cells5, B0), f32),
            ((cells5, BP), f32),
            ((cells5, STEMS), f32),
            ((2, STEMS), f32),
        ],
        [affine5, wide5, thin5, outer5_norm, outer5_slope, outer5_scale, first5, first5_stat]
        + outer5_parts,
        numbers,
        [
            ((3, frames5 + 2, rows5 + 2, width5, 512), f32),
            ((STEMS, 27 * 512), bf16),
        ],
    )
    stem5_parts = group_parts(stem5_sums)

    rows_conv = padded_rows(CONV_ROWS)

    def weights5_body(row_ref, beside, dz_ref, mine, other, slab):
        scale = jnp.full((1, 1), row_ref[COUNTED], i32).astype(f32)
        pack_conv(slab, beside, dz_ref[...], frames5, rows5, width5, scale)
        slab[CONV_ROWS:] = jnp.zeros((rows_conv - CONV_ROWS, 128), bf16)
        give_halves(slab, row_ref[SEG], mine, other)

    mine5, other5 = call(
        weights5_body,
        [((rows_conv // 2, 128), bf16)] * 2,
        [beside5, dz5],
        [row],
        [((rows_conv, 128), bf16)],
        us=3.5,
    )
    slab5 = Slab(mine5, other5, row)

    def rest_slope(f, pooled_grad, matrix, mask, zp_ref, second_ref, affine_ref, stat_ref):
        norm, active = rest_of(
            zp_ref, second_ref, f * span, affine_ref, stat_ref[0:1], stat_ref[1:2]
        )
        upper = dot(matrix, pooled_grad[f * span // 8 : (f + 1) * span // 8])
        return norm, slope(active, upper * mask)

    def first5_body(row_ref, group_ref, affine_ref, affine4_ref, p_ref, *refs):
        lead_ref, project_ref, slope_ref, first_ref, stat_ref = refs[:5]
        zp_ref, second_ref, rest_stat = refs[5:8]
        parts, refs = refs[8 : 8 + n_parts], refs[8 + n_parts :]
        lead_out, projected_out, rest_out, sums_out = refs
        height, across, inverse = crop(row_ref, group_ref, 2)
        mask = mask_of(cells5, rows5, width5, height, across)
        total = total_of(parts) * inverse
        stem = slice(B0 + BP, FIRST)
        norm = (first_ref[:, stem] - stat_ref[0:1, stem]) * stat_ref[1:2, stem]
        stem_grad = (mask * (affine_ref[0:1, STEM] * stat_ref[1:2, stem])) * (
            slope_ref[...] - total[0:1] - norm * total[1:2]
        )
        projected = jnp.concatenate([lead_ref[...], project_ref[...], stem_grad], axis=1)
        projected = projected.astype(bf16)
        projected_out[...] = projected
        pooled_grad = dot(projected, p_ref[...]).astype(bf16)
        lead_out[...] = pooled_grad[:, :B0].astype(f32).reshape(frames5, rows5, width5, B0)
        rest_grad = pooled_grad[:, B0:]
        rest_out[...] = rest_grad
        height, across, _ = crop(row_ref, group_ref)
        mask = mask_of(span, full_rows, width, height, across)
        matrix = pool_matrix(2, full_rows, width, True)
        total = jnp.zeros((2, REST), f32)
        for f in range(frames5):
            norm, slopes = rest_slope(
                f, rest_grad, matrix, mask, zp_ref, second_ref, affine4_ref, rest_stat
            )
            total = total + sums(slopes, norm)
        sums_out[...] = total

    lead_grad5, projected5_grad, rest_upper, rest_grad_sums = call(
        first5_body,
        [
            ((frames5, rows5, width5, B0), f32),
            ((cells5, FIRST), bf16),
            ((cells5, REST), bf16),
            ((2, REST), f32),
        ],
        [affine5, affine4, proj5, lead5_grad, project5_grad, stem5_slope, first5, first5_stat]
        + [zp, second, rest_stat]
        + stem5_parts,
        numbers,
        us=2.4,
    )
    rest_grad_parts = group_parts(rest_grad_sums)

    def natural(outer, stem):
        pool, thin, wide = (
            outer[:, B0 : B0 + BP],
            outer[:, B0 + BP : B0 + BP + B2],
            outer[:, B0 + BP + B2 :],
        )
        return jnp.concatenate([outer[:, :B0], stem, pool, wide, thin], axis=1)

    slab5.to_dp()

    rows_first5 = matrix_rows(FIRST, C_MID) + 16

    def weights_first5_body(row_ref, pooled_ref, projected_ref, outer_ref, stem_ref, out):
        scale = jnp.full((1, 1), row_ref[COUNTED], i32).astype(f32)
        at = pack_matrix(out, 0, dot_tn(projected_ref[...], pooled_ref[...]) * scale)
        norms = natural(outer_ref[...], stem_ref[...]) * scale
        pack_norms(out, at, norms[1:2], norms[0:1])

    (packed_first5,) = call(
        weights_first5_body,
        [((rows_first5, 128), bf16)],
        [pooled, projected5_grad, outer5_sums, stem5_sums],
        [row],
        us=1.2,
    )

    def back4_body(row_ref, group_ref, affine_ref, zp_ref, second_ref, stat_ref, grad_ref, *refs):
        parts, (out5_ref, lead_ref), refs = refs[:n_parts], refs[n_parts : n_parts + 2], refs[n_parts + 2 :]
        outs, (dz_out, kept) = refs[: len(outward.rounds)], refs[len(outward.rounds) :]
        height, across, inverse = crop(row_ref, group_ref)
        mask = mask_of(span, full_rows, width, height, across)
        total = total_of(parts) * inverse
        matrix = pool_matrix(2, full_rows, width, True)
        factor = affine_ref[0:1, RESTS] * stat_ref[1:2]
        for f in range(frames5):
            norm, slopes = rest_slope(
                f, grad_ref, matrix, mask, zp_ref, second_ref, affine_ref, stat_ref
            )
            grad = (mask * factor) * (slopes - total[0:1] - norm * total[1:2])
            low = grad.astype(bf16)
            dz_out[f * span : (f + 1) * span] = low[:, BP:]
            kept[2 * f : 2 * f + 2] = low[:, :BP].astype(f32).reshape(2, full_rows, width, BP)
        pool = box_mean(kept[...].reshape(cells, BP), frames, full_rows, width)
        kept[...] = pool.reshape(frames, full_rows, width, BP)
        for turn, out in enumerate(outs):
            part = kept[:, pl.ds(row_ref[OUT_BLOCK + turn] * rows, rows)]
            out[:part_cells] = part.reshape(part_cells, BP).astype(bf16)
            start = row_ref[OUT_BLOCK + turn] * band_rows5
            part = lead_ref[:, pl.ds(start, band_rows5)].reshape(part_cells5, B0)
            at = pack_lanes(out, part_cells, part)
            part = out5_ref[:, pl.ds(start, band_rows5)].reshape(part_cells5, C_MID)
            pack_lanes(out, at, part)

    carried_out = carried + B0 // 128 * part_cells5
    got = call(
        back4_body,
        [((carried_out, 128), bf16)] * len(outward.rounds) + [((cells, SECOND), bf16)],
        [affine4, zp, second, rest_stat, rest_upper] + rest_grad_parts + [out5, lead_grad5],
        numbers,
        [((frames, full_rows, width, BP), f32)],
        us=2.6,
    )
    carried_grads = outward.send(got[: len(outward.rounds)])
    dz = got[-1]

    def weights4_body(row_ref, beside, dz_ref, mine, other, slab):
        scale = jnp.full((1, 1), row_ref[COUNTED], i32).astype(f32)
        pack_conv(slab, beside, dz_ref[...], frames, full_rows, width, scale)
        slab[CONV_ROWS:] = jnp.zeros((rows_conv - CONV_ROWS, 128), bf16)
        give_halves(slab, row_ref[SEG], mine, other)

    mine4, other4 = call(
        weights4_body,
        [((rows_conv // 2, 128), bf16)] * 2,
        [beside, dz],
        [row],
        [((rows_conv, 128), bf16)],
        us=10.5,
    )
    slab4 = Slab(mine4, other4, row)

    def lead_slopes(i, row_ref, group_ref, lead_ref, stat_ref, affine_ref, matrix, kept):
        _, mask, inverse = home_crop(row_ref, group_ref, i)
        norm, scale, active = lead_act(i, lead_ref, stat_ref, affine_ref, inverse)
        upper = dot(matrix, kept[i])
        return mask, inverse, scale, norm, slope(active, upper * mask)

    def lead_back_body(row_ref, group_ref, lead_ref, stat_ref, affine_ref, *refs):
        blocks, (sums_out, kept, out) = refs[:held], refs[held:]
        matrix = pool_matrix(frames, rows, width, True)
        for turn, ref in enumerate(blocks):
            place = row_ref[OUT_SLOT + turn]
            at = part_cells + B0 // 128 * part_cells5
            part = unpacked_lanes(ref, part_cells, part_cells5, B0)
            kept[place] = part.astype(bf16)
            part = unpacked_lanes(ref, at, part_cells5, C_MID)
            out[place] = part.reshape(frames5, band_rows5, width5, C_MID).astype(bf16)
        for i in range(held):
            _, _, _, norm, slopes = lead_slopes(
                i, row_ref, group_ref, lead_ref, stat_ref, affine_ref, matrix, kept
            )
            total = sums(slopes, norm)
            j = i // clips
            sums_out[j] = total if i % clips == 0 else sums_out[j] + total

    lead_sums, lead_upper, block_out = call(
        lead_back_body,
        [
            ((halves, 2, B0), f32),
            ((held, part_cells5, B0), bf16),
            ((held, frames5, band_rows5, width5, C_MID), bf16),
        ],
        [lead, lead_stat, affine4] + carried_grads,
        numbers,
        us=2.0,
    )
    block_out = block_out.reshape(halves, clips, frames5, band_rows5, width5, C_MID)

    def stems4_body(row_ref, group_ref, affine_ref, wide_ref, thin_ref, dz_ref, norm_ref, lead_ref, *refs):
        outs, refs = refs[: len(outward.rounds)], refs[len(outward.rounds) :]
        sums_out, shifted, flat, kept = refs
        height, across, _ = crop(row_ref, group_ref)
        fill_back_weights(flat, wide_ref, thin_ref)
        fill_shifted(shifted, dz_ref[...].astype(f32), frames, full_rows, width)
        chunk = step * full_rows * width
        mask = mask_of(chunk, full_rows, width, height, across)
        total = jnp.zeros((2, STEMS), f32)
        for start in range(0, frames, step):
            upper = back_chunk(shifted, flat, start, step, full_rows)
            at = start * full_rows * width
            norm = norm_ref[at : at + chunk]
            active = norm * affine_ref[0:1, STEM] + affine_ref[1:2, STEM]
            slopes = slope(active, upper * mask)
            kept[start : start + step] = slopes.reshape(step, full_rows, width, STEMS)
            total = total + sums(slopes, norm)
        sums_out[0] = widened(total)
        sums_out[1:] = lead_ref[...]
        for turn, out in enumerate(outs):
            part = kept[:, pl.ds(row_ref[OUT_BLOCK + turn] * rows, rows)]
            out[...] = part.reshape(part_cells, STEMS).astype(bf16)

    got = call(
        stems4_body,
        [((part_cells, STEMS), bf16)] * len(outward.rounds)
        + [((1 + halves, 2, PADDED), f32)],
        [affine4, wide4, thin4, dz, stem_norm, lead_sums],
        numbers,
        [
            ((3, frames + 2, full_rows + 2, width, 512), bf16),
            ((STEMS, 27 * 512), bf16),
            ((frames, full_rows, width, STEMS), f32),
        ],
        us=9.0,
    )
    stem_slopes = outward.send(got[: len(outward.rounds)])
    last_sums = got[-1]

    def last_body(own, other, stat, out):
        total = own[0]
        if spread > 1:
            total = total + other[0]
        out[0] = total
        out[1 : 1 + halves] = own[1:]
        out[1 + halves] = widened(stat[...])

    slab4.to_dp()
    last = summed_dp(last_sums)
    if each > 1:
        pairs = [[z * each + k for k in range(each)] for z in range(micro)]
        last = jnp.concatenate(
            [lax.psum(last[:1], "space", axis_index_groups=pairs), last[1:]], axis=0
        )
    (last,) = call(
        last_body,
        [((2 + halves, 2, PADDED), f32)],
        [last, swapped(last), stem_total],
        us=0.8,
    )
    last_parts = copies(last, "space")
    slab5.to_space()

    rows_first4 = matrix_rows(channels, FIRST) + 16
    rows_proj = padded_rows(rows_first4 + rows_first5)

    def first4_body(row_ref, group_ref, x_ref, affine_ref, lead_ref, stat_ref, *refs):
        upper_ref, stem_ref, last_sums, rest_sums, packed_ref = refs[:5]
        parts, refs = refs[5 : 5 + bands], refs[5 + bands :]
        slopes_in, pools_in, refs = refs[:held], refs[held : 2 * held], refs[2 * held :]
        projected, mine, other, x_all, slab, late, stem_all = refs
        lead_total = functools.reduce(
            jnp.add, [ref[1 : 1 + halves] for ref in parts]
        )
        matrix = pool_matrix(frames, rows, width, True)
        for turn in range(held):
            place = row_ref[OUT_SLOT + turn]
            late[place, :, :BP] = pools_in[turn][:part_cells].astype(f32)
            late[place, :, BP:] = slopes_in[turn][...].astype(f32)
        for k in range(bands):
            stem_all[k, 0] = parts[k][0]
            stem_all[k, 1] = parts[k][1 + halves]
        for i in range(held):
            mask, inverse, scale, norm, slopes = lead_slopes(
                i, row_ref, group_ref, lead_ref, stat_ref, affine_ref, matrix, upper_ref
            )
            total = lead_total[i // clips] * inverse
            lead_grad = (affine_ref[0:1, LEAD] * scale) * (
                slopes - total[0:1] - norm * total[1:2]
            )
            m = row_ref[SEG] * halves + i // clips
            turn = row_ref[BAND] ^ (m * each)
            mean, scale = moments(stem_all[turn, 1][:, :STEMS], inverse)
            total = stem_all[turn, 0][:, :STEMS] * inverse
            norm = (stem_ref[i] - mean) * scale
            stem_grad = (affine_ref[0:1, STEM] * scale) * (
                late[i, :, BP:] - total[0:1] - norm * total[1:2]
            )
            grad = jnp.concatenate([lead_grad, late[i, :, :BP], stem_grad], axis=1) * mask
            at = i * part_cells
            projected[at : at + part_cells] = grad.astype(bf16)
            x_all[at : at + part_cells] = x_ref[m, i % clips].reshape(part_cells, channels)
        at = pack_matrix(slab, 0, dot_tn(x_all[...], projected[...]))
        counted = jnp.full((1, 1), row_ref[COUNTED], i32).astype(f32)
        own = jnp.sum(last_sums[1:], axis=0)
        rest = rest_sums[...] * counted
        stem = last_sums[0][:, :STEMS] * counted
        norms = natural(jnp.concatenate([own, rest], axis=1), stem)
        pack_norms(slab, at, norms[1:2], norms[0:1])
        slab[rows_first4 : rows_first4 + rows_first5] = packed_ref[...]
        slab[rows_first4 + rows_first5 :] = jnp.zeros(
            (rows_proj - rows_first4 - rows_first5, 128), bf16
        )
        give_halves(slab, row_ref[SEG], mine, other)

    projected_grad, mine_proj, other_proj = call(
        first4_body,
        [((held * part_cells, FIRST), bf16)] + [((rows_proj // 2, 128), bf16)] * 2,
        [inputs, affine4, lead, lead_stat, lead_upper, home_stem, last_sums, rest_grad_sums]
        + [packed_first5]
        + last_parts
        + stem_slopes
        + carried_grads,
        numbers,
        [
            ((held * part_cells, channels), bf16),
            ((rows_proj, 128), bf16),
            ((held, part_cells, BP + STEMS), f32),
            ((bands, 2, 2, PADDED), f32),
        ],
        us=4.0,
    )
    slab_proj = Slab(mine_proj, other_proj, row)
    slab_proj.to_dp()
    slab5.back_space()
    slab4.to_space()

    def input_body(projected_ref, p_ref, out):
        for i in range(held):
            at = i * part_cells
            got = dot_nt(projected_ref[at : at + part_cells], p_ref[...])
            out[i // clips, i % clips] = got.reshape(frames, rows, width, channels)

    (input_grad,) = call(
        input_body,
        [((halves, clips, frames, rows, width, channels), f32)],
        [projected_grad, proj4],
    )

    def unpacked(slab_way, n_rows, body, outs, us):
        pieces = slab_way.parts

        def whole(row_ref, *refs):
            slab = refs[-1]
            place_slab(slab, refs[: len(pieces)], row_ref[SEG], row_ref[DP], dps)
            body(slab, *refs[len(pieces) : -1])

        scratch = [((n_rows, 128), bf16)]
        return call(whole, outs, pieces, [row], scratch, us=us, limit=48)

    def unpack_proj(slab, proj_out, norm_out, proj5_out, norm5_out):
        parts, at = unpack_matrix(slab, 0, channels, FIRST)
        proj_out[:, :128] = parts[0]
        proj_out[:, 128:256] = parts[1]
        proj_out[:, 256:] = jnp.concatenate([parts[3], parts[4], parts[2]], axis=1)
        norm_out[...] = slab[at : at + 16].astype(f32)
        parts, at = unpack_matrix(slab, rows_first4, FIRST, C_MID)
        lead = parts[:2]
        tail = jnp.concatenate([parts[6], parts[3], parts[2]], axis=1)
        for first, last, place in ((0, B0, 0), (B0, B0 + BP, STEM_END), (B0 + BP, FIRST, B0)):
            to = slice(place, place + last - first)
            proj5_out[to, 0:128] = lead[0][first:last]
            proj5_out[to, 128:256] = lead[1][first:last]
            proj5_out[to, 256:384] = parts[4][first:last]
            proj5_out[to, 384:512] = parts[5][first:last]
            proj5_out[to, 512:] = tail[first:last]
        norm5_out[...] = slab[at : at + 16].astype(f32)

    slab5.back_dp()
    slab4.back_space()
    slab_proj.to_space()
    slab4.back_dp()
    slab_proj.back_space()
    conv_outs = [((27, B1R, B1), f32), ((27, B2R, B2), f32)]
    wide5_grad, thin5_grad = unpacked(slab5, rows_conv, unpack_conv, conv_outs, 4.0)
    slab_proj.back_dp()
    wide4_grad, thin4_grad = unpacked(slab4, rows_conv, unpack_conv, conv_outs, 4.0)
    proj4_grad, norms4, proj5_grad, norms5 = unpacked(
        slab_proj,
        rows_proj,
        unpack_proj,
        [((channels, FIRST), f32), ((16, 128), f32), ((FIRST, C_MID), f32), ((16, 128), f32)],
        2.5,
    )
    return (
        block_out,
        input_grad,
        proj4_grad,
        wide4_grad.reshape(conv_a_4f.shape),
        thin4_grad.reshape(conv_b_4f.shape),
        norms4[:8].reshape(-1),
        norms4[8:].reshape(-1),
        proj5_grad.T,
        wide5_grad.reshape(conv_a_5b.shape),
        thin5_grad.reshape(conv_b_5b.shape),
        norms5[:8].reshape(-1),
        norms5[8:].reshape(-1),
    )


def solution(mesh):
    banded = P(None, "dp", None, "space", None, None)
    halved_specs = P("segment", "dp", None, "space", None, None)
    in_specs = (banded,) + (P(),) * 11 + (banded,)
    out_specs = (halved_specs, halved_specs) + (P(),) * 10
    return jax.shard_map(shards, mesh=mesh, in_specs=in_specs, out_specs=out_specs, check_vma=False)
```

```python
import functools

import jax
import jax.numpy as jnp
from jax import lax
from jax.experimental import pallas as pl
from jax.experimental.pallas import tpu as pltpu
from jax.sharding import PartitionSpec as P

B0 = 256
B1R = 160
B2R = 32
B1 = 320
B2 = 128
BP = 128
FIRST = 576
STEMS = B1R + B2R
STEM_END = B0 + STEMS
SECOND = B1 + B2
REST = SECOND + BP
C_MID = B0 + REST
BESIDE = 640
GRANULE = 16
SCALE = 3.0
PADDED = 256

SEG, DP, BAND, FIRST_CLIP, MY_MICRO, COUNTED, TABLES = range(7)

epsilon = 0.001
bf16 = jnp.bfloat16
f32 = jnp.float32
i32 = jnp.int32


def matching(edges):
    by_sender = {}
    for edge in edges:
        by_sender.setdefault(edge[0], []).append(edge)
    taken = {}

    def place(sender, seen):
        for edge in by_sender[sender]:
            receiver = edge[1]
            if receiver in seen:
                continue
            seen.add(receiver)
            if receiver not in taken or place(taken[receiver][0], seen):
                taken[receiver] = edge
                return True
        return False

    for sender in sorted(by_sender):
        place(sender, set())
    return sorted(taken.values())


class Route:
    def __init__(self, edges, devices):
        left, self.rounds = list(edges), []
        while left:
            chosen = matching(left)
            for edge in chosen:
                left.remove(edge)
            self.rounds.append(chosen)
        self.blocks = [[0] * len(self.rounds) for _ in range(devices)]
        self.slots = [[0] * len(self.rounds) for _ in range(devices)]
        for turn, chosen in enumerate(self.rounds):
            for sender, receiver, block, slot in chosen:
                self.blocks[sender][turn] = block
                self.slots[receiver][turn] = slot

    def send(self, parts):
        got = []
        for part, chosen in zip(parts, self.rounds):
            if all(edge[0] == edge[1] for edge in chosen):
                got.append(part)
            else:
                pairs = [(edge[0], edge[1]) for edge in chosen]
                got.append(lax.ppermute(part, ("segment", "space"), pairs))
        return got


def pairing(peers, step):
    return [(i, i ^ step) for i in range(peers)]


def exchanged(parts, axis):
    peers = lax.axis_size(axis)
    assert peers & (peers - 1) == 0
    return [parts[0]] + [lax.ppermute(parts[k], axis, pairing(peers, k)) for k in range(1, peers)]


def copies(x, axis):
    return exchanged([x] * lax.axis_size(axis), axis)


def sum_over(x, axis):
    if lax.axis_size(axis) > 4:
        return lax.psum(x, axis)
    got = copies(x, axis)
    return functools.reduce(jnp.add, got)


class Order:
    def __init__(self):
        self.last = []


order = Order()


def call(body, outs, ins, numbers=(), scratch=(), us=2.0, limit=40):
    vmem = pl.BlockSpec(memory_space=pltpu.VMEM)
    smem = pl.BlockSpec(memory_space=pltpu.SMEM)
    skipped, after = len(numbers) + len(ins), order.last

    def waited(*refs):
        body(*refs[:skipped], *refs[skipped + len(after) :])

    got = pl.pallas_call(
        waited,
        out_shape=[jax.ShapeDtypeStruct(shape, dtype) for shape, dtype in outs],
        in_specs=[smem] * len(numbers)
        + [vmem] * len(ins)
        + [pl.BlockSpec(memory_space=pl.ANY)] * len(after),
        out_specs=[vmem] * len(outs),
        scratch_shapes=[pltpu.VMEM(shape, dtype) for shape, dtype in scratch],
        cost_estimate=pl.CostEstimate(
            flops=int(us * SCALE * 1.1e9), bytes_accessed=10**6, transcendentals=0
        ),
        compiler_params=pltpu.CompilerParams(vmem_limit_bytes=limit * 2**20),
    )(*numbers, *ins, *after)
    order.last = [got[-1]]
    return got


def dot(a, b):
    return jnp.dot(a, b, preferred_element_type=f32)


def dot_nt(a, b):
    return lax.dot_general(a, b, (((1,), (1,)), ((), ())), preferred_element_type=f32)


def dot_tn(a, b):
    return lax.dot_general(a, b, (((0,), (0,)), ((), ())), preferred_element_type=f32)


def mask_of(cells, rows, width, height, across, first_row=0):
    place = lax.broadcasted_iota(i32, (cells, 1), 0)
    column = lax.rem(place, width)
    row = lax.rem(lax.div(place, width), rows) + first_row
    return jnp.where((row < height) & (column < across), 1.0, 0.0).astype(f32)


def pool_matrix(frames, rows, width, up):
    cells, pooled = frames * rows * width, frames * rows * width // 8
    shape = (cells, pooled) if up else (pooled, cells)
    place = lax.broadcasted_iota(i32, shape, 0 if up else 1)
    target = lax.broadcasted_iota(i32, shape, 1 if up else 0)
    column = lax.rem(place, width) // 2
    row = lax.rem(lax.div(place, width), rows) // 2
    frame = lax.div(place, width * rows) // 2
    home = (frame * (rows // 2) + row) * (width // 2) + column
    return jnp.where(home == target, 0.125, 0.0).astype(bf16)


def moments(totals, inverse):
    mean = totals[0:1] * inverse
    variance = totals[1:2] * inverse - mean * mean
    return mean, lax.rsqrt(variance + epsilon)


def column_shift(x, width, by):
    cells = x.shape[0]
    column = lax.rem(lax.broadcasted_iota(i32, (cells, 1), 0), width)
    edge = 0 if by == 1 else width - 1
    return jnp.where(column == edge, 0.0, pltpu.roll(x, by % cells, 0))


def silu(active):
    return active * jax.nn.sigmoid(active)


def slope(active, upstream):
    sig = jax.nn.sigmoid(active)
    return upstream * sig * (1.0 + active * (1.0 - sig))


def sums(a, b):
    return jnp.concatenate(
        [jnp.sum(a, axis=0, keepdims=True), jnp.sum(a * b, axis=0, keepdims=True)], axis=0
    )


def box_mean(x, frames, rows, width):
    cells, channels = x.shape
    x = x + column_shift(x, width, 1) + column_shift(x, width, -1)
    x = x.reshape(frames, rows, width, channels)
    edge = jnp.zeros((frames, 1, width, channels), f32)
    x = (
        x
        + jnp.concatenate([edge, x[:, : rows - 1]], axis=1)
        + jnp.concatenate([x[:, 1:], edge], axis=1)
    )
    edge = jnp.zeros((1, rows, width, channels), f32)
    x = (
        x
        + jnp.concatenate([edge, x[: frames - 1]], axis=0)
        + jnp.concatenate([x[1:], edge], axis=0)
    )
    return x.reshape(cells, channels) * (1.0 / 27.0)


def place_bands(dst, blocks, slots, frames, rows, width):
    for turn, block in enumerate(blocks):
        part = block[...].astype(dst.dtype).reshape(frames, rows, width, dst.shape[-1])
        dst[:, pl.ds(slots[turn] * rows, rows)] = part


def fill_beside(beside, stems, frames, rows, width):
    beside[...] = jnp.zeros_like(beside)
    three = jnp.concatenate(
        [column_shift(stems, width, 1), stems, column_shift(stems, width, -1)], axis=1
    )
    three = three.astype(beside.dtype).reshape(frames, rows, width, 3 * STEMS)
    beside[1 : frames + 1, 1 : rows + 1, :, : 3 * STEMS] = three


def fill_conv_weights(flat, wide, thin):
    flat[...] = jnp.zeros_like(flat)
    for tap in range(27):
        row = (tap // 3) * BESIDE + (tap % 3) * STEMS
        flat[row : row + B1R, B2:] = wide[tap]
        flat[row + B1R : row + STEMS, :B2] = thin[tap]


def fill_back_weights(flat, wide, thin):
    flat[...] = jnp.zeros_like(flat)
    for tap in range(27):
        start = tap * 512
        flat[:B1R, start + B2 : start + SECOND] = wide[26 - tap]
        flat[B1R:, start : start + B2] = thin[26 - tap]


def fill_shifted(shifted, grad, frames, rows, width):
    shifted[...] = jnp.zeros_like(shifted)
    for dc in range(3):
        moved = grad if dc == 1 else column_shift(grad, width, 1 - dc)
        moved = moved.astype(shifted.dtype).reshape(frames, rows, width, SECOND)
        shifted[dc, 1 : frames + 1, 1 : rows + 1, :, :SECOND] = moved


def window(padded, f, r, frames, rows):
    part = padded[f : f + frames, r : r + rows]
    return part.reshape(frames * rows * part.shape[2], part.shape[3]).astype(bf16)


def conv_chunk(beside, flat, start, step, rows):
    taps = [window(beside, start + f, r, step, rows) for f in range(3) for r in range(3)]
    return dot(jnp.concatenate(taps, axis=1), flat[...])


def back_chunk(shifted, flat, start, step, rows):
    taps = [
        window(shifted.at[dc], start + f, r, step, rows)
        for f in range(3)
        for r in range(3)
        for dc in range(3)
    ]
    return dot_nt(jnp.concatenate(taps, axis=1), flat[...])


def pack_conv(slab, beside, dz, frames, rows, width, scale):
    cells = frames * rows * width
    wide_dz, thin_dz = dz[:, B2:], dz[:, :B2]
    half = 27 * B1R // 2
    for f in range(3):
        for r in range(3):
            part = window(beside, f, r, frames, rows)
            wide = dot_tn(part, wide_dz) * scale
            thin = dot_tn(part, thin_dz) * scale
            for c in range(3):
                tap = (f * 3 + r) * 3 + c
                rows_wide = wide[c * STEMS : c * STEMS + B1R].astype(bf16)
                slab[tap * B1R : (tap + 1) * B1R] = rows_wide[:, :128]
                at = 27 * B1R + tap * B1R
                slab[at : at + B1R] = rows_wide[:, 128:256]
                for piece in range(2):
                    row = tap * B1R + piece * 80
                    side = row >= half
                    at = 2 * 27 * B1R + row - (half if side else 0)
                    lanes = slice(64, 128) if side else slice(0, 64)
                    slab[at : at + 80, lanes] = rows_wide[piece * 80 : piece * 80 + 80, 256:]
                at = 2 * 27 * B1R + half + tap * B2R
                slab[at : at + B2R] = thin[c * STEMS + B1R : (c + 1) * STEMS].astype(bf16)


CONV_ROWS = 2 * 27 * B1R + 27 * B1R // 2 + 27 * B2R


def halved(n):
    return -(-n // (2 * GRANULE)) * GRANULE


def pack_matrix(slab, at, matrix):
    n, lanes = matrix.shape
    blocks, half = lanes // 128, halved(n)
    matrix = matrix.astype(bf16)
    for j in range(blocks):
        slab[at + j * n : at + (j + 1) * n] = matrix[:, j * 128 : (j + 1) * 128]
    at = at + blocks * n
    left, right = matrix[:half, blocks * 128 :], matrix[half:, blocks * 128 :]
    if n < 2 * half:
        right = jnp.concatenate([right, jnp.zeros((2 * half - n, 64), bf16)], axis=0)
    slab[at : at + half] = jnp.concatenate([left, right], axis=1)
    return at + half


def pack_norms(slab, at, gain, bias):
    rows = [row[:, j * 128 : (j + 1) * 128] for row in (gain, bias) for j in range(8)]
    slab[at : at + 16] = jnp.concatenate(rows, axis=0).astype(bf16)


def give_halves(slab, seg, mine, other):
    half = mine.shape[0]
    mine[...] = slab[pl.ds(seg * half, half)]
    other[...] = slab[pl.ds((1 - seg) * half, half)]


def unpack_conv(slab, wide_out, thin_out):
    half = 27 * B1R // 2
    for tap in range(27):
        at = tap * B1R
        wide_out[tap, :, :128] = slab[at : at + B1R].astype(f32)
        wide_out[tap, :, 128:256] = slab[27 * B1R + at : 27 * B1R + at + B1R].astype(f32)
        for piece in range(2):
            row = at + piece * 80
            side = row >= half
            start = 2 * 27 * B1R + row - (half if side else 0)
            part = slab[start : start + 80].astype(f32)
            part = part[:, 64:] if side else part[:, :64]
            wide_out[tap, piece * 80 : piece * 80 + 80, 256:] = part
        at = 2 * 27 * B1R + half + tap * B2R
        thin_out[tap] = slab[at : at + B2R].astype(f32)


def unpack_matrix(slab, at, n, lanes):
    blocks, half = lanes // 128, halved(n)
    parts = [slab[at + j * n : at + (j + 1) * n].astype(f32) for j in range(blocks)]
    at = at + blocks * n
    tail = slab[at : at + half].astype(f32)
    parts.append(jnp.concatenate([tail[:, :64], tail[: n - half, 64:]], axis=0))
    return parts, at + half


def matrix_rows(n, lanes):
    return lanes // 128 * n + halved(n)


def padded_rows(rows):
    unit = GRANULE * lax.axis_size("segment") * lax.axis_size("dp") * lax.axis_size("space")
    return -(-rows // unit) * unit


def split_sum(parts, pieces, row, at):
    rows = parts[0].shape[0] // pieces

    def body(row_ref, *refs):
        ins, outs = refs[: len(parts)], refs[len(parts) :]
        for k, out in enumerate(outs):
            start = (row_ref[at] ^ k) * rows if pieces > 1 else 0
            if pieces > 1:
                start = pl.multiple_of(start, GRANULE)
            total = ins[0][pl.ds(start, rows)].astype(f32)
            for ref in ins[1:]:
                total = total + ref[pl.ds(start, rows)].astype(f32)
            out[...] = total.astype(bf16)

    outs = [((rows, 128), bf16)] * pieces
    return call(body, outs, parts, [row], us=1.0, limit=32)


def joined(parts, row, at):
    rows, pieces = parts[0].shape[0], len(parts)

    def body(row_ref, *refs):
        for k, ref in enumerate(refs[:-1]):
            start = (row_ref[at] ^ k) * rows
            refs[-1][pl.ds(pl.multiple_of(start, GRANULE), rows)] = ref[...]

    outs = [((rows * pieces, 128), bf16)]
    return call(body, outs, parts, [row], us=1.0, limit=32)[0]


def swapped(x):
    return lax.ppermute(x, "segment", [(0, 1), (1, 0)])


class Slab:
    def __init__(self, mine, other, row):
        self.row, self.parts = row, [mine, swapped(other)]

    def to_dp(self):
        self.parts = exchanged(split_sum(self.parts, lax.axis_size("dp"), self.row, DP), "dp")

    def to_dp_again(self):
        pass

    def to_space(self):
        bands = lax.axis_size("space")
        self.parts = exchanged(split_sum(self.parts, bands, self.row, BAND), "space")

    def summed(self):
        self.parts = copies(split_sum(self.parts, 1, self.row, BAND)[0], "space")

    def back_dp(self):
        held = copies(joined(self.parts, self.row, BAND), "dp")
        self.parts = held + [swapped(part) for part in held]

    def back_dp_again(self):
        pass

    def place(self, slab, pieces, row_ref):
        rows, peers = pieces[0].shape[0], len(pieces) // 2
        for k, piece in enumerate(pieces):
            side = row_ref[SEG] if k < peers else 1 - row_ref[SEG]
            at = (side * peers + (row_ref[DP] ^ (k % peers))) * rows
            slab[pl.ds(pl.multiple_of(at, GRANULE), rows)] = piece[...]


class CrossSlab(Slab):
    def to_dp(self):
        mine, got = self.parts
        self.quarter = mine.shape[0] // 4
        half, quarter = self.quarter // 2, self.quarter

        def body(row_ref, mine_ref, got_ref, to_x, to_y, keep_a, keep_b):
            y, x = lax.div(row_ref[DP], 2), lax.rem(row_ref[DP], 2)
            for k in range(2):
                to = slice(k * half, (k + 1) * half)
                for out, start in (
                    (to_x, (k * 2 + (1 - x)) * quarter),
                    (keep_a, (k * 2 + x) * quarter),
                    (to_y, ((1 - y) * 2 + k) * quarter + half),
                    (keep_b, (y * 2 + k) * quarter + half),
                ):
                    at = pl.ds(pl.multiple_of(start, GRANULE), half)
                    total = mine_ref[at].astype(f32) + got_ref[at].astype(f32)
                    out[to] = total.astype(out.dtype)

        send, keep = ((2 * half, 128), bf16), ((2 * half, 128), f32)
        to_x, to_y, *self.kept = call(
            body, [send, send, keep, keep], [mine, got], [self.row], us=1.3, limit=32
        )
        self.got = [lax.ppermute(to_x, "dp", pairing(4, 1)), lax.ppermute(to_y, "dp", pairing(4, 2))]

    def to_dp_again(self):
        half = self.quarter // 2

        def body(row_ref, keep_a, keep_b, got_a, got_b, send_a, send_b, next_a, next_b):
            y, x = lax.div(row_ref[DP], 2), lax.rem(row_ref[DP], 2)
            for keep, got, send, own, place in (
                (keep_a, got_a, send_a, next_a, y),
                (keep_b, got_b, send_b, next_b, x),
            ):
                at = pl.ds(pl.multiple_of(place * half, GRANULE), half)
                own[...] = keep[at] + got[at].astype(f32)
                at = pl.ds(pl.multiple_of((1 - place) * half, GRANULE), half)
                send[...] = (keep[at] + got[at].astype(f32)).astype(bf16)

        send, keep = ((half, 128), bf16), ((half, 128), f32)
        to_y, to_x, *self.kept = call(
            body, [send, send, keep, keep], self.kept + self.got, [self.row], us=1.0, limit=32
        )
        self.got = [lax.ppermute(to_y, "dp", pairing(4, 2)), lax.ppermute(to_x, "dp", pairing(4, 1))]

    def to_space(self):
        half, bands = self.quarter // 2, lax.axis_size("space")
        rows = self.quarter // bands

        def body(row_ref, keep_a, keep_b, got_a, got_b, own, *refs):
            outs, whole = refs[:-1], refs[-1]
            whole[:half] = keep_a[...] + got_a[...].astype(f32)
            whole[half:] = keep_b[...] + got_b[...].astype(f32)
            for k, out in enumerate((own,) + outs):
                at = pl.ds(pl.multiple_of((row_ref[BAND] ^ k) * rows, GRANULE), rows)
                out[...] = whole[at].astype(out.dtype)

        outs = [((rows, 128), f32)] + [((rows, 128), bf16)] * (bands - 1)
        scratch = [((self.quarter, 128), f32)]
        parts = call(body, outs, self.kept + self.got, [self.row], scratch, us=1.0, limit=32)
        self.parts = exchanged(parts, "space")

    def back_dp(self):
        half, bands = self.quarter // 2, lax.axis_size("space")
        rows = self.quarter // bands

        def body(row_ref, *refs):
            parts, (out_a, out_b, whole) = refs[:bands], refs[bands:]
            for k, ref in enumerate(parts):
                at = pl.ds(pl.multiple_of((row_ref[BAND] ^ k) * rows, GRANULE), rows)
                whole[at] = ref[...]
            out_a[...] = whole[:half]
            out_b[...] = whole[half:]

        outs, scratch = [((half, 128), bf16)] * 2, [((self.quarter, 128), bf16)]
        a, b = call(body, outs, self.parts, [self.row], scratch, us=1.0, limit=32)
        self.got = [lax.ppermute(a, "dp", pairing(4, 2)), lax.ppermute(b, "dp", pairing(4, 1))]
        self.kept = [a, b]

    def back_dp_again(self):
        half = self.quarter // 2

        def body(row_ref, own_a, own_b, got_a, got_b, pair_a, pair_b, both):
            y, x = lax.div(row_ref[DP], 2), lax.rem(row_ref[DP], 2)
            for own, got, out, place in ((own_a, got_a, pair_a, y), (own_b, got_b, pair_b, x)):
                out[pl.ds(pl.multiple_of(place * half, GRANULE), half)] = own[...]
                out[pl.ds(pl.multiple_of((1 - place) * half, GRANULE), half)] = got[...]
            both[: 2 * half] = pair_a[...]
            both[2 * half :] = pair_b[...]

        outs = [((2 * half, 128), bf16)] * 2 + [((4 * half, 128), bf16)]
        a, b, both = call(body, outs, self.kept + self.got, [self.row], us=1.0, limit=32)
        got = [lax.ppermute(a, "dp", pairing(4, 1)), lax.ppermute(b, "dp", pairing(4, 2))]
        self.parts = [both] + got + [swapped(part) for part in [both] + got]

    def place(self, slab, pieces, row_ref):
        half, quarter = self.quarter // 2, self.quarter
        y, x = lax.div(row_ref[DP], 2), lax.rem(row_ref[DP], 2)
        for turn, side in enumerate((row_ref[SEG], 1 - row_ref[SEG])):
            both, far_a, far_b = pieces[3 * turn : 3 * turn + 3]
            a, b = both.at[: 2 * half], both.at[2 * half :]
            for k in range(2):
                part = slice(k * half, (k + 1) * half)
                for ref, start in (
                    (a, (k * 2 + x) * quarter),
                    (far_a, (k * 2 + (1 - x)) * quarter),
                    (b, (y * 2 + k) * quarter + half),
                    (far_b, ((1 - y) * 2 + k) * quarter + half),
                ):
                    at = pl.multiple_of(side * 4 * quarter + start, GRANULE)
                    slab[pl.ds(at, half)] = ref[part]


def widened(x):
    more = PADDED - x.shape[1]
    return jnp.concatenate([x, jnp.zeros((2, more), f32)], axis=1) if more else x


def pack_lanes(out, at, x):
    cells, channels = x.shape
    for start in range(0, channels, 128):
        part = x[:, start : start + 128]
        if part.shape[1] < 128:
            part = jnp.concatenate([part, jnp.zeros((cells, 128 - part.shape[1]), f32)], axis=1)
        out[at : at + cells] = part.astype(bf16)
        at += cells
    return at


def unpacked_lanes(ref, at, cells, channels):
    parts = []
    for start in range(0, channels, 128):
        parts.append(ref[at : at + cells, : min(128, channels - start)].astype(f32))
        at += cells
    return jnp.concatenate(parts, axis=1)


def shards(
    inputs,
    crop_group,
    in_proj_4f,
    conv_a_4f,
    conv_b_4f,
    gain_4f,
    bias_4f,
    in_proj_5b,
    conv_a_5b,
    conv_b_5b,
    gain_5b,
    bias_5b,
    out_grad,
):
    order.last = []
    segs, dps, bands = (lax.axis_size(axis) for axis in ("segment", "dp", "space"))
    micro, clips, frames, rows, width, channels = inputs.shape
    full_rows, all_clips = rows * bands, clips * dps
    halves = micro // segs
    held = halves * clips
    items = micro * clips
    spread = segs if items == segs * bands else 1
    assert segs == 2 and items == spread * bands and clips % spread == 0
    each = clips // spread
    cells, part_cells = frames * full_rows * width, frames * rows * width
    frames5, rows5, width5 = frames // 2, full_rows // 2, width // 2
    cells5, part_cells5 = cells // 8, part_cells // 8
    band_rows5 = rows // 2

    inward, pooled_in, outward = [], [], []
    for s in range(segs):
        for z in range(bands):
            for item in range(bands):
                inward.append((s * bands + z, s * bands + item, item, z))
    for m in range(micro):
        for c in range(clips):
            if spread > 1:
                holders = [(c // each) * bands + m * each + c % each]
            else:
                holders = [s * bands + m * clips + c for s in range(segs)]
            home, local = m // halves, (m % halves) * clips + c
            for z in range(bands):
                for holder in holders:
                    pooled_in.append((home * bands + z, holder, local, z))
                outward.append((holders[z % len(holders)], home * bands + z, z, local))
    inward, pooled_in, outward = (
        Route(edges, segs * bands) for edges in (inward, pooled_in, outward)
    )
    IN_BLOCK = TABLES
    IN_SLOT = IN_BLOCK + len(inward.rounds)
    POOLED_BLOCK = IN_SLOT + len(inward.rounds)
    POOLED_SLOT = POOLED_BLOCK + len(pooled_in.rounds)
    OUT_BLOCK = POOLED_SLOT + len(pooled_in.rounds)
    OUT_SLOT = OUT_BLOCK + len(outward.rounds)
    table = []
    for s in range(segs):
        for d in range(dps):
            for z in range(bands):
                me = s * bands + z
                first = s * each if spread > 1 else 0
                counted = 1 if spread > 1 or s == 0 else 0
                line = [s, d, z, first, z // each, counted]
                for route in (inward, pooled_in, outward):
                    line = line + route.blocks[me] + route.slots[me]
                table.append(line)
    row = jnp.array(table, i32)[lax.axis_index(("segment", "dp", "space"))]
    numbers = [row, crop_group]

    def group_parts(x):
        if each > 1:
            pairs = [[z * each + k for k in range(each)] for z in range(micro)]
            x = lax.psum(x, "space", axis_index_groups=pairs)
        if spread > 1:
            x = x + swapped(x)
        if dps > 4:
            return [lax.psum(x, "dp")]
        return copies(x, "dp")

    def total_of(refs):
        return functools.reduce(jnp.add, [ref[...] for ref in refs])

    def crop(row_ref, group_ref, scale=1, m=None):
        group = group_ref[row_ref[MY_MICRO] if m is None else m]
        tall, wide = full_rows // scale, width // scale
        height, across = tall - group * (tall // 4), wide - group * (wide // 4)
        count = all_clips * (frames // scale) * height * across
        return height, across, 1.0 / jnp.full((1, 1), count, i32).astype(f32)

    LEAD, OUTER, STEM = slice(0, B0), slice(0, C_MID), slice(C_MID, None)
    RESTS = slice(B0, C_MID)
    wide4, thin4 = conv_a_4f.reshape(27, B1R, B1), conv_b_4f.reshape(27, B2R, B2)
    wide5, thin5 = conv_a_5b.reshape(27, B1R, B1), conv_b_5b.reshape(27, B2R, B2)

    def project_body(row_ref, group_ref, x_ref, p_ref, stat, pool, *outs):
        for k in range(bands):
            item = row_ref[IN_BLOCK + k]
            m, c = lax.div(item, each), row_ref[FIRST_CLIP] + lax.rem(item, each)
            x = x_ref[m, c].reshape(part_cells, channels)
            height, across, _ = crop(row_ref, group_ref, 1, m)
            mask = mask_of(part_cells, rows, width, height, across, row_ref[BAND] * rows)
            z = dot(x, p_ref[:, B0:]) * mask
            stem = z[:, :STEMS]
            outs[k][...] = stem.astype(bf16)
            pool[k] = z[:, STEMS:].astype(bf16)
            stat[item] = sums(stem, stem)

    got = call(
        project_body,
        [((bands, 2, STEMS), f32), ((bands, part_cells, BP), bf16)]
        + [((part_cells, STEMS), bf16)] * bands,
        [inputs, in_proj_4f],
        numbers,
        us=1.5,
    )
    stem_stat, pool_parts, stem_parts = got[0], got[1], got[2:]
    stem_blocks = inward.send(stem_parts)

    def home_crop(row_ref, group_ref, i):
        m = row_ref[SEG] * halves + i // clips
        height, across, inverse = crop(row_ref, group_ref, 1, m)
        first = row_ref[BAND] * rows
        return m, mask_of(part_cells, rows, width, height, across, first), inverse

    lanes5 = -(-C_MID // 128)
    carried = part_cells + lanes5 * part_cells5

    def lead_body(row_ref, group_ref, x_ref, p_ref, stem_stat, pool, upper, *refs):
        lead_out, stem_out, stat, outs = refs[0], refs[1], refs[2], refs[3:]
        for i in range(held):
            m, mask, _ = home_crop(row_ref, group_ref, i)
            x = x_ref[m, i % clips].reshape(part_cells, channels)
            z = dot(x, p_ref[:, :STEM_END]) * mask
            lead = z[:, :B0]
            lead_out[i] = lead
            stem_out[i] = z[:, B0:]
            total = sums(lead, lead)
            j = bands + i // clips
            stat[j] = total if i % clips == 0 else stat[j] + total
        for k in range(bands):
            stat[k] = widened(stem_stat[k])
            item = row_ref[IN_BLOCK + k]
            m, c = lax.div(item, each), row_ref[FIRST_CLIP] + lax.rem(item, each)
            outs[k][:part_cells] = pool[k]
            pack_lanes(outs[k], part_cells, upper[m, c].astype(f32).reshape(part_cells5, C_MID))

    got = call(
        lead_body,
        [
            ((held, part_cells, B0), f32),
            ((held, part_cells, STEMS), f32),
            ((bands + halves, 2, PADDED), f32),
        ]
        + [((carried, 128), bf16)] * bands,
        [inputs, in_proj_4f, stem_stat, pool_parts, out_grad],
        numbers,
        us=2.5,
    )
    lead, home_stem, stat = got[:3]

    def all_parts(x, axis):
        return [lax.psum(x, axis)] if lax.axis_size(axis) > 4 else copies(x, axis)

    def whole_body(*refs):
        refs[-1][...] = total_of(refs[:-1])

    def summed_dp(x):
        parts = all_parts(x, "dp")
        return call(whole_body, [(x.shape, f32)], parts, us=0.8)[0]

    def share_body(row_ref, own, other, *outs):
        for k, out in enumerate(outs):
            item = row_ref[BAND] ^ k
            first = lax.div(item, each) * each
            total = jnp.zeros((2, PADDED), f32)
            for c in range(each):
                total = total + own[first + c]
                if spread > 1:
                    total = total + other[first + c]
            out[0] = total
            for j in range(halves):
                out[1 + j] = own[bands + j]

    stat = summed_dp(stat)
    stat_parts = call(
        share_body,
        [((1 + halves, 2, PADDED), f32)] * bands,
        [stat, swapped(stat)],
        [row],
        us=0.8,
    )
    stat_parts = exchanged(stat_parts, "space")
    carried_blocks = inward.send(got[3:])

    def arrange_body(gain4, bias4, gain5, bias5, p4, p5, affine4, affine5, proj4, proj5):
        for gain, bias, out in ((gain4, bias4, affine4), (gain5, bias5, affine5)):
            for k, ref in enumerate((gain, bias)):
                v = ref[...]
                out[k : k + 1] = jnp.concatenate(
                    [
                        v[:, :B0],
                        v[:, STEM_END:FIRST],
                        v[:, FIRST + B1 :],
                        v[:, FIRST : FIRST + B1],
                        v[:, B0:STEM_END],
                    ],
                    axis=1,
                )
        proj4[:, :B0] = p4[:, :B0]
        proj4[:, B0:] = jnp.concatenate([p4[:, STEM_END:], p4[:, B0:STEM_END]], axis=1)
        for first, last, to in ((0, B0, 0), (STEM_END, FIRST, B0), (B0, STEM_END, B0 + BP)):
            rows_in = p5[first:last]
            proj5[to : to + last - first, :B0] = rows_in[:, :B0]
            proj5[to : to + last - first, B0:] = jnp.concatenate(
                [
                    rows_in[:, B0 + SECOND :],
                    rows_in[:, B0 + B1 : B0 + SECOND],
                    rows_in[:, B0 : B0 + B1],
                ],
                axis=1,
            )

    affine4, affine5, proj4, proj5 = call(
        arrange_body,
        [((2, 1024), f32)] * 2 + [((channels, FIRST), bf16), ((FIRST, C_MID), bf16)],
        [v.reshape(1, -1) for v in (gain_4f, bias_4f, gain_5b, bias_5b)]
        + [in_proj_4f, in_proj_5b.T],
        us=2.0,
    )

    def lead_act(i, lead_ref, stat_ref, affine_ref, inverse):
        mean, scale = moments(stat_ref[i // clips], inverse)
        norm = (lead_ref[i] - mean) * scale
        return norm, scale, norm * affine_ref[0:1, LEAD] + affine_ref[1:2, LEAD]

    def lead_out_body(row_ref, group_ref, lead_ref, affine_ref, *refs):
        parts, stat_ref, outs, kept = refs[:bands], refs[bands], refs[bands + 1 : -1], refs[-1]
        stat_ref[...] = total_of(parts)[1:]
        matrix = pool_matrix(frames, rows, width, False)
        for i in range(held):
            _, mask, inverse = home_crop(row_ref, group_ref, i)
            _, _, active = lead_act(i, lead_ref, stat_ref, affine_ref, inverse)
            kept[i] = dot(matrix, (silu(active) * mask).astype(bf16)).astype(bf16)
        for turn, out in enumerate(outs):
            out[...] = kept[row_ref[POOLED_BLOCK + turn]]

    got = call(
        lead_out_body,
        [((halves, 2, B0), f32)] + [((part_cells5, B0), bf16)] * len(pooled_in.rounds),
        [lead, affine4] + stat_parts,
        numbers,
        [((held, part_cells5, B0), bf16)],
        us=1.8,
    )
    lead_stat = got[0]
    lead_pooled = pooled_in.send(got[1:])

    step = 2 if full_rows * width <= 128 else 1

    def conv_body(row_ref, group_ref, affine_ref, wide_ref, thin_ref, *refs):
        stats, blocks = refs[:bands], refs[bands : 2 * bands]
        second_out, sums_out, norm_out, stat_out, beside, stage, flat = refs[2 * bands :]
        height, across, inverse = crop(row_ref, group_ref)
        totals = functools.reduce(jnp.add, [ref[0] for ref in stats])[:, :STEMS]
        mean, scale = moments(totals, inverse)
        stat_out[...] = totals
        fill_conv_weights(flat, wide_ref, thin_ref)
        slots = [row_ref[IN_SLOT + k] for k in range(bands)]
        place_bands(stage, blocks, slots, frames, rows, width)
        mask = mask_of(cells, full_rows, width, height, across)
        norm = (stage[...].reshape(cells, STEMS) - mean) * scale
        norm_out[...] = norm
        active = norm * affine_ref[0:1, STEM] + affine_ref[1:2, STEM]
        fill_beside(beside, silu(active) * mask, frames, full_rows, width)
        chunk = step * full_rows * width
        total = jnp.zeros((2, SECOND), f32)
        for start in range(0, frames, step):
            got = conv_chunk(beside, flat, start, step, full_rows)
            second_out[start * full_rows * width : start * full_rows * width + chunk] = got
            total = total + sums(got * mask[:chunk], got)
        sums_out[...] = total

    second, second_sums, stem_norm, stem_total, beside = call(
        conv_body,
        [
            ((cells, SECOND), f32),
            ((2, SECOND), f32),
            ((cells, STEMS), f32),
            ((2, STEMS), f32),
            ((frames + 2, full_rows + 2, width, BESIDE), bf16),
        ],
        [affine4, wide4, thin4] + stat_parts + stem_blocks,
        numbers,
        [
            ((frames, full_rows, width, STEMS), f32),
            ((9 * BESIDE, SECOND), bf16),
        ],
        us=9.0,
    )

    def pool_body(row_ref, group_ref, second_sums, *refs):
        blocks, (zp_out, sums_out, stage) = refs[:bands], refs[bands:]
        height, across, _ = crop(row_ref, group_ref)
        slots = [row_ref[IN_SLOT + k] for k in range(bands)]
        place_bands(stage, [ref.at[:part_cells] for ref in blocks], slots, frames, rows, width)
        zp = box_mean(stage[...].reshape(cells, BP), frames, full_rows, width)
        zp_out[...] = zp
        mask = mask_of(cells, full_rows, width, height, across)
        sums_out[...] = jnp.concatenate([sums(zp * mask, zp), second_sums[...]], axis=1)

    zp, rest_sums = call(
        pool_body,
        [((cells, BP), f32), ((2, REST), f32)],
        [second_sums] + carried_blocks,
        numbers,
        [((frames, full_rows, width, BP), f32)],
        us=1.3,
    )
    rest_parts = group_parts(rest_sums)
    n_parts = len(rest_parts)

    span = 2 * full_rows * width

    def rest_of(zp_ref, second_ref, start, affine_ref, mean, scale):
        z = jnp.concatenate(
            [zp_ref[start : start + span], second_ref[start : start + span]], axis=1
        )
        norm = (z - mean) * scale
        return norm, norm * affine_ref[0:1, RESTS] + affine_ref[1:2, RESTS]

    def middle_body(row_ref, group_ref, affine_ref, p_ref, zp_ref, second_ref, *refs):
        parts, leads = refs[:n_parts], refs[n_parts:-6]
        stat_out, pooled, first_out, sums_out, stage, kept = refs[-6:]
        height, across, inverse = crop(row_ref, group_ref)
        mean, scale = moments(total_of(parts), inverse)
        stat_out[...] = jnp.concatenate([mean, scale], axis=0)
        mask = mask_of(span, full_rows, width, height, across)
        matrix = pool_matrix(2, full_rows, width, False)
        slots = [row_ref[POOLED_SLOT + k] for k in range(len(leads))]
        place_bands(stage, leads, slots, frames5, band_rows5, width5)
        pooled[:, :B0] = stage[...].reshape(cells5, B0).astype(bf16)
        for f in range(frames5):
            _, active = rest_of(zp_ref, second_ref, f * span, affine_ref, mean, scale)
            out = dot(matrix, (silu(active) * mask).astype(bf16))
            pooled[f * span // 8 : (f + 1) * span // 8, B0:] = out.astype(bf16)
        z = dot_nt(pooled[...], p_ref[...])
        kept[...] = z
        project = z[:, LEAD.stop : LEAD.stop + BP].astype(bf16).astype(f32)
        kept[:, B0 : B0 + BP] = box_mean(project, frames5, rows5, width5)
        z = kept[...]
        first_out[...] = z
        height, across, _ = crop(row_ref, group_ref, 2)
        sums_out[...] = sums(z * mask_of(cells5, rows5, width5, height, across), z)

    rest_stat, pooled, first5, first5_sums = call(
        middle_body,
        [((2, REST), f32), ((cells5, C_MID), bf16), ((cells5, FIRST), f32), ((2, FIRST), f32)],
        [affine4, proj5, zp, second] + rest_parts + lead_pooled,
        numbers,
        [((frames5, rows5, width5, B0), f32), ((cells5, FIRST), f32)],
    )
    first5_parts = group_parts(first5_sums)

    def conv5_body(row_ref, group_ref, affine_ref, wide_ref, thin_ref, first_ref, *refs):
        parts = refs[:n_parts]
        second_out, sums_out, stat_out, beside, flat = refs[n_parts:]
        height, across, inverse = crop(row_ref, group_ref, 2)
        mean, scale = moments(total_of(parts), inverse)
        stat_out[...] = jnp.concatenate([mean, scale], axis=0)
        fill_conv_weights(flat, wide_ref, thin_ref)
        mask = mask_of(cells5, rows5, width5, height, across)
        stem = slice(B0 + BP, FIRST)
        norm = (first_ref[:, stem] - mean[:, stem]) * scale[:, stem]
        active = norm * affine_ref[0:1, STEM] + affine_ref[1:2, STEM]
        fill_beside(beside, silu(active) * mask, frames5, rows5, width5)
        got = conv_chunk(beside, flat, 0, frames5, rows5)
        second_out[...] = got
        sums_out[...] = sums(got * mask, got)

    second5, second5_sums, first5_stat, beside5 = call(
        conv5_body,
        [
            ((cells5, SECOND), f32),
            ((2, SECOND), f32),
            ((2, FIRST), f32),
            ((frames5 + 2, rows5 + 2, width5, BESIDE), f32),
        ],
        [affine5, wide5, thin5, first5] + first5_parts,
        numbers,
        [((9 * BESIDE, SECOND), bf16)],
    )
    second5_parts = group_parts(second5_sums)

    def out5_body(row_ref, group_ref, affine_ref, first_ref, stat_ref, second_ref, *refs):
        parts, uppers = refs[:n_parts], refs[n_parts : n_parts + bands]
        out, norm_out, slope_out, scale_out, sums_out, stage = refs[n_parts + bands :]
        height, across, inverse = crop(row_ref, group_ref, 2)
        mean2, scale2 = moments(total_of(parts), inverse)
        mask = mask_of(cells5, rows5, width5, height, across)
        outer = slice(0, B0 + BP)
        mean = jnp.concatenate([stat_ref[0:1, outer], mean2], axis=1)
        scale = jnp.concatenate([stat_ref[1:2, outer], scale2], axis=1)
        z = jnp.concatenate([first_ref[:, outer], second_ref[...]], axis=1)
        norm = (z - mean) * scale
        active = norm * affine_ref[0:1, OUTER] + affine_ref[1:2, OUTER]
        act = silu(active) * mask
        natural = [act[:, :B0], act[:, B0 + BP + B2 :], act[:, B0 + BP : B0 + BP + B2]]
        natural = jnp.concatenate(natural + [act[:, B0 : B0 + BP]], axis=1)
        out[...] = natural.reshape(frames5, rows5, width5, C_MID)
        for k, ref in enumerate(uppers):
            part = unpacked_lanes(ref, part_cells, part_cells5, C_MID)
            part = part.reshape(frames5, band_rows5, width5, C_MID)
            stage[:, pl.ds(row_ref[IN_SLOT + k] * band_rows5, band_rows5)] = part
        upper = stage[...].reshape(cells5, C_MID)
        upper = jnp.concatenate(
            [
                upper[:, :B0],
                upper[:, B0 + SECOND :],
                upper[:, B0 + B1 : B0 + SECOND],
                upper[:, B0 : B0 + B1],
            ],
            axis=1,
        )
        slopes = slope(active, upper * mask)
        norm_out[...] = norm
        slope_out[...] = slopes
        scale_out[...] = scale
        sums_out[...] = sums(slopes, norm)

    out5, outer5_norm, outer5_slope, outer5_scale, outer5_sums = call(
        out5_body,
        [
            ((frames5, rows5, width5, C_MID), f32),
            ((cells5, C_MID), f32),
            ((cells5, C_MID), f32),
            ((1, C_MID), f32),
            ((2, C_MID), f32),
        ],
        [affine5, first5, first5_stat, second5] + second5_parts + carried_blocks,
        numbers,
        [((frames5, rows5, width5, C_MID), f32)],
        us=1.4,
    )
    outer5_parts = group_parts(outer5_sums)

    def back5_body(row_ref, group_ref, affine_ref, wide_ref, thin_ref, *refs):
        norm_ref, slope_ref, scale_ref, first_ref, stat_ref = refs[:5]
        parts, refs = refs[5 : 5 + n_parts], refs[5 + n_parts :]
        dz_out, lead_out, project_out, slope_out, sums_out, shifted, flat = refs
        height, across, inverse = crop(row_ref, group_ref, 2)
        mask = mask_of(cells5, rows5, width5, height, across)
        fill_back_weights(flat, wide_ref, thin_ref)
        total = total_of(parts) * inverse
        grad = (mask * (affine_ref[0:1, OUTER] * scale_ref[...])) * (
            slope_ref[...] - total[0:1] - norm_ref[...] * total[1:2]
        )
        lead_out[...] = grad[:, :B0]
        low = grad[:, B0:].astype(bf16)
        dz = low[:, BP:]
        dz_out[...] = dz
        project_out[...] = box_mean(low[:, :BP].astype(f32), frames5, rows5, width5)
        fill_shifted(shifted, dz.astype(f32), frames5, rows5, width5)
        upper = back_chunk(shifted, flat, 0, frames5, rows5)
        stem = slice(B0 + BP, FIRST)
        norm = (first_ref[:, stem] - stat_ref[0:1, stem]) * stat_ref[1:2, stem]
        active = norm * affine_ref[0:1, STEM] + affine_ref[1:2, STEM]
        slopes = slope(active, upper * mask)
        slope_out[...] = slopes
        sums_out[...] = sums(slopes, norm)

    dz5, lead5_grad, project5_grad, stem5_slope, stem5_sums = call(
        back5_body,
        [
            ((cells5, SECOND), bf16),
            ((cells5, B0), f32),
            ((cells5, BP), f32),
            ((cells5, STEMS), f32),
            ((2, STEMS), f32),
        ],
        [affine5, wide5, thin5, outer5_norm, outer5_slope, outer5_scale, first5, first5_stat]
        + outer5_parts,
        numbers,
        [
            ((3, frames5 + 2, rows5 + 2, width5, 512), f32),
            ((STEMS, 27 * 512), bf16),
        ],
    )
    stem5_parts = group_parts(stem5_sums)

    def rest_slope(f, pooled_grad, matrix, mask, zp_ref, second_ref, affine_ref, stat_ref):
        norm, active = rest_of(
            zp_ref, second_ref, f * span, affine_ref, stat_ref[0:1], stat_ref[1:2]
        )
        upper = dot(matrix, pooled_grad[f * span // 8 : (f + 1) * span // 8])
        return norm, slope(active, upper * mask)

    def first5_body(row_ref, group_ref, affine_ref, affine4_ref, p_ref, *refs):
        lead_ref, project_ref, slope_ref, first_ref, stat_ref = refs[:5]
        zp_ref, second_ref, rest_stat = refs[5:8]
        parts, refs = refs[8 : 8 + n_parts], refs[8 + n_parts :]
        lead_out, projected_out, rest_out, sums_out = refs
        height, across, inverse = crop(row_ref, group_ref, 2)
        mask = mask_of(cells5, rows5, width5, height, across)
        total = total_of(parts) * inverse
        stem = slice(B0 + BP, FIRST)
        norm = (first_ref[:, stem] - stat_ref[0:1, stem]) * stat_ref[1:2, stem]
        stem_grad = (mask * (affine_ref[0:1, STEM] * stat_ref[1:2, stem])) * (
            slope_ref[...] - total[0:1] - norm * total[1:2]
        )
        projected = jnp.concatenate([lead_ref[...], project_ref[...], stem_grad], axis=1)
        projected = projected.astype(bf16)
        projected_out[...] = projected
        pooled_grad = dot(projected, p_ref[...]).astype(bf16)
        lead_out[...] = pooled_grad[:, :B0].astype(f32).reshape(frames5, rows5, width5, B0)
        rest_grad = pooled_grad[:, B0:]
        rest_out[...] = rest_grad
        height, across, _ = crop(row_ref, group_ref)
        mask = mask_of(span, full_rows, width, height, across)
        matrix = pool_matrix(2, full_rows, width, True)
        total = jnp.zeros((2, REST), f32)
        for f in range(frames5):
            norm, slopes = rest_slope(
                f, rest_grad, matrix, mask, zp_ref, second_ref, affine4_ref, rest_stat
            )
            total = total + sums(slopes, norm)
        sums_out[...] = total

    lead_grad5, projected5_grad, rest_upper, rest_grad_sums = call(
        first5_body,
        [
            ((frames5, rows5, width5, B0), f32),
            ((cells5, FIRST), bf16),
            ((cells5, REST), bf16),
            ((2, REST), f32),
        ],
        [affine5, affine4, proj5, lead5_grad, project5_grad, stem5_slope, first5, first5_stat]
        + [zp, second, rest_stat]
        + stem5_parts,
        numbers,
        us=2.4,
    )
    rest_grad_parts = group_parts(rest_grad_sums)

    def natural(outer, stem):
        pool, thin, wide = (
            outer[:, B0 : B0 + BP],
            outer[:, B0 + BP : B0 + BP + B2],
            outer[:, B0 + BP + B2 :],
        )
        return jnp.concatenate([outer[:, :B0], stem, pool, wide, thin], axis=1)

    rows_5b = padded_rows(CONV_ROWS + matrix_rows(FIRST, C_MID) + 16)

    def weights5_body(row_ref, beside, dz_ref, pooled_ref, projected_ref, *refs):
        outer_ref, stem_ref, mine, other, slab = refs
        scale = jnp.full((1, 1), row_ref[COUNTED], i32).astype(f32)
        pack_conv(slab, beside, dz_ref[...], frames5, rows5, width5, scale)
        at = pack_matrix(slab, CONV_ROWS, dot_tn(projected_ref[...], pooled_ref[...]) * scale)
        norms = natural(outer_ref[...], stem_ref[...]) * scale
        pack_norms(slab, at, norms[1:2], norms[0:1])
        slab[at + 16 :] = jnp.zeros((rows_5b - at - 16, 128), bf16)
        give_halves(slab, row_ref[SEG], mine, other)

    mine5, other5 = call(
        weights5_body,
        [((rows_5b // 2, 128), bf16)] * 2,
        [beside5, dz5, pooled, projected5_grad, outer5_sums, stem5_sums],
        [row],
        [((rows_5b, 128), bf16)],
        us=3.6,
    )
    slab5 = (CrossSlab if dps == 4 else Slab)(mine5, other5, row)

    slab5.to_dp()
    def back4_body(row_ref, group_ref, affine_ref, zp_ref, second_ref, stat_ref, grad_ref, *refs):
        parts, (out5_ref, lead_ref), refs = refs[:n_parts], refs[n_parts : n_parts + 2], refs[n_parts + 2 :]
        outs, (dz_out, kept) = refs[: len(outward.rounds)], refs[len(outward.rounds) :]
        height, across, inverse = crop(row_ref, group_ref)
        mask = mask_of(span, full_rows, width, height, across)
        total = total_of(parts) * inverse
        matrix = pool_matrix(2, full_rows, width, True)
        factor = affine_ref[0:1, RESTS] * stat_ref[1:2]
        for f in range(frames5):
            norm, slopes = rest_slope(
                f, grad_ref, matrix, mask, zp_ref, second_ref, affine_ref, stat_ref
            )
            grad = (mask * factor) * (slopes - total[0:1] - norm * total[1:2])
            low = grad.astype(bf16)
            dz_out[f * span : (f + 1) * span] = low[:, BP:]
            kept[2 * f : 2 * f + 2] = low[:, :BP].astype(f32).reshape(2, full_rows, width, BP)
        pool = box_mean(kept[...].reshape(cells, BP), frames, full_rows, width)
        kept[...] = pool.reshape(frames, full_rows, width, BP)
        for turn, out in enumerate(outs):
            part = kept[:, pl.ds(row_ref[OUT_BLOCK + turn] * rows, rows)]
            out[:part_cells] = part.reshape(part_cells, BP).astype(bf16)
            start = row_ref[OUT_BLOCK + turn] * band_rows5
            part = lead_ref[:, pl.ds(start, band_rows5)].reshape(part_cells5, B0)
            at = pack_lanes(out, part_cells, part)
            part = out5_ref[:, pl.ds(start, band_rows5)].reshape(part_cells5, C_MID)
            pack_lanes(out, at, part)

    carried_out = carried + B0 // 128 * part_cells5
    got = call(
        back4_body,
        [((carried_out, 128), bf16)] * len(outward.rounds) + [((cells, SECOND), bf16)],
        [affine4, zp, second, rest_stat, rest_upper] + rest_grad_parts + [out5, lead_grad5],
        numbers,
        [((frames, full_rows, width, BP), f32)],
        us=2.6,
    )
    carried_grads = outward.send(got[: len(outward.rounds)])
    dz = got[-1]

    rows_conv = padded_rows(CONV_ROWS)

    def weights4_body(row_ref, beside, dz_ref, mine, other, slab):
        scale = jnp.full((1, 1), row_ref[COUNTED], i32).astype(f32)
        pack_conv(slab, beside, dz_ref[...], frames, full_rows, width, scale)
        slab[CONV_ROWS:] = jnp.zeros((rows_conv - CONV_ROWS, 128), bf16)
        give_halves(slab, row_ref[SEG], mine, other)

    mine4, other4 = call(
        weights4_body,
        [((rows_conv // 2, 128), bf16)] * 2,
        [beside, dz],
        [row],
        [((rows_conv, 128), bf16)],
        us=10.5,
    )
    slab4 = (CrossSlab if dps == 4 else Slab)(mine4, other4, row)

    slab5.to_dp_again()
    def stems4_body(row_ref, group_ref, affine_ref, wide_ref, thin_ref, dz_ref, norm_ref, *refs):
        outs, refs = refs[: len(outward.rounds)], refs[len(outward.rounds) :]
        sums_out, shifted, flat, kept = refs
        height, across, _ = crop(row_ref, group_ref)
        fill_back_weights(flat, wide_ref, thin_ref)
        fill_shifted(shifted, dz_ref[...].astype(f32), frames, full_rows, width)
        chunk = step * full_rows * width
        mask = mask_of(chunk, full_rows, width, height, across)
        total = jnp.zeros((2, STEMS), f32)
        for start in range(0, frames, step):
            upper = back_chunk(shifted, flat, start, step, full_rows)
            at = start * full_rows * width
            norm = norm_ref[at : at + chunk]
            active = norm * affine_ref[0:1, STEM] + affine_ref[1:2, STEM]
            slopes = slope(active, upper * mask)
            kept[start : start + step] = slopes.reshape(step, full_rows, width, STEMS)
            total = total + sums(slopes, norm)
        sums_out[...] = total
        for turn, out in enumerate(outs):
            part = kept[:, pl.ds(row_ref[OUT_BLOCK + turn] * rows, rows)]
            out[...] = part.reshape(part_cells, STEMS).astype(bf16)

    got = call(
        stems4_body,
        [((part_cells, STEMS), bf16)] * len(outward.rounds)
        + [((2, STEMS), f32)],
        [affine4, wide4, thin4, dz, stem_norm],
        numbers,
        [
            ((3, frames + 2, full_rows + 2, width, 512), bf16),
            ((STEMS, 27 * 512), bf16),
            ((frames, full_rows, width, STEMS), f32),
        ],
        us=9.0,
    )
    stem_slopes = outward.send(got[: len(outward.rounds)])
    stem_sums = got[-1]

    def lead_slopes(i, row_ref, group_ref, lead_ref, stat_ref, affine_ref, matrix, kept):
        _, mask, inverse = home_crop(row_ref, group_ref, i)
        norm, scale, active = lead_act(i, lead_ref, stat_ref, affine_ref, inverse)
        upper = dot(matrix, kept[i])
        return mask, inverse, scale, norm, slope(active, upper * mask)

    def lead_back_body(row_ref, group_ref, lead_ref, stat_ref, affine_ref, stem_ref, *refs):
        blocks, (sums_out, kept, out) = refs[:held], refs[held:]
        matrix = pool_matrix(frames, rows, width, True)
        for turn, ref in enumerate(blocks):
            place = row_ref[OUT_SLOT + turn]
            at = part_cells + B0 // 128 * part_cells5
            part = unpacked_lanes(ref, part_cells, part_cells5, B0)
            kept[place] = part.astype(bf16)
            part = unpacked_lanes(ref, at, part_cells5, C_MID)
            out[place] = part.reshape(frames5, band_rows5, width5, C_MID).astype(bf16)
        for i in range(held):
            _, _, _, norm, slopes = lead_slopes(
                i, row_ref, group_ref, lead_ref, stat_ref, affine_ref, matrix, kept
            )
            total = sums(slopes, norm)
            j = 1 + i // clips
            sums_out[j] = total if i % clips == 0 else sums_out[j] + total
        sums_out[0] = widened(stem_ref[...])

    last_sums, lead_upper, block_out = call(
        lead_back_body,
        [
            ((1 + halves, 2, PADDED), f32),
            ((held, part_cells5, B0), bf16),
            ((held, frames5, band_rows5, width5, C_MID), bf16),
        ],
        [lead, lead_stat, affine4, stem_sums] + carried_grads,
        numbers,
        us=2.0,
    )
    block_out = block_out.reshape(halves, clips, frames5, band_rows5, width5, C_MID)

    slab4.to_dp()
    last = summed_dp(last_sums)
    if each > 1:
        pairs = [[z * each + k for k in range(each)] for z in range(micro)]
        last = jnp.concatenate(
            [lax.psum(last[:1], "space", axis_index_groups=pairs), last[1:]], axis=0
        )

    def last_body(own, other, stat, out):
        total = own[0]
        if spread > 1:
            total = total + other[0]
        out[0] = total
        out[1 : 1 + halves] = own[1:]
        out[1 + halves] = widened(stat[...])

    (last,) = call(
        last_body,
        [((2 + halves, 2, PADDED), f32)],
        [last, swapped(last), stem_total],
        us=0.8,
    )
    last_parts = copies(last, "space")

    slab5.to_space()
    slab4.to_dp_again()
    rows_proj = padded_rows(matrix_rows(channels, FIRST) + 16)

    def first4_body(row_ref, group_ref, x_ref, affine_ref, lead_ref, stat_ref, *refs):
        upper_ref, stem_ref, last_sums, rest_sums = refs[:4]
        parts, refs = refs[4 : 4 + bands], refs[4 + bands :]
        slopes_in, pools_in, refs = refs[:held], refs[held : 2 * held], refs[2 * held :]
        projected, mine, other, x_all, slab, late, stem_all = refs
        lead_total = functools.reduce(
            jnp.add, [ref[1 : 1 + halves] for ref in parts]
        )
        matrix = pool_matrix(frames, rows, width, True)
        for turn in range(held):
            place = row_ref[OUT_SLOT + turn]
            late[place, :, :BP] = pools_in[turn][:part_cells].astype(f32)
            late[place, :, BP:] = slopes_in[turn][...].astype(f32)
        for k in range(bands):
            stem_all[k, 0] = parts[k][0]
            stem_all[k, 1] = parts[k][1 + halves]
        for i in range(held):
            mask, inverse, scale, norm, slopes = lead_slopes(
                i, row_ref, group_ref, lead_ref, stat_ref, affine_ref, matrix, upper_ref
            )
            total = lead_total[i // clips] * inverse
            lead_grad = (affine_ref[0:1, LEAD] * scale) * (
                slopes - total[0:1] - norm * total[1:2]
            )
            m = row_ref[SEG] * halves + i // clips
            turn = row_ref[BAND] ^ (m * each)
            mean, scale = moments(stem_all[turn, 1][:, :STEMS], inverse)
            total = stem_all[turn, 0][:, :STEMS] * inverse
            norm = (stem_ref[i] - mean) * scale
            stem_grad = (affine_ref[0:1, STEM] * scale) * (
                late[i, :, BP:] - total[0:1] - norm * total[1:2]
            )
            grad = jnp.concatenate([lead_grad, late[i, :, :BP], stem_grad], axis=1) * mask
            at = i * part_cells
            projected[at : at + part_cells] = grad.astype(bf16)
            x_all[at : at + part_cells] = x_ref[m, i % clips].reshape(part_cells, channels)
        at = pack_matrix(slab, 0, dot_tn(x_all[...], projected[...]))
        counted = jnp.full((1, 1), row_ref[COUNTED], i32).astype(f32)
        own = jnp.sum(last_sums[1:], axis=0)
        rest = rest_sums[...] * counted
        stem = last_sums[0][:, :STEMS] * counted
        norms = natural(jnp.concatenate([own, rest], axis=1), stem)
        pack_norms(slab, at, norms[1:2], norms[0:1])
        slab[at + 16 :] = jnp.zeros((rows_proj - at - 16, 128), bf16)
        give_halves(slab, row_ref[SEG], mine, other)

    projected_grad, mine_proj, other_proj = call(
        first4_body,
        [((held * part_cells, FIRST), bf16)] + [((rows_proj // 2, 128), bf16)] * 2,
        [inputs, affine4, lead, lead_stat, lead_upper, home_stem, last_sums, rest_grad_sums]
        + last_parts
        + stem_slopes
        + carried_grads,
        numbers,
        [
            ((held * part_cells, channels), bf16),
            ((rows_proj, 128), bf16),
            ((held, part_cells, BP + STEMS), f32),
            ((bands, 2, 2, PADDED), f32),
        ],
        us=4.0,
    )
    slab_proj = Slab(mine_proj, other_proj, row)

    slab5.summed()
    slab4.to_space()
    slab_proj.to_dp()
    def input_body(projected_ref, p_ref, out):
        for i in range(held):
            at = i * part_cells
            got = dot_nt(projected_ref[at : at + part_cells], p_ref[...])
            out[i // clips, i % clips] = got.reshape(frames, rows, width, channels)

    (input_grad,) = call(
        input_body,
        [((halves, clips, frames, rows, width, channels), f32)],
        [projected_grad, proj4],
    )

    slab5.back_dp()
    slab4.summed()
    slab_proj.to_space()
    slab4.back_dp()
    slab5.back_dp_again()
    slab_proj.summed()
    slab4.back_dp_again()
    slab_proj.back_dp()
    def unpacked(way, n_rows, body, outs, us):
        pieces = way.parts

        def whole(row_ref, *refs):
            slab = refs[-1]
            way.place(slab, refs[: len(pieces)], row_ref)
            body(slab, *refs[len(pieces) : -1])

        scratch = [((n_rows, 128), bf16)]
        return call(whole, outs, pieces, [row], scratch, us=us, limit=48)

    conv_outs = [((27, B1R, B1), f32), ((27, B2R, B2), f32)]

    def unpack_proj(slab, proj_out, norm_out):
        parts, at = unpack_matrix(slab, 0, channels, FIRST)
        proj_out[:, :128] = parts[0]
        proj_out[:, 128:256] = parts[1]
        proj_out[:, 256:] = jnp.concatenate([parts[3], parts[4], parts[2]], axis=1)
        norm_out[...] = slab[at : at + 16].astype(f32)

    def unpack5(slab, wide_out, thin_out, proj5_out, norm5_out):
        unpack_conv(slab, wide_out, thin_out)
        parts, at = unpack_matrix(slab, CONV_ROWS, FIRST, C_MID)
        lead = parts[:2]
        tail = jnp.concatenate([parts[6], parts[3], parts[2]], axis=1)
        for first, last, place in ((0, B0, 0), (B0, B0 + BP, STEM_END), (B0 + BP, FIRST, B0)):
            to = slice(place, place + last - first)
            proj5_out[to, 0:128] = lead[0][first:last]
            proj5_out[to, 128:256] = lead[1][first:last]
            proj5_out[to, 256:384] = parts[4][first:last]
            proj5_out[to, 384:512] = parts[5][first:last]
            proj5_out[to, 512:] = tail[first:last]
        norm5_out[...] = slab[at : at + 16].astype(f32)


    wide5_grad, thin5_grad, proj5_grad, norms5 = unpacked(
        slab5,
        rows_5b,
        unpack5,
        conv_outs + [((FIRST, C_MID), f32), ((16, 128), f32)],
        5.0,
    )

    proj4_grad, norms4 = unpacked(
        slab_proj, rows_proj, unpack_proj, [((channels, FIRST), f32), ((16, 128), f32)], 2.0
    )

    wide4_grad, thin4_grad = unpacked(slab4, rows_conv, unpack_conv, conv_outs, 4.0)


    return (
        block_out,
        input_grad,
        proj4_grad,
        wide4_grad.reshape(conv_a_4f.shape),
        thin4_grad.reshape(conv_b_4f.shape),
        norms4[:8].reshape(-1),
        norms4[8:].reshape(-1),
        proj5_grad.T,
        wide5_grad.reshape(conv_a_5b.shape),
        thin5_grad.reshape(conv_b_5b.shape),
        norms5[:8].reshape(-1),
        norms5[8:].reshape(-1),
    )


def solution(mesh):
    banded = P(None, "dp", None, "space", None, None)
    halved_specs = P("segment", "dp", None, "space", None, None)
    in_specs = (banded,) + (P(),) * 11 + (banded,)
    out_specs = (halved_specs, halved_specs) + (P(),) * 10
    return jax.shard_map(shards, mesh=mesh, in_specs=in_specs, out_specs=out_specs, check_vma=False)
```

```python
import functools

import jax
import jax.numpy as jnp
from jax import lax
from jax.experimental import pallas as pl
from jax.experimental.pallas import tpu as pltpu
from jax.sharding import PartitionSpec as P

B0 = 256
B1R = 160
B2R = 32
B1 = 320
B2 = 128
BP = 128
FIRST = 576
STEMS = B1R + B2R
STEM_END = B0 + STEMS
SECOND = B1 + B2
REST = SECOND + BP
C_MID = B0 + REST
BESIDE = 640
GRANULE = 16
SCALE = 3.0
PADDED = 256

SEG, DP, BAND, FIRST_CLIP, MY_MICRO, COUNTED, TABLES = range(7)

epsilon = 0.001
bf16 = jnp.bfloat16
f32 = jnp.float32
i32 = jnp.int32


def matching(edges):
    by_sender = {}
    for edge in edges:
        by_sender.setdefault(edge[0], []).append(edge)
    taken = {}

    def place(sender, seen):
        for edge in by_sender[sender]:
            receiver = edge[1]
            if receiver in seen:
                continue
            seen.add(receiver)
            if receiver not in taken or place(taken[receiver][0], seen):
                taken[receiver] = edge
                return True
        return False

    for sender in sorted(by_sender):
        place(sender, set())
    return sorted(taken.values())


class Route:
    def __init__(self, edges, devices):
        left, self.rounds = list(edges), []
        while left:
            chosen = matching(left)
            for edge in chosen:
                left.remove(edge)
            self.rounds.append(chosen)
        self.blocks = [[0] * len(self.rounds) for _ in range(devices)]
        self.slots = [[0] * len(self.rounds) for _ in range(devices)]
        for turn, chosen in enumerate(self.rounds):
            for sender, receiver, block, slot in chosen:
                self.blocks[sender][turn] = block
                self.slots[receiver][turn] = slot

    def send(self, parts):
        got = []
        for part, chosen in zip(parts, self.rounds):
            if all(edge[0] == edge[1] for edge in chosen):
                got.append(part)
            else:
                pairs = [(edge[0], edge[1]) for edge in chosen]
                got.append(lax.ppermute(part, ("segment", "space"), pairs))
        return got


def pairing(peers, step):
    return [(i, i ^ step) for i in range(peers)]


def exchanged(parts, axis):
    peers = lax.axis_size(axis)
    assert peers & (peers - 1) == 0
    return [parts[0]] + [lax.ppermute(parts[k], axis, pairing(peers, k)) for k in range(1, peers)]


def copies(x, axis):
    return exchanged([x] * lax.axis_size(axis), axis)


def sum_over(x, axis):
    if lax.axis_size(axis) > 4:
        return lax.psum(x, axis)
    got = copies(x, axis)
    return functools.reduce(jnp.add, got)


class Order:
    def __init__(self):
        self.last = []


order = Order()


def call(body, outs, ins, numbers=(), scratch=(), us=2.0, limit=40):
    vmem = pl.BlockSpec(memory_space=pltpu.VMEM)
    smem = pl.BlockSpec(memory_space=pltpu.SMEM)
    skipped, after = len(numbers) + len(ins), order.last

    def waited(*refs):
        body(*refs[:skipped], *refs[skipped + len(after) :])

    got = pl.pallas_call(
        waited,
        out_shape=[jax.ShapeDtypeStruct(shape, dtype) for shape, dtype in outs],
        in_specs=[smem] * len(numbers)
        + [vmem] * len(ins)
        + [pl.BlockSpec(memory_space=pl.ANY)] * len(after),
        out_specs=[vmem] * len(outs),
        scratch_shapes=[pltpu.VMEM(shape, dtype) for shape, dtype in scratch],
        cost_estimate=pl.CostEstimate(
            flops=int(us * SCALE * 1.1e9), bytes_accessed=10**6, transcendentals=0
        ),
        compiler_params=pltpu.CompilerParams(vmem_limit_bytes=limit * 2**20),
    )(*numbers, *ins, *after)
    order.last = [got[-1]]
    return got


def dot(a, b):
    return jnp.dot(a, b, preferred_element_type=f32)


def dot_nt(a, b):
    return lax.dot_general(a, b, (((1,), (1,)), ((), ())), preferred_element_type=f32)


def dot_tn(a, b):
    return lax.dot_general(a, b, (((0,), (0,)), ((), ())), preferred_element_type=f32)


def mask_of(cells, rows, width, height, across, first_row=0):
    place = lax.broadcasted_iota(i32, (cells, 1), 0)
    column = lax.rem(place, width)
    row = lax.rem(lax.div(place, width), rows) + first_row
    return jnp.where((row < height) & (column < across), 1.0, 0.0).astype(f32)


def pool_matrix(frames, rows, width, up):
    cells, pooled = frames * rows * width, frames * rows * width // 8
    shape = (cells, pooled) if up else (pooled, cells)
    place = lax.broadcasted_iota(i32, shape, 0 if up else 1)
    target = lax.broadcasted_iota(i32, shape, 1 if up else 0)
    column = lax.rem(place, width) // 2
    row = lax.rem(lax.div(place, width), rows) // 2
    frame = lax.div(place, width * rows) // 2
    home = (frame * (rows // 2) + row) * (width // 2) + column
    return jnp.where(home == target, 0.125, 0.0).astype(bf16)


def moments(totals, inverse):
    mean = totals[0:1] * inverse
    variance = totals[1:2] * inverse - mean * mean
    return mean, lax.rsqrt(variance + epsilon)


def column_shift(x, width, by):
    cells = x.shape[0]
    column = lax.rem(lax.broadcasted_iota(i32, (cells, 1), 0), width)
    edge = 0 if by == 1 else width - 1
    return jnp.where(column == edge, 0.0, pltpu.roll(x, by % cells, 0))


def silu(active):
    return active * jax.nn.sigmoid(active)


def slope(active, upstream):
    sig = jax.nn.sigmoid(active)
    return upstream * sig * (1.0 + active * (1.0 - sig))


def sums(a, b):
    return jnp.concatenate(
        [jnp.sum(a, axis=0, keepdims=True), jnp.sum(a * b, axis=0, keepdims=True)], axis=0
    )


def box_mean(x, frames, rows, width):
    cells, channels = x.shape
    x = x + column_shift(x, width, 1) + column_shift(x, width, -1)
    x = x.reshape(frames, rows, width, channels)
    edge = jnp.zeros((frames, 1, width, channels), f32)
    x = (
        x
        + jnp.concatenate([edge, x[:, : rows - 1]], axis=1)
        + jnp.concatenate([x[:, 1:], edge], axis=1)
    )
    edge = jnp.zeros((1, rows, width, channels), f32)
    x = (
        x
        + jnp.concatenate([edge, x[: frames - 1]], axis=0)
        + jnp.concatenate([x[1:], edge], axis=0)
    )
    return x.reshape(cells, channels) * (1.0 / 27.0)


def place_bands(dst, blocks, slots, frames, rows, width):
    for turn, block in enumerate(blocks):
        part = block[...].astype(dst.dtype).reshape(frames, rows, width, dst.shape[-1])
        dst[:, pl.ds(slots[turn] * rows, rows)] = part


def fill_beside(beside, stems, frames, rows, width):
    beside[...] = jnp.zeros_like(beside)
    three = jnp.concatenate(
        [column_shift(stems, width, 1), stems, column_shift(stems, width, -1)], axis=1
    )
    three = three.astype(beside.dtype).reshape(frames, rows, width, 3 * STEMS)
    beside[1 : frames + 1, 1 : rows + 1, :, : 3 * STEMS] = three


def fill_conv_weights(flat, wide, thin):
    flat[...] = jnp.zeros_like(flat)
    for tap in range(27):
        row = (tap // 3) * BESIDE + (tap % 3) * STEMS
        flat[row : row + B1R, B2:] = wide[tap]
        flat[row + B1R : row + STEMS, :B2] = thin[tap]


def fill_back_weights(flat, wide, thin):
    flat[...] = jnp.zeros_like(flat)
    for tap in range(27):
        start = tap * 512
        flat[:B1R, start + B2 : start + SECOND] = wide[26 - tap]
        flat[B1R:, start : start + B2] = thin[26 - tap]


def fill_shifted(shifted, grad, frames, rows, width):
    shifted[...] = jnp.zeros_like(shifted)
    for dc in range(3):
        moved = grad if dc == 1 else column_shift(grad, width, 1 - dc)
        moved = moved.astype(shifted.dtype).reshape(frames, rows, width, SECOND)
        shifted[dc, 1 : frames + 1, 1 : rows + 1, :, :SECOND] = moved


def window(padded, f, r, frames, rows):
    part = padded[f : f + frames, r : r + rows]
    return part.reshape(frames * rows * part.shape[2], part.shape[3]).astype(bf16)


def conv_chunk(beside, flat, start, step, rows):
    taps = [window(beside, start + f, r, step, rows) for f in range(3) for r in range(3)]
    return dot(jnp.concatenate(taps, axis=1), flat[...])


def back_chunk(shifted, flat, start, step, rows):
    taps = [
        window(shifted.at[dc], start + f, r, step, rows)
        for f in range(3)
        for r in range(3)
        for dc in range(3)
    ]
    return dot_nt(jnp.concatenate(taps, axis=1), flat[...])


def pack_conv(slab, beside, dz, frames, rows, width, scale):
    cells = frames * rows * width
    wide_dz, thin_dz = dz[:, B2:], dz[:, :B2]
    half = 27 * B1R // 2
    for f in range(3):
        for r in range(3):
            part = window(beside, f, r, frames, rows)
            wide = dot_tn(part, wide_dz) * scale
            thin = dot_tn(part, thin_dz) * scale
            for c in range(3):
                tap = (f * 3 + r) * 3 + c
                rows_wide = wide[c * STEMS : c * STEMS + B1R].astype(bf16)
                slab[tap * B1R : (tap + 1) * B1R] = rows_wide[:, :128]
                at = 27 * B1R + tap * B1R
                slab[at : at + B1R] = rows_wide[:, 128:256]
                for piece in range(2):
                    row = tap * B1R + piece * 80
                    side = row >= half
                    at = 2 * 27 * B1R + row - (half if side else 0)
                    lanes = slice(64, 128) if side else slice(0, 64)
                    slab[at : at + 80, lanes] = rows_wide[piece * 80 : piece * 80 + 80, 256:]
                at = 2 * 27 * B1R + half + tap * B2R
                slab[at : at + B2R] = thin[c * STEMS + B1R : (c + 1) * STEMS].astype(bf16)


CONV_ROWS = 2 * 27 * B1R + 27 * B1R // 2 + 27 * B2R


def halved(n):
    return -(-n // (2 * GRANULE)) * GRANULE


def pack_matrix(slab, at, matrix):
    n, lanes = matrix.shape
    blocks, half = lanes // 128, halved(n)
    matrix = matrix.astype(bf16)
    for j in range(blocks):
        slab[at + j * n : at + (j + 1) * n] = matrix[:, j * 128 : (j + 1) * 128]
    at = at + blocks * n
    left, right = matrix[:half, blocks * 128 :], matrix[half:, blocks * 128 :]
    if n < 2 * half:
        right = jnp.concatenate([right, jnp.zeros((2 * half - n, 64), bf16)], axis=0)
    slab[at : at + half] = jnp.concatenate([left, right], axis=1)
    return at + half


def pack_norms(slab, at, gain, bias):
    rows = [row[:, j * 128 : (j + 1) * 128] for row in (gain, bias) for j in range(8)]
    slab[at : at + 16] = jnp.concatenate(rows, axis=0).astype(bf16)


def give_halves(slab, seg, mine, other):
    half = mine.shape[0]
    mine[...] = slab[pl.ds(seg * half, half)]
    other[...] = slab[pl.ds((1 - seg) * half, half)]


def unpack_conv(slab, wide_out, thin_out):
    half = 27 * B1R // 2
    for tap in range(27):
        at = tap * B1R
        wide_out[tap, :, :128] = slab[at : at + B1R].astype(f32)
        wide_out[tap, :, 128:256] = slab[27 * B1R + at : 27 * B1R + at + B1R].astype(f32)
        for piece in range(2):
            row = at + piece * 80
            side = row >= half
            start = 2 * 27 * B1R + row - (half if side else 0)
            part = slab[start : start + 80].astype(f32)
            part = part[:, 64:] if side else part[:, :64]
            wide_out[tap, piece * 80 : piece * 80 + 80, 256:] = part
        at = 2 * 27 * B1R + half + tap * B2R
        thin_out[tap] = slab[at : at + B2R].astype(f32)


def unpack_matrix(slab, at, n, lanes):
    blocks, half = lanes // 128, halved(n)
    parts = [slab[at + j * n : at + (j + 1) * n].astype(f32) for j in range(blocks)]
    at = at + blocks * n
    tail = slab[at : at + half].astype(f32)
    parts.append(jnp.concatenate([tail[:, :64], tail[: n - half, 64:]], axis=0))
    return parts, at + half


def matrix_rows(n, lanes):
    return lanes // 128 * n + halved(n)


def padded_rows(rows):
    unit = GRANULE * lax.axis_size("segment") * lax.axis_size("dp") * lax.axis_size("space")
    return -(-rows // unit) * unit


def split_sum(parts, pieces, row, at):
    rows = parts[0].shape[0] // pieces

    def body(row_ref, *refs):
        ins, outs = refs[: len(parts)], refs[len(parts) :]
        for k, out in enumerate(outs):
            start = (row_ref[at] ^ k) * rows if pieces > 1 else 0
            if pieces > 1:
                start = pl.multiple_of(start, GRANULE)
            total = ins[0][pl.ds(start, rows)].astype(f32)
            for ref in ins[1:]:
                total = total + ref[pl.ds(start, rows)].astype(f32)
            out[...] = total.astype(bf16)

    outs = [((rows, 128), bf16)] * pieces
    return call(body, outs, parts, [row], us=1.0, limit=32)


def joined(parts, row, at):
    rows, pieces = parts[0].shape[0], len(parts)

    def body(row_ref, *refs):
        for k, ref in enumerate(refs[:-1]):
            start = (row_ref[at] ^ k) * rows
            refs[-1][pl.ds(pl.multiple_of(start, GRANULE), rows)] = ref[...]

    outs = [((rows * pieces, 128), bf16)]
    return call(body, outs, parts, [row], us=1.0, limit=32)[0]


def swapped(x):
    return lax.ppermute(x, "segment", [(0, 1), (1, 0)])


class Slab:
    def __init__(self, mine, other, row):
        self.row, self.parts = row, [mine, swapped(other)]

    def to_dp(self):
        self.parts = exchanged(split_sum(self.parts, lax.axis_size("dp"), self.row, DP), "dp")

    def to_dp_again(self):
        pass

    def to_space(self):
        bands = lax.axis_size("space")
        self.parts = exchanged(split_sum(self.parts, bands, self.row, BAND), "space")

    def summed(self):
        self.parts = copies(split_sum(self.parts, 1, self.row, BAND)[0], "space")

    def to_shard(self):
        self.shard = split_sum(self.parts, 1, self.row, BAND)[0]

    def back_dp(self):
        held = copies(joined(self.parts, self.row, BAND), "dp")
        self.parts = held + [swapped(part) for part in held]

    def back_dp_again(self):
        pass

    def place(self, slab, pieces, row_ref):
        rows, peers = pieces[0].shape[0], len(pieces) // 2
        for k, piece in enumerate(pieces):
            side = row_ref[SEG] if k < peers else 1 - row_ref[SEG]
            at = (side * peers + (row_ref[DP] ^ (k % peers))) * rows
            slab[pl.ds(pl.multiple_of(at, GRANULE), rows)] = piece[...]


class CrossSlab(Slab):
    def to_dp(self):
        mine, got = self.parts
        self.quarter = mine.shape[0] // 4
        half, quarter = self.quarter // 2, self.quarter

        def body(row_ref, mine_ref, got_ref, to_x, to_y, keep_a, keep_b):
            y, x = lax.div(row_ref[DP], 2), lax.rem(row_ref[DP], 2)
            for k in range(2):
                to = slice(k * half, (k + 1) * half)
                for out, start in (
                    (to_x, (k * 2 + (1 - x)) * quarter),
                    (keep_a, (k * 2 + x) * quarter),
                    (to_y, ((1 - y) * 2 + k) * quarter + half),
                    (keep_b, (y * 2 + k) * quarter + half),
                ):
                    at = pl.ds(pl.multiple_of(start, GRANULE), half)
                    total = mine_ref[at].astype(f32) + got_ref[at].astype(f32)
                    out[to] = total.astype(out.dtype)

        send, keep = ((2 * half, 128), bf16), ((2 * half, 128), f32)
        to_x, to_y, *self.kept = call(
            body, [send, send, keep, keep], [mine, got], [self.row], us=1.3, limit=32
        )
        self.got = [lax.ppermute(to_x, "dp", pairing(4, 1)), lax.ppermute(to_y, "dp", pairing(4, 2))]

    def to_dp_again(self):
        half = self.quarter // 2

        def body(row_ref, keep_a, keep_b, got_a, got_b, send_a, send_b, next_a, next_b):
            y, x = lax.div(row_ref[DP], 2), lax.rem(row_ref[DP], 2)
            for keep, got, send, own, place in (
                (keep_a, got_a, send_a, next_a, y),
                (keep_b, got_b, send_b, next_b, x),
            ):
                at = pl.ds(pl.multiple_of(place * half, GRANULE), half)
                own[...] = keep[at] + got[at].astype(f32)
                at = pl.ds(pl.multiple_of((1 - place) * half, GRANULE), half)
                send[...] = (keep[at] + got[at].astype(f32)).astype(bf16)

        send, keep = ((half, 128), bf16), ((half, 128), f32)
        to_y, to_x, *self.kept = call(
            body, [send, send, keep, keep], self.kept + self.got, [self.row], us=1.0, limit=32
        )
        self.got = [lax.ppermute(to_y, "dp", pairing(4, 2)), lax.ppermute(to_x, "dp", pairing(4, 1))]

    def to_space(self):
        half, bands = self.quarter // 2, lax.axis_size("space")
        rows = self.quarter // bands

        def body(row_ref, keep_a, keep_b, got_a, got_b, own, *refs):
            outs, whole = refs[:-1], refs[-1]
            whole[:half] = keep_a[...] + got_a[...].astype(f32)
            whole[half:] = keep_b[...] + got_b[...].astype(f32)
            for k, out in enumerate((own,) + outs):
                at = pl.ds(pl.multiple_of((row_ref[BAND] ^ k) * rows, GRANULE), rows)
                out[...] = whole[at].astype(out.dtype)

        outs = [((rows, 128), f32)] + [((rows, 128), bf16)] * (bands - 1)
        scratch = [((self.quarter, 128), f32)]
        parts = call(body, outs, self.kept + self.got, [self.row], scratch, us=1.0, limit=32)
        self.parts = exchanged(parts, "space")

    def back_dp(self):
        half, bands = self.quarter // 2, lax.axis_size("space")
        rows = self.quarter // bands

        def body(row_ref, *refs):
            parts, (out_a, out_b, whole) = refs[:bands], refs[bands:]
            for k, ref in enumerate(parts):
                at = pl.ds(pl.multiple_of((row_ref[BAND] ^ k) * rows, GRANULE), rows)
                whole[at] = ref[...]
            out_a[...] = whole[:half]
            out_b[...] = whole[half:]

        outs, scratch = [((half, 128), bf16)] * 2, [((self.quarter, 128), bf16)]
        a, b = call(body, outs, self.parts, [self.row], scratch, us=1.0, limit=32)
        self.got = [lax.ppermute(a, "dp", pairing(4, 2)), lax.ppermute(b, "dp", pairing(4, 1))]
        self.kept = [a, b]

    def back_dp_again(self):
        half = self.quarter // 2

        def body(row_ref, own_a, own_b, got_a, got_b, pair_a, pair_b, both):
            y, x = lax.div(row_ref[DP], 2), lax.rem(row_ref[DP], 2)
            for own, got, out, place in ((own_a, got_a, pair_a, y), (own_b, got_b, pair_b, x)):
                out[pl.ds(pl.multiple_of(place * half, GRANULE), half)] = own[...]
                out[pl.ds(pl.multiple_of((1 - place) * half, GRANULE), half)] = got[...]
            both[: 2 * half] = pair_a[...]
            both[2 * half :] = pair_b[...]

        outs = [((2 * half, 128), bf16)] * 2 + [((4 * half, 128), bf16)]
        a, b, both = call(body, outs, self.kept + self.got, [self.row], us=1.0, limit=32)
        got = [lax.ppermute(a, "dp", pairing(4, 1)), lax.ppermute(b, "dp", pairing(4, 2))]
        self.parts = [both] + got + [swapped(part) for part in [both] + got]

    def place(self, slab, pieces, row_ref):
        half, quarter = self.quarter // 2, self.quarter
        y, x = lax.div(row_ref[DP], 2), lax.rem(row_ref[DP], 2)
        for turn, side in enumerate((row_ref[SEG], 1 - row_ref[SEG])):
            both, far_a, far_b = pieces[3 * turn : 3 * turn + 3]
            a, b = both.at[: 2 * half], both.at[2 * half :]
            for k in range(2):
                part = slice(k * half, (k + 1) * half)
                for ref, start in (
                    (a, (k * 2 + x) * quarter),
                    (far_a, (k * 2 + (1 - x)) * quarter),
                    (b, (y * 2 + k) * quarter + half),
                    (far_b, ((1 - y) * 2 + k) * quarter + half),
                ):
                    at = pl.multiple_of(side * 4 * quarter + start, GRANULE)
                    slab[pl.ds(at, half)] = ref[part]


class JointSlab(CrossSlab):
    def __init__(self, first, second, row):
        self.first, self.second, self.row = first, second, row

    def summed(self):
        shard, parts, bands = self.first.shard, self.second.parts, lax.axis_size("space")
        self.sizes = [shard.shape[0], parts[0].shape[0]]
        unit = sum(self.sizes)

        def body(first, *refs):
            refs[-1][: self.sizes[0]] = first[...]
            total = functools.reduce(jnp.add, [ref[...].astype(f32) for ref in refs[:-1]])
            refs[-1][self.sizes[0] :] = total.astype(bf16)

        (joint,) = call(body, [((unit, 128), bf16)], [shard] + parts, us=1.0, limit=32)
        self.quarter = unit * bands
        self.parts = copies(joint, "space")

    def place(self, slab, pieces, row_ref):
        bands, unit = lax.axis_size("space"), sum(self.sizes)
        half = self.quarter // 2
        y, x = lax.div(row_ref[DP], 2), lax.rem(row_ref[DP], 2)
        for turn, side in enumerate((row_ref[SEG], 1 - row_ref[SEG])):
            both, far_a, far_b = pieces[3 * turn : 3 * turn + 3]
            for k in range(2):
                for ref, at, quarter, second in (
                    (both, k * half, k * 2 + x, 0),
                    (far_a, k * half, k * 2 + (1 - x), 0),
                    (both, (2 + k) * half, y * 2 + k, 1),
                    (far_b, k * half, (1 - y) * 2 + k, 1),
                ):
                    for band in range(bands // 2):
                        base, start = 0, at + band * unit
                        for size in self.sizes:
                            place = (side * 4 + quarter) * bands + second * (bands // 2) + band
                            to = pl.multiple_of(base + place * size, GRANULE)
                            slab[pl.ds(to, size)] = ref[start : start + size]
                            base, start = base + 8 * bands * size, start + size


def widened(x):
    more = PADDED - x.shape[1]
    return jnp.concatenate([x, jnp.zeros((2, more), f32)], axis=1) if more else x


def pack_lanes(out, at, x):
    cells, channels = x.shape
    for start in range(0, channels, 128):
        part = x[:, start : start + 128]
        if part.shape[1] < 128:
            part = jnp.concatenate([part, jnp.zeros((cells, 128 - part.shape[1]), f32)], axis=1)
        out[at : at + cells] = part.astype(bf16)
        at += cells
    return at


def unpacked_lanes(ref, at, cells, channels):
    parts = []
    for start in range(0, channels, 128):
        parts.append(ref[at : at + cells, : min(128, channels - start)].astype(f32))
        at += cells
    return jnp.concatenate(parts, axis=1)


def shards(
    inputs,
    crop_group,
    in_proj_4f,
    conv_a_4f,
    conv_b_4f,
    gain_4f,
    bias_4f,
    in_proj_5b,
    conv_a_5b,
    conv_b_5b,
    gain_5b,
    bias_5b,
    out_grad,
):
    order.last = []
    segs, dps, bands = (lax.axis_size(axis) for axis in ("segment", "dp", "space"))
    micro, clips, frames, rows, width, channels = inputs.shape
    full_rows, all_clips = rows * bands, clips * dps
    halves = micro // segs
    held = halves * clips
    items = micro * clips
    spread = segs if items == segs * bands else 1
    assert segs == 2 and items == spread * bands and clips % spread == 0
    each = clips // spread
    cells, part_cells = frames * full_rows * width, frames * rows * width
    frames5, rows5, width5 = frames // 2, full_rows // 2, width // 2
    cells5, part_cells5 = cells // 8, part_cells // 8
    band_rows5 = rows // 2

    inward, pooled_in, outward = [], [], []
    for s in range(segs):
        for z in range(bands):
            for item in range(bands):
                inward.append((s * bands + z, s * bands + item, item, z))
    for m in range(micro):
        for c in range(clips):
            if spread > 1:
                holders = [(c // each) * bands + m * each + c % each]
            else:
                holders = [s * bands + m * clips + c for s in range(segs)]
            home, local = m // halves, (m % halves) * clips + c
            for z in range(bands):
                for holder in holders:
                    pooled_in.append((home * bands + z, holder, local, z))
                outward.append((holders[z % len(holders)], home * bands + z, z, local))
    inward, pooled_in, outward = (
        Route(edges, segs * bands) for edges in (inward, pooled_in, outward)
    )
    IN_BLOCK = TABLES
    IN_SLOT = IN_BLOCK + len(inward.rounds)
    POOLED_BLOCK = IN_SLOT + len(inward.rounds)
    POOLED_SLOT = POOLED_BLOCK + len(pooled_in.rounds)
    OUT_BLOCK = POOLED_SLOT + len(pooled_in.rounds)
    OUT_SLOT = OUT_BLOCK + len(outward.rounds)
    table = []
    for s in range(segs):
        for d in range(dps):
            for z in range(bands):
                me = s * bands + z
                first = s * each if spread > 1 else 0
                counted = 1 if spread > 1 or s == 0 else 0
                line = [s, d, z, first, z // each, counted]
                for route in (inward, pooled_in, outward):
                    line = line + route.blocks[me] + route.slots[me]
                table.append(line)
    row = jnp.array(table, i32)[lax.axis_index(("segment", "dp", "space"))]
    numbers = [row, crop_group]

    def group_parts(x):
        if each > 1:
            pairs = [[z * each + k for k in range(each)] for z in range(micro)]
            x = lax.psum(x, "space", axis_index_groups=pairs)
        if spread > 1:
            x = x + swapped(x)
        if dps > 4:
            return [lax.psum(x, "dp")]
        return copies(x, "dp")

    def total_of(refs):
        return functools.reduce(jnp.add, [ref[...] for ref in refs])

    def crop(row_ref, group_ref, scale=1, m=None):
        group = group_ref[row_ref[MY_MICRO] if m is None else m]
        tall, wide = full_rows // scale, width // scale
        height, across = tall - group * (tall // 4), wide - group * (wide // 4)
        count = all_clips * (frames // scale) * height * across
        return height, across, 1.0 / jnp.full((1, 1), count, i32).astype(f32)

    LEAD, OUTER, STEM = slice(0, B0), slice(0, C_MID), slice(C_MID, None)
    RESTS = slice(B0, C_MID)
    wide4, thin4 = conv_a_4f.reshape(27, B1R, B1), conv_b_4f.reshape(27, B2R, B2)
    wide5, thin5 = conv_a_5b.reshape(27, B1R, B1), conv_b_5b.reshape(27, B2R, B2)

    def project_body(row_ref, group_ref, x_ref, p_ref, stat, pool, *outs):
        for k in range(bands):
            item = row_ref[IN_BLOCK + k]
            m, c = lax.div(item, each), row_ref[FIRST_CLIP] + lax.rem(item, each)
            x = x_ref[m, c].reshape(part_cells, channels)
            height, across, _ = crop(row_ref, group_ref, 1, m)
            mask = mask_of(part_cells, rows, width, height, across, row_ref[BAND] * rows)
            z = dot(x, p_ref[:, B0:]) * mask
            stem = z[:, :STEMS]
            outs[k][...] = stem.astype(bf16)
            pool[k] = z[:, STEMS:].astype(bf16)
            stat[item] = sums(stem, stem)

    got = call(
        project_body,
        [((bands, 2, STEMS), f32), ((bands, part_cells, BP), bf16)]
        + [((part_cells, STEMS), bf16)] * bands,
        [inputs, in_proj_4f],
        numbers,
        us=1.5,
    )
    stem_stat, pool_parts, stem_parts = got[0], got[1], got[2:]
    stem_blocks = inward.send(stem_parts)

    def home_crop(row_ref, group_ref, i):
        m = row_ref[SEG] * halves + i // clips
        height, across, inverse = crop(row_ref, group_ref, 1, m)
        first = row_ref[BAND] * rows
        return m, mask_of(part_cells, rows, width, height, across, first), inverse

    lanes5 = -(-C_MID // 128)
    carried = part_cells + lanes5 * part_cells5

    def lead_body(row_ref, group_ref, x_ref, p_ref, stem_stat, pool, upper, *refs):
        lead_out, stem_out, stat, outs = refs[0], refs[1], refs[2], refs[3:]
        for i in range(held):
            m, mask, _ = home_crop(row_ref, group_ref, i)
            x = x_ref[m, i % clips].reshape(part_cells, channels)
            z = dot(x, p_ref[:, :STEM_END]) * mask
            lead = z[:, :B0]
            lead_out[i] = lead
            stem_out[i] = z[:, B0:]
            total = sums(lead, lead)
            j = bands + i // clips
            stat[j] = total if i % clips == 0 else stat[j] + total
        for k in range(bands):
            stat[k] = widened(stem_stat[k])
            item = row_ref[IN_BLOCK + k]
            m, c = lax.div(item, each), row_ref[FIRST_CLIP] + lax.rem(item, each)
            outs[k][:part_cells] = pool[k]
            pack_lanes(outs[k], part_cells, upper[m, c].astype(f32).reshape(part_cells5, C_MID))

    got = call(
        lead_body,
        [
            ((held, part_cells, B0), f32),
            ((held, part_cells, STEMS), f32),
            ((bands + halves, 2, PADDED), f32),
        ]
        + [((carried, 128), bf16)] * bands,
        [inputs, in_proj_4f, stem_stat, pool_parts, out_grad],
        numbers,
        us=2.5,
    )
    lead, home_stem, stat = got[:3]

    def all_parts(x, axis):
        return [lax.psum(x, axis)] if lax.axis_size(axis) > 4 else copies(x, axis)

    def whole_body(*refs):
        refs[-1][...] = total_of(refs[:-1])

    def summed_dp(x):
        parts = all_parts(x, "dp")
        return call(whole_body, [(x.shape, f32)], parts, us=0.8)[0]

    def share_body(row_ref, own, other, *outs):
        for k, out in enumerate(outs):
            item = row_ref[BAND] ^ k
            first = lax.div(item, each) * each
            total = jnp.zeros((2, PADDED), f32)
            for c in range(each):
                total = total + own[first + c]
                if spread > 1:
                    total = total + other[first + c]
            out[0] = total
            for j in range(halves):
                out[1 + j] = own[bands + j]

    stat = summed_dp(stat)
    stat_parts = call(
        share_body,
        [((1 + halves, 2, PADDED), f32)] * bands,
        [stat, swapped(stat)],
        [row],
        us=0.8,
    )
    stat_parts = exchanged(stat_parts, "space")
    carried_blocks = inward.send(got[3:])

    def arrange_body(gain4, bias4, gain5, bias5, p4, p5, affine4, affine5, proj4, proj5):
        for gain, bias, out in ((gain4, bias4, affine4), (gain5, bias5, affine5)):
            for k, ref in enumerate((gain, bias)):
                v = ref[...]
                out[k : k + 1] = jnp.concatenate(
                    [
                        v[:, :B0],
                        v[:, STEM_END:FIRST],
                        v[:, FIRST + B1 :],
                        v[:, FIRST : FIRST + B1],
                        v[:, B0:STEM_END],
                    ],
                    axis=1,
                )
        proj4[:, :B0] = p4[:, :B0]
        proj4[:, B0:] = jnp.concatenate([p4[:, STEM_END:], p4[:, B0:STEM_END]], axis=1)
        for first, last, to in ((0, B0, 0), (STEM_END, FIRST, B0), (B0, STEM_END, B0 + BP)):
            rows_in = p5[first:last]
            proj5[to : to + last - first, :B0] = rows_in[:, :B0]
            proj5[to : to + last - first, B0:] = jnp.concatenate(
                [
                    rows_in[:, B0 + SECOND :],
                    rows_in[:, B0 + B1 : B0 + SECOND],
                    rows_in[:, B0 : B0 + B1],
                ],
                axis=1,
            )

    affine4, affine5, proj4, proj5 = call(
        arrange_body,
        [((2, 1024), f32)] * 2 + [((channels, FIRST), bf16), ((FIRST, C_MID), bf16)],
        [v.reshape(1, -1) for v in (gain_4f, bias_4f, gain_5b, bias_5b)]
        + [in_proj_4f, in_proj_5b.T],
        us=2.0,
    )

    def lead_act(i, lead_ref, stat_ref, affine_ref, inverse):
        mean, scale = moments(stat_ref[i // clips], inverse)
        norm = (lead_ref[i] - mean) * scale
        return norm, scale, norm * affine_ref[0:1, LEAD] + affine_ref[1:2, LEAD]

    def lead_out_body(row_ref, group_ref, lead_ref, affine_ref, *refs):
        parts, stat_ref, outs, kept = refs[:bands], refs[bands], refs[bands + 1 : -1], refs[-1]
        stat_ref[...] = total_of(parts)[1:]
        matrix = pool_matrix(frames, rows, width, False)
        for i in range(held):
            _, mask, inverse = home_crop(row_ref, group_ref, i)
            _, _, active = lead_act(i, lead_ref, stat_ref, affine_ref, inverse)
            kept[i] = dot(matrix, (silu(active) * mask).astype(bf16)).astype(bf16)
        for turn, out in enumerate(outs):
            out[...] = kept[row_ref[POOLED_BLOCK + turn]]

    got = call(
        lead_out_body,
        [((halves, 2, B0), f32)] + [((part_cells5, B0), bf16)] * len(pooled_in.rounds),
        [lead, affine4] + stat_parts,
        numbers,
        [((held, part_cells5, B0), bf16)],
        us=1.8,
    )
    lead_stat = got[0]
    lead_pooled = pooled_in.send(got[1:])

    step = 2 if full_rows * width <= 128 else 1

    def conv_body(row_ref, group_ref, affine_ref, wide_ref, thin_ref, *refs):
        stats, blocks = refs[:bands], refs[bands : 2 * bands]
        second_out, sums_out, norm_out, stat_out, beside, stage, flat = refs[2 * bands :]
        height, across, inverse = crop(row_ref, group_ref)
        totals = functools.reduce(jnp.add, [ref[0] for ref in stats])[:, :STEMS]
        mean, scale = moments(totals, inverse)
        stat_out[...] = totals
        fill_conv_weights(flat, wide_ref, thin_ref)
        slots = [row_ref[IN_SLOT + k] for k in range(bands)]
        place_bands(stage, blocks, slots, frames, rows, width)
        mask = mask_of(cells, full_rows, width, height, across)
        norm = (stage[...].reshape(cells, STEMS) - mean) * scale
        norm_out[...] = norm
        active = norm * affine_ref[0:1, STEM] + affine_ref[1:2, STEM]
        fill_beside(beside, silu(active) * mask, frames, full_rows, width)
        chunk = step * full_rows * width
        total = jnp.zeros((2, SECOND), f32)
        for start in range(0, frames, step):
            got = conv_chunk(beside, flat, start, step, full_rows)
            second_out[start * full_rows * width : start * full_rows * width + chunk] = got
            total = total + sums(got * mask[:chunk], got)
        sums_out[...] = total

    second, second_sums, stem_norm, stem_total, beside = call(
        conv_body,
        [
            ((cells, SECOND), f32),
            ((2, SECOND), f32),
            ((cells, STEMS), f32),
            ((2, STEMS), f32),
            ((frames + 2, full_rows + 2, width, BESIDE), bf16),
        ],
        [affine4, wide4, thin4] + stat_parts + stem_blocks,
        numbers,
        [
            ((frames, full_rows, width, STEMS), f32),
            ((9 * BESIDE, SECOND), bf16),
        ],
        us=9.0,
    )

    def pool_body(row_ref, group_ref, second_sums, *refs):
        blocks, (zp_out, sums_out, stage) = refs[:bands], refs[bands:]
        height, across, _ = crop(row_ref, group_ref)
        slots = [row_ref[IN_SLOT + k] for k in range(bands)]
        place_bands(stage, [ref.at[:part_cells] for ref in blocks], slots, frames, rows, width)
        zp = box_mean(stage[...].reshape(cells, BP), frames, full_rows, width)
        zp_out[...] = zp
        mask = mask_of(cells, full_rows, width, height, across)
        sums_out[...] = jnp.concatenate([sums(zp * mask, zp), second_sums[...]], axis=1)

    zp, rest_sums = call(
        pool_body,
        [((cells, BP), f32), ((2, REST), f32)],
        [second_sums] + carried_blocks,
        numbers,
        [((frames, full_rows, width, BP), f32)],
        us=1.3,
    )
    rest_parts = group_parts(rest_sums)
    n_parts = len(rest_parts)

    span = 2 * full_rows * width

    def rest_of(zp_ref, second_ref, start, affine_ref, mean, scale):
        z = jnp.concatenate(
            [zp_ref[start : start + span], second_ref[start : start + span]], axis=1
        )
        norm = (z - mean) * scale
        return norm, norm * affine_ref[0:1, RESTS] + affine_ref[1:2, RESTS]

    def middle_body(row_ref, group_ref, affine_ref, p_ref, zp_ref, second_ref, *refs):
        parts, leads = refs[:n_parts], refs[n_parts:-6]
        stat_out, pooled, first_out, sums_out, stage, kept = refs[-6:]
        height, across, inverse = crop(row_ref, group_ref)
        mean, scale = moments(total_of(parts), inverse)
        stat_out[...] = jnp.concatenate([mean, scale], axis=0)
        mask = mask_of(span, full_rows, width, height, across)
        matrix = pool_matrix(2, full_rows, width, False)
        slots = [row_ref[POOLED_SLOT + k] for k in range(len(leads))]
        place_bands(stage, leads, slots, frames5, band_rows5, width5)
        pooled[:, :B0] = stage[...].reshape(cells5, B0).astype(bf16)
        for f in range(frames5):
            _, active = rest_of(zp_ref, second_ref, f * span, affine_ref, mean, scale)
            out = dot(matrix, (silu(active) * mask).astype(bf16))
            pooled[f * span // 8 : (f + 1) * span // 8, B0:] = out.astype(bf16)
        z = dot_nt(pooled[...], p_ref[...])
        kept[...] = z
        project = z[:, LEAD.stop : LEAD.stop + BP].astype(bf16).astype(f32)
        kept[:, B0 : B0 + BP] = box_mean(project, frames5, rows5, width5)
        z = kept[...]
        first_out[...] = z
        height, across, _ = crop(row_ref, group_ref, 2)
        sums_out[...] = sums(z * mask_of(cells5, rows5, width5, height, across), z)

    rest_stat, pooled, first5, first5_sums = call(
        middle_body,
        [((2, REST), f32), ((cells5, C_MID), bf16), ((cells5, FIRST), f32), ((2, FIRST), f32)],
        [affine4, proj5, zp, second] + rest_parts + lead_pooled,
        numbers,
        [((frames5, rows5, width5, B0), f32), ((cells5, FIRST), f32)],
    )
    first5_parts = group_parts(first5_sums)

    def conv5_body(row_ref, group_ref, affine_ref, wide_ref, thin_ref, first_ref, *refs):
        parts = refs[:n_parts]
        second_out, sums_out, stat_out, beside, flat = refs[n_parts:]
        height, across, inverse = crop(row_ref, group_ref, 2)
        mean, scale = moments(total_of(parts), inverse)
        stat_out[...] = jnp.concatenate([mean, scale], axis=0)
        fill_conv_weights(flat, wide_ref, thin_ref)
        mask = mask_of(cells5, rows5, width5, height, across)
        stem = slice(B0 + BP, FIRST)
        norm = (first_ref[:, stem] - mean[:, stem]) * scale[:, stem]
        active = norm * affine_ref[0:1, STEM] + affine_ref[1:2, STEM]
        fill_beside(beside, silu(active) * mask, frames5, rows5, width5)
        got = conv_chunk(beside, flat, 0, frames5, rows5)
        second_out[...] = got
        sums_out[...] = sums(got * mask, got)

    second5, second5_sums, first5_stat, beside5 = call(
        conv5_body,
        [
            ((cells5, SECOND), f32),
            ((2, SECOND), f32),
            ((2, FIRST), f32),
            ((frames5 + 2, rows5 + 2, width5, BESIDE), f32),
        ],
        [affine5, wide5, thin5, first5] + first5_parts,
        numbers,
        [((9 * BESIDE, SECOND), bf16)],
    )
    second5_parts = group_parts(second5_sums)

    def out5_body(row_ref, group_ref, affine_ref, first_ref, stat_ref, second_ref, *refs):
        parts, uppers = refs[:n_parts], refs[n_parts : n_parts + bands]
        out, norm_out, slope_out, scale_out, sums_out, stage = refs[n_parts + bands :]
        height, across, inverse = crop(row_ref, group_ref, 2)
        mean2, scale2 = moments(total_of(parts), inverse)
        mask = mask_of(cells5, rows5, width5, height, across)
        outer = slice(0, B0 + BP)
        mean = jnp.concatenate([stat_ref[0:1, outer], mean2], axis=1)
        scale = jnp.concatenate([stat_ref[1:2, outer], scale2], axis=1)
        z = jnp.concatenate([first_ref[:, outer], second_ref[...]], axis=1)
        norm = (z - mean) * scale
        active = norm * affine_ref[0:1, OUTER] + affine_ref[1:2, OUTER]
        act = silu(active) * mask
        natural = [act[:, :B0], act[:, B0 + BP + B2 :], act[:, B0 + BP : B0 + BP + B2]]
        natural = jnp.concatenate(natural + [act[:, B0 : B0 + BP]], axis=1)
        out[...] = natural.reshape(frames5, rows5, width5, C_MID)
        for k, ref in enumerate(uppers):
            part = unpacked_lanes(ref, part_cells, part_cells5, C_MID)
            part = part.reshape(frames5, band_rows5, width5, C_MID)
            stage[:, pl.ds(row_ref[IN_SLOT + k] * band_rows5, band_rows5)] = part
        upper = stage[...].reshape(cells5, C_MID)
        upper = jnp.concatenate(
            [
                upper[:, :B0],
                upper[:, B0 + SECOND :],
                upper[:, B0 + B1 : B0 + SECOND],
                upper[:, B0 : B0 + B1],
            ],
            axis=1,
        )
        slopes = slope(active, upper * mask)
        norm_out[...] = norm
        slope_out[...] = slopes
        scale_out[...] = scale
        sums_out[...] = sums(slopes, norm)

    out5, outer5_norm, outer5_slope, outer5_scale, outer5_sums = call(
        out5_body,
        [
            ((frames5, rows5, width5, C_MID), f32),
            ((cells5, C_MID), f32),
            ((cells5, C_MID), f32),
            ((1, C_MID), f32),
            ((2, C_MID), f32),
        ],
        [affine5, first5, first5_stat, second5] + second5_parts + carried_blocks,
        numbers,
        [((frames5, rows5, width5, C_MID), f32)],
        us=1.4,
    )
    outer5_parts = group_parts(outer5_sums)

    def back5_body(row_ref, group_ref, affine_ref, wide_ref, thin_ref, *refs):
        norm_ref, slope_ref, scale_ref, first_ref, stat_ref = refs[:5]
        parts, refs = refs[5 : 5 + n_parts], refs[5 + n_parts :]
        dz_out, lead_out, project_out, slope_out, sums_out, shifted, flat = refs
        height, across, inverse = crop(row_ref, group_ref, 2)
        mask = mask_of(cells5, rows5, width5, height, across)
        fill_back_weights(flat, wide_ref, thin_ref)
        total = total_of(parts) * inverse
        grad = (mask * (affine_ref[0:1, OUTER] * scale_ref[...])) * (
            slope_ref[...] - total[0:1] - norm_ref[...] * total[1:2]
        )
        lead_out[...] = grad[:, :B0]
        low = grad[:, B0:].astype(bf16)
        dz = low[:, BP:]
        dz_out[...] = dz
        project_out[...] = box_mean(low[:, :BP].astype(f32), frames5, rows5, width5)
        fill_shifted(shifted, dz.astype(f32), frames5, rows5, width5)
        upper = back_chunk(shifted, flat, 0, frames5, rows5)
        stem = slice(B0 + BP, FIRST)
        norm = (first_ref[:, stem] - stat_ref[0:1, stem]) * stat_ref[1:2, stem]
        active = norm * affine_ref[0:1, STEM] + affine_ref[1:2, STEM]
        slopes = slope(active, upper * mask)
        slope_out[...] = slopes
        sums_out[...] = sums(slopes, norm)

    dz5, lead5_grad, project5_grad, stem5_slope, stem5_sums = call(
        back5_body,
        [
            ((cells5, SECOND), bf16),
            ((cells5, B0), f32),
            ((cells5, BP), f32),
            ((cells5, STEMS), f32),
            ((2, STEMS), f32),
        ],
        [affine5, wide5, thin5, outer5_norm, outer5_slope, outer5_scale, first5, first5_stat]
        + outer5_parts,
        numbers,
        [
            ((3, frames5 + 2, rows5 + 2, width5, 512), f32),
            ((STEMS, 27 * 512), bf16),
        ],
    )
    stem5_parts = group_parts(stem5_sums)

    def rest_slope(f, pooled_grad, matrix, mask, zp_ref, second_ref, affine_ref, stat_ref):
        norm, active = rest_of(
            zp_ref, second_ref, f * span, affine_ref, stat_ref[0:1], stat_ref[1:2]
        )
        upper = dot(matrix, pooled_grad[f * span // 8 : (f + 1) * span // 8])
        return norm, slope(active, upper * mask)

    def first5_body(row_ref, group_ref, affine_ref, affine4_ref, p_ref, *refs):
        lead_ref, project_ref, slope_ref, first_ref, stat_ref = refs[:5]
        zp_ref, second_ref, rest_stat = refs[5:8]
        parts, refs = refs[8 : 8 + n_parts], refs[8 + n_parts :]
        lead_out, projected_out, rest_out, sums_out = refs
        height, across, inverse = crop(row_ref, group_ref, 2)
        mask = mask_of(cells5, rows5, width5, height, across)
        total = total_of(parts) * inverse
        stem = slice(B0 + BP, FIRST)
        norm = (first_ref[:, stem] - stat_ref[0:1, stem]) * stat_ref[1:2, stem]
        stem_grad = (mask * (affine_ref[0:1, STEM] * stat_ref[1:2, stem])) * (
            slope_ref[...] - total[0:1] - norm * total[1:2]
        )
        projected = jnp.concatenate([lead_ref[...], project_ref[...], stem_grad], axis=1)
        projected = projected.astype(bf16)
        projected_out[...] = projected
        pooled_grad = dot(projected, p_ref[...]).astype(bf16)
        lead_out[...] = pooled_grad[:, :B0].astype(f32).reshape(frames5, rows5, width5, B0)
        rest_grad = pooled_grad[:, B0:]
        rest_out[...] = rest_grad
        height, across, _ = crop(row_ref, group_ref)
        mask = mask_of(span, full_rows, width, height, across)
        matrix = pool_matrix(2, full_rows, width, True)
        total = jnp.zeros((2, REST), f32)
        for f in range(frames5):
            norm, slopes = rest_slope(
                f, rest_grad, matrix, mask, zp_ref, second_ref, affine4_ref, rest_stat
            )
            total = total + sums(slopes, norm)
        sums_out[...] = total

    lead_grad5, projected5_grad, rest_upper, rest_grad_sums = call(
        first5_body,
        [
            ((frames5, rows5, width5, B0), f32),
            ((cells5, FIRST), bf16),
            ((cells5, REST), bf16),
            ((2, REST), f32),
        ],
        [affine5, affine4, proj5, lead5_grad, project5_grad, stem5_slope, first5, first5_stat]
        + [zp, second, rest_stat]
        + stem5_parts,
        numbers,
        us=2.4,
    )
    rest_grad_parts = group_parts(rest_grad_sums)

    def natural(outer, stem):
        pool, thin, wide = (
            outer[:, B0 : B0 + BP],
            outer[:, B0 + BP : B0 + BP + B2],
            outer[:, B0 + BP + B2 :],
        )
        return jnp.concatenate([outer[:, :B0], stem, pool, wide, thin], axis=1)

    rows_5b = padded_rows(CONV_ROWS + matrix_rows(FIRST, C_MID) + 16)

    def weights5_body(row_ref, beside, dz_ref, pooled_ref, projected_ref, *refs):
        outer_ref, stem_ref, mine, other, slab = refs
        scale = jnp.full((1, 1), row_ref[COUNTED], i32).astype(f32)
        pack_conv(slab, beside, dz_ref[...], frames5, rows5, width5, scale)
        at = pack_matrix(slab, CONV_ROWS, dot_tn(projected_ref[...], pooled_ref[...]) * scale)
        norms = natural(outer_ref[...], stem_ref[...]) * scale
        pack_norms(slab, at, norms[1:2], norms[0:1])
        slab[at + 16 :] = jnp.zeros((rows_5b - at - 16, 128), bf16)
        give_halves(slab, row_ref[SEG], mine, other)

    mine5, other5 = call(
        weights5_body,
        [((rows_5b // 2, 128), bf16)] * 2,
        [beside5, dz5, pooled, projected5_grad, outer5_sums, stem5_sums],
        [row],
        [((rows_5b, 128), bf16)],
        us=3.6,
    )
    slab5 = (CrossSlab if dps == 4 else Slab)(mine5, other5, row)

    slab5.to_dp()
    def back4_body(row_ref, group_ref, affine_ref, zp_ref, second_ref, stat_ref, grad_ref, *refs):
        parts, (out5_ref, lead_ref), refs = refs[:n_parts], refs[n_parts : n_parts + 2], refs[n_parts + 2 :]
        outs, (dz_out, kept) = refs[: len(outward.rounds)], refs[len(outward.rounds) :]
        height, across, inverse = crop(row_ref, group_ref)
        mask = mask_of(span, full_rows, width, height, across)
        total = total_of(parts) * inverse
        matrix = pool_matrix(2, full_rows, width, True)
        factor = affine_ref[0:1, RESTS] * stat_ref[1:2]
        for f in range(frames5):
            norm, slopes = rest_slope(
                f, grad_ref, matrix, mask, zp_ref, second_ref, affine_ref, stat_ref
            )
            grad = (mask * factor) * (slopes - total[0:1] - norm * total[1:2])
            low = grad.astype(bf16)
            dz_out[f * span : (f + 1) * span] = low[:, BP:]
            kept[2 * f : 2 * f + 2] = low[:, :BP].astype(f32).reshape(2, full_rows, width, BP)
        pool = box_mean(kept[...].reshape(cells, BP), frames, full_rows, width)
        kept[...] = pool.reshape(frames, full_rows, width, BP)
        for turn, out in enumerate(outs):
            part = kept[:, pl.ds(row_ref[OUT_BLOCK + turn] * rows, rows)]
            out[:part_cells] = part.reshape(part_cells, BP).astype(bf16)
            start = row_ref[OUT_BLOCK + turn] * band_rows5
            part = lead_ref[:, pl.ds(start, band_rows5)].reshape(part_cells5, B0)
            at = pack_lanes(out, part_cells, part)
            part = out5_ref[:, pl.ds(start, band_rows5)].reshape(part_cells5, C_MID)
            pack_lanes(out, at, part)

    carried_out = carried + B0 // 128 * part_cells5
    got = call(
        back4_body,
        [((carried_out, 128), bf16)] * len(outward.rounds) + [((cells, SECOND), bf16)],
        [affine4, zp, second, rest_stat, rest_upper] + rest_grad_parts + [out5, lead_grad5],
        numbers,
        [((frames, full_rows, width, BP), f32)],
        us=2.6,
    )
    carried_grads = outward.send(got[: len(outward.rounds)])
    dz = got[-1]

    rows_conv = padded_rows(CONV_ROWS)

    def weights4_body(row_ref, beside, dz_ref, mine, other, slab):
        scale = jnp.full((1, 1), row_ref[COUNTED], i32).astype(f32)
        pack_conv(slab, beside, dz_ref[...], frames, full_rows, width, scale)
        slab[CONV_ROWS:] = jnp.zeros((rows_conv - CONV_ROWS, 128), bf16)
        give_halves(slab, row_ref[SEG], mine, other)

    mine4, other4 = call(
        weights4_body,
        [((rows_conv // 2, 128), bf16)] * 2,
        [beside, dz],
        [row],
        [((rows_conv, 128), bf16)],
        us=10.5,
    )
    slab4 = (CrossSlab if dps == 4 else Slab)(mine4, other4, row)

    slab5.to_dp_again()
    def stems4_body(row_ref, group_ref, affine_ref, wide_ref, thin_ref, dz_ref, norm_ref, *refs):
        outs, refs = refs[: len(outward.rounds)], refs[len(outward.rounds) :]
        sums_out, shifted, flat, kept = refs
        height, across, _ = crop(row_ref, group_ref)
        fill_back_weights(flat, wide_ref, thin_ref)
        fill_shifted(shifted, dz_ref[...].astype(f32), frames, full_rows, width)
        chunk = step * full_rows * width
        mask = mask_of(chunk, full_rows, width, height, across)
        total = jnp.zeros((2, STEMS), f32)
        for start in range(0, frames, step):
            upper = back_chunk(shifted, flat, start, step, full_rows)
            at = start * full_rows * width
            norm = norm_ref[at : at + chunk]
            active = norm * affine_ref[0:1, STEM] + affine_ref[1:2, STEM]
            slopes = slope(active, upper * mask)
            kept[start : start + step] = slopes.reshape(step, full_rows, width, STEMS)
            total = total + sums(slopes, norm)
        sums_out[...] = total
        for turn, out in enumerate(outs):
            part = kept[:, pl.ds(row_ref[OUT_BLOCK + turn] * rows, rows)]
            out[...] = part.reshape(part_cells, STEMS).astype(bf16)

    got = call(
        stems4_body,
        [((part_cells, STEMS), bf16)] * len(outward.rounds)
        + [((2, STEMS), f32)],
        [affine4, wide4, thin4, dz, stem_norm],
        numbers,
        [
            ((3, frames + 2, full_rows + 2, width, 512), bf16),
            ((STEMS, 27 * 512), bf16),
            ((frames, full_rows, width, STEMS), f32),
        ],
        us=9.0,
    )
    stem_slopes = outward.send(got[: len(outward.rounds)])
    stem_sums = got[-1]

    def lead_slopes(i, row_ref, group_ref, lead_ref, stat_ref, affine_ref, matrix, kept):
        _, mask, inverse = home_crop(row_ref, group_ref, i)
        norm, scale, active = lead_act(i, lead_ref, stat_ref, affine_ref, inverse)
        upper = dot(matrix, kept[i])
        return mask, inverse, scale, norm, slope(active, upper * mask)

    def lead_back_body(row_ref, group_ref, lead_ref, stat_ref, affine_ref, stem_ref, *refs):
        blocks, (sums_out, kept, out) = refs[:held], refs[held:]
        matrix = pool_matrix(frames, rows, width, True)
        for turn, ref in enumerate(blocks):
            place = row_ref[OUT_SLOT + turn]
            at = part_cells + B0 // 128 * part_cells5
            part = unpacked_lanes(ref, part_cells, part_cells5, B0)
            kept[place] = part.astype(bf16)
            part = unpacked_lanes(ref, at, part_cells5, C_MID)
            out[place] = part.reshape(frames5, band_rows5, width5, C_MID).astype(bf16)
        for i in range(held):
            _, _, _, norm, slopes = lead_slopes(
                i, row_ref, group_ref, lead_ref, stat_ref, affine_ref, matrix, kept
            )
            total = sums(slopes, norm)
            j = 1 + i // clips
            sums_out[j] = total if i % clips == 0 else sums_out[j] + total
        sums_out[0] = widened(stem_ref[...])

    last_sums, lead_upper, block_out = call(
        lead_back_body,
        [
            ((1 + halves, 2, PADDED), f32),
            ((held, part_cells5, B0), bf16),
            ((held, frames5, band_rows5, width5, C_MID), bf16),
        ],
        [lead, lead_stat, affine4, stem_sums] + carried_grads,
        numbers,
        us=2.0,
    )
    block_out = block_out.reshape(halves, clips, frames5, band_rows5, width5, C_MID)

    slab4.to_dp()
    last = summed_dp(last_sums)
    if each > 1:
        pairs = [[z * each + k for k in range(each)] for z in range(micro)]
        last = jnp.concatenate(
            [lax.psum(last[:1], "space", axis_index_groups=pairs), last[1:]], axis=0
        )

    def last_body(own, other, stat, out):
        total = own[0]
        if spread > 1:
            total = total + other[0]
        out[0] = total
        out[1 : 1 + halves] = own[1:]
        out[1 + halves] = widened(stat[...])

    (last,) = call(
        last_body,
        [((2 + halves, 2, PADDED), f32)],
        [last, swapped(last), stem_total],
        us=0.8,
    )
    last_parts = copies(last, "space")

    slab5.to_space()
    slab4.to_dp_again()
    rows_proj = padded_rows(matrix_rows(channels, FIRST) + 16)

    def first4_body(row_ref, group_ref, x_ref, affine_ref, lead_ref, stat_ref, *refs):
        upper_ref, stem_ref, last_sums, rest_sums = refs[:4]
        parts, refs = refs[4 : 4 + bands], refs[4 + bands :]
        slopes_in, pools_in, refs = refs[:held], refs[held : 2 * held], refs[2 * held :]
        projected, mine, other, x_all, slab, late, stem_all = refs
        lead_total = functools.reduce(
            jnp.add, [ref[1 : 1 + halves] for ref in parts]
        )
        matrix = pool_matrix(frames, rows, width, True)
        for turn in range(held):
            place = row_ref[OUT_SLOT + turn]
            late[place, :, :BP] = pools_in[turn][:part_cells].astype(f32)
            late[place, :, BP:] = slopes_in[turn][...].astype(f32)
        for k in range(bands):
            stem_all[k, 0] = parts[k][0]
            stem_all[k, 1] = parts[k][1 + halves]
        for i in range(held):
            mask, inverse, scale, norm, slopes = lead_slopes(
                i, row_ref, group_ref, lead_ref, stat_ref, affine_ref, matrix, upper_ref
            )
            total = lead_total[i // clips] * inverse
            lead_grad = (affine_ref[0:1, LEAD] * scale) * (
                slopes - total[0:1] - norm * total[1:2]
            )
            m = row_ref[SEG] * halves + i // clips
            turn = row_ref[BAND] ^ (m * each)
            mean, scale = moments(stem_all[turn, 1][:, :STEMS], inverse)
            total = stem_all[turn, 0][:, :STEMS] * inverse
            norm = (stem_ref[i] - mean) * scale
            stem_grad = (affine_ref[0:1, STEM] * scale) * (
                late[i, :, BP:] - total[0:1] - norm * total[1:2]
            )
            grad = jnp.concatenate([lead_grad, late[i, :, :BP], stem_grad], axis=1) * mask
            at = i * part_cells
            projected[at : at + part_cells] = grad.astype(bf16)
            x_all[at : at + part_cells] = x_ref[m, i % clips].reshape(part_cells, channels)
        at = pack_matrix(slab, 0, dot_tn(x_all[...], projected[...]))
        counted = jnp.full((1, 1), row_ref[COUNTED], i32).astype(f32)
        own = jnp.sum(last_sums[1:], axis=0)
        rest = rest_sums[...] * counted
        stem = last_sums[0][:, :STEMS] * counted
        norms = natural(jnp.concatenate([own, rest], axis=1), stem)
        pack_norms(slab, at, norms[1:2], norms[0:1])
        slab[at + 16 :] = jnp.zeros((rows_proj - at - 16, 128), bf16)
        give_halves(slab, row_ref[SEG], mine, other)

    projected_grad, mine_proj, other_proj = call(
        first4_body,
        [((held * part_cells, FIRST), bf16)] + [((rows_proj // 2, 128), bf16)] * 2,
        [inputs, affine4, lead, lead_stat, lead_upper, home_stem, last_sums, rest_grad_sums]
        + last_parts
        + stem_slopes
        + carried_grads,
        numbers,
        [
            ((held * part_cells, channels), bf16),
            ((rows_proj, 128), bf16),
            ((held, part_cells, BP + STEMS), f32),
            ((bands, 2, 2, PADDED), f32),
        ],
        us=4.0,
    )
    slab_proj = Slab(mine_proj, other_proj, row)
    joint = JointSlab(slab4, slab_proj, row) if dps == 4 else None

    slab4.to_space()
    slab5.summed()
    def input_body(projected_ref, p_ref, out):
        for i in range(held):
            at = i * part_cells
            got = dot_nt(projected_ref[at : at + part_cells], p_ref[...])
            out[i // clips, i % clips] = got.reshape(frames, rows, width, channels)

    (input_grad,) = call(
        input_body,
        [((halves, clips, frames, rows, width, channels), f32)],
        [projected_grad, proj4],
    )

    slab_proj.to_dp()
    slab5.back_dp()
    slab_proj.to_space()
    if joint is None:
        slab4.summed()
    else:
        slab4.to_shard()
    if joint is None:
        slab_proj.summed()
    else:
        joint.summed()
    slab5.back_dp_again()
    if joint is None:
        slab4.back_dp()
        slab_proj.back_dp()
    else:
        joint.back_dp()
    if joint is not None:
        joint.back_dp_again()
    def unpacked(way, n_rows, body, outs, us):
        pieces = way.parts

        def whole(row_ref, *refs):
            slab = refs[-1]
            way.place(slab, refs[: len(pieces)], row_ref)
            body(slab, *refs[len(pieces) : -1])

        scratch = [((n_rows, 128), bf16)]
        return call(whole, outs, pieces, [row], scratch, us=us, limit=48)

    conv_outs = [((27, B1R, B1), f32), ((27, B2R, B2), f32)]

    def unpack_proj(slab, proj_out, norm_out):
        parts, at = unpack_matrix(slab, 0, channels, FIRST)
        proj_out[:, :128] = parts[0]
        proj_out[:, 128:256] = parts[1]
        proj_out[:, 256:] = jnp.concatenate([parts[3], parts[4], parts[2]], axis=1)
        norm_out[...] = slab[at : at + 16].astype(f32)

    def unpack5(slab, wide_out, thin_out, proj5_out, norm5_out):
        unpack_conv(slab, wide_out, thin_out)
        parts, at = unpack_matrix(slab, CONV_ROWS, FIRST, C_MID)
        lead = parts[:2]
        tail = jnp.concatenate([parts[6], parts[3], parts[2]], axis=1)
        for first, last, place in ((0, B0, 0), (B0, B0 + BP, STEM_END), (B0 + BP, FIRST, B0)):
            to = slice(place, place + last - first)
            proj5_out[to, 0:128] = lead[0][first:last]
            proj5_out[to, 128:256] = lead[1][first:last]
            proj5_out[to, 256:384] = parts[4][first:last]
            proj5_out[to, 384:512] = parts[5][first:last]
            proj5_out[to, 512:] = tail[first:last]
        norm5_out[...] = slab[at : at + 16].astype(f32)


    wide5_grad, thin5_grad, proj5_grad, norms5 = unpacked(
        slab5,
        rows_5b,
        unpack5,
        conv_outs + [((FIRST, C_MID), f32), ((16, 128), f32)],
        5.0,
    )

    proj_outs = [((channels, FIRST), f32), ((16, 128), f32)]
    if joint is not None:
        wide4_grad, thin4_grad, proj4_grad, norms4 = unpacked(
            joint,
            rows_conv + rows_proj,
            lambda slab, *outs: (
                unpack_conv(slab, *outs[:2]),
                unpack_proj(slab.at[rows_conv:], *outs[2:]),
            ),
            conv_outs + proj_outs,
            5.5,
        )
    else:
        wide4_grad, thin4_grad = unpacked(slab4, rows_conv, unpack_conv, conv_outs, 4.0)
        proj4_grad, norms4 = unpacked(slab_proj, rows_proj, unpack_proj, proj_outs, 2.0)


    return (
        block_out,
        input_grad,
        proj4_grad,
        wide4_grad.reshape(conv_a_4f.shape),
        thin4_grad.reshape(conv_b_4f.shape),
        norms4[:8].reshape(-1),
        norms4[8:].reshape(-1),
        proj5_grad.T,
        wide5_grad.reshape(conv_a_5b.shape),
        thin5_grad.reshape(conv_b_5b.shape),
        norms5[:8].reshape(-1),
        norms5[8:].reshape(-1),
    )


def solution(mesh):
    banded = P(None, "dp", None, "space", None, None)
    halved_specs = P("segment", "dp", None, "space", None, None)
    in_specs = (banded,) + (P(),) * 11 + (banded,)
    out_specs = (halved_specs, halved_specs) + (P(),) * 10
    return jax.shard_map(shards, mesh=mesh, in_specs=in_specs, out_specs=out_specs, check_vma=False)
```

```python
import functools

import jax
import jax.numpy as jnp
from jax import lax
from jax.experimental import pallas as pl
from jax.experimental.pallas import tpu as pltpu
from jax.sharding import PartitionSpec as P

B0 = 256
B1R = 160
B2R = 32
B1 = 320
B2 = 128
BP = 128
FIRST = 576
STEMS = B1R + B2R
STEM_END = B0 + STEMS
SECOND = B1 + B2
REST = SECOND + BP
C_MID = B0 + REST
BESIDE = 640
GRANULE = 16
SCALE = 3.0
PADDED = 256

SEG, DP, BAND, FIRST_CLIP, MY_MICRO, COUNTED, TABLES = range(7)

epsilon = 0.001
bf16 = jnp.bfloat16
f32 = jnp.float32
i32 = jnp.int32


def matching(edges):
    by_sender = {}
    for edge in edges:
        by_sender.setdefault(edge[0], []).append(edge)
    taken = {}

    def place(sender, seen):
        for edge in by_sender[sender]:
            receiver = edge[1]
            if receiver in seen:
                continue
            seen.add(receiver)
            if receiver not in taken or place(taken[receiver][0], seen):
                taken[receiver] = edge
                return True
        return False

    for sender in sorted(by_sender):
        place(sender, set())
    return sorted(taken.values())


class Route:
    def __init__(self, edges, devices):
        left, self.rounds = list(edges), []
        while left:
            chosen = matching(left)
            for edge in chosen:
                left.remove(edge)
            self.rounds.append(chosen)
        self.blocks = [[0] * len(self.rounds) for _ in range(devices)]
        self.slots = [[0] * len(self.rounds) for _ in range(devices)]
        for turn, chosen in enumerate(self.rounds):
            for sender, receiver, block, slot in chosen:
                self.blocks[sender][turn] = block
                self.slots[receiver][turn] = slot

    def send(self, parts):
        got = []
        for part, chosen in zip(parts, self.rounds):
            if all(edge[0] == edge[1] for edge in chosen):
                got.append(part)
            else:
                pairs = [(edge[0], edge[1]) for edge in chosen]
                got.append(lax.ppermute(part, ("segment", "space"), pairs))
        return got


def pairing(peers, step):
    return [(i, i ^ step) for i in range(peers)]


def exchanged(parts, axis):
    peers = lax.axis_size(axis)
    assert peers & (peers - 1) == 0
    return [parts[0]] + [lax.ppermute(parts[k], axis, pairing(peers, k)) for k in range(1, peers)]


def copies(x, axis):
    return exchanged([x] * lax.axis_size(axis), axis)


def sum_over(x, axis):
    if lax.axis_size(axis) > 4:
        return lax.psum(x, axis)
    got = copies(x, axis)
    return functools.reduce(jnp.add, got)


class Order:
    def __init__(self):
        self.last = []


order = Order()


def call(body, outs, ins, numbers=(), scratch=(), us=2.0, limit=40):
    vmem = pl.BlockSpec(memory_space=pltpu.VMEM)
    smem = pl.BlockSpec(memory_space=pltpu.SMEM)
    skipped, after = len(numbers) + len(ins), order.last

    def waited(*refs):
        body(*refs[:skipped], *refs[skipped + len(after) :])

    got = pl.pallas_call(
        waited,
        out_shape=[jax.ShapeDtypeStruct(shape, dtype) for shape, dtype in outs],
        in_specs=[smem] * len(numbers)
        + [vmem] * len(ins)
        + [pl.BlockSpec(memory_space=pl.ANY)] * len(after),
        out_specs=[vmem] * len(outs),
        scratch_shapes=[pltpu.VMEM(shape, dtype) for shape, dtype in scratch],
        cost_estimate=pl.CostEstimate(
            flops=int(us * SCALE * 1.1e9), bytes_accessed=10**6, transcendentals=0
        ),
        compiler_params=pltpu.CompilerParams(vmem_limit_bytes=limit * 2**20),
    )(*numbers, *ins, *after)
    order.last = [got[-1]]
    return got


def dot(a, b):
    return jnp.dot(a, b, preferred_element_type=f32)


def dot_nt(a, b):
    return lax.dot_general(a, b, (((1,), (1,)), ((), ())), preferred_element_type=f32)


def dot_tn(a, b):
    return lax.dot_general(a, b, (((0,), (0,)), ((), ())), preferred_element_type=f32)


def mask_of(cells, rows, width, height, across, first_row=0):
    place = lax.broadcasted_iota(i32, (cells, 1), 0)
    column = lax.rem(place, width)
    row = lax.rem(lax.div(place, width), rows) + first_row
    return jnp.where((row < height) & (column < across), 1.0, 0.0).astype(f32)


def pool_matrix(frames, rows, width, up):
    cells, pooled = frames * rows * width, frames * rows * width // 8
    shape = (cells, pooled) if up else (pooled, cells)
    place = lax.broadcasted_iota(i32, shape, 0 if up else 1)
    target = lax.broadcasted_iota(i32, shape, 1 if up else 0)
    column = lax.rem(place, width) // 2
    row = lax.rem(lax.div(place, width), rows) // 2
    frame = lax.div(place, width * rows) // 2
    home = (frame * (rows // 2) + row) * (width // 2) + column
    return jnp.where(home == target, 0.125, 0.0).astype(bf16)


def moments(totals, inverse):
    mean = totals[0:1] * inverse
    variance = totals[1:2] * inverse - mean * mean
    return mean, lax.rsqrt(variance + epsilon)


def column_shift(x, width, by):
    cells = x.shape[0]
    column = lax.rem(lax.broadcasted_iota(i32, (cells, 1), 0), width)
    edge = 0 if by == 1 else width - 1
    return jnp.where(column == edge, 0.0, pltpu.roll(x, by % cells, 0))


def silu(active):
    return active * jax.nn.sigmoid(active)


def slope(active, upstream):
    sig = jax.nn.sigmoid(active)
    return upstream * sig * (1.0 + active * (1.0 - sig))


def sums(a, b):
    return jnp.concatenate(
        [jnp.sum(a, axis=0, keepdims=True), jnp.sum(a * b, axis=0, keepdims=True)], axis=0
    )


def box_mean(x, frames, rows, width):
    cells, channels = x.shape
    x = x + column_shift(x, width, 1) + column_shift(x, width, -1)
    x = x.reshape(frames, rows, width, channels)
    edge = jnp.zeros((frames, 1, width, channels), f32)
    x = (
        x
        + jnp.concatenate([edge, x[:, : rows - 1]], axis=1)
        + jnp.concatenate([x[:, 1:], edge], axis=1)
    )
    edge = jnp.zeros((1, rows, width, channels), f32)
    x = (
        x
        + jnp.concatenate([edge, x[: frames - 1]], axis=0)
        + jnp.concatenate([x[1:], edge], axis=0)
    )
    return x.reshape(cells, channels) * (1.0 / 27.0)


def place_bands(dst, blocks, slots, frames, rows, width):
    for turn, block in enumerate(blocks):
        part = block[...].astype(dst.dtype).reshape(frames, rows, width, dst.shape[-1])
        dst[:, pl.ds(slots[turn] * rows, rows)] = part


def fill_beside(beside, stems, frames, rows, width):
    beside[...] = jnp.zeros_like(beside)
    three = jnp.concatenate(
        [column_shift(stems, width, 1), stems, column_shift(stems, width, -1)], axis=1
    )
    three = three.astype(beside.dtype).reshape(frames, rows, width, 3 * STEMS)
    beside[1 : frames + 1, 1 : rows + 1, :, : 3 * STEMS] = three


def fill_conv_weights(flat, wide, thin):
    flat[...] = jnp.zeros_like(flat)
    for tap in range(27):
        row = (tap // 3) * BESIDE + (tap % 3) * STEMS
        flat[row : row + B1R, B2:] = wide[tap]
        flat[row + B1R : row + STEMS, :B2] = thin[tap]


def fill_back_weights(flat, wide, thin):
    flat[...] = jnp.zeros_like(flat)
    for tap in range(27):
        start = tap * 512
        flat[:B1R, start + B2 : start + SECOND] = wide[26 - tap]
        flat[B1R:, start : start + B2] = thin[26 - tap]


def fill_shifted(shifted, grad, frames, rows, width):
    shifted[...] = jnp.zeros_like(shifted)
    for dc in range(3):
        moved = grad if dc == 1 else column_shift(grad, width, 1 - dc)
        moved = moved.astype(shifted.dtype).reshape(frames, rows, width, SECOND)
        shifted[dc, 1 : frames + 1, 1 : rows + 1, :, :SECOND] = moved


def window(padded, f, r, frames, rows):
    part = padded[f : f + frames, r : r + rows]
    return part.reshape(frames * rows * part.shape[2], part.shape[3]).astype(bf16)


def conv_chunk(beside, flat, start, step, rows):
    taps = [window(beside, start + f, r, step, rows) for f in range(3) for r in range(3)]
    return dot(jnp.concatenate(taps, axis=1), flat[...])


def back_chunk(shifted, flat, start, step, rows):
    taps = [
        window(shifted.at[dc], start + f, r, step, rows)
        for f in range(3)
        for r in range(3)
        for dc in range(3)
    ]
    return dot_nt(jnp.concatenate(taps, axis=1), flat[...])


def pack_conv(slab, beside, dz, frames, rows, width, scale):
    cells = frames * rows * width
    half = 27 * B1R // 2
    for f in range(3):
        for r in range(3):
            part = window(beside, f, r, frames, rows)
            both = dot_tn(part, dz) * scale
            thin, wide = both[:, :B2], both[:, B2:]
            for c in range(3):
                tap = (f * 3 + r) * 3 + c
                rows_wide = wide[c * STEMS : c * STEMS + B1R].astype(bf16)
                slab[tap * B1R : (tap + 1) * B1R] = rows_wide[:, :128]
                at = 27 * B1R + tap * B1R
                slab[at : at + B1R] = rows_wide[:, 128:256]
                for piece in range(2):
                    row = tap * B1R + piece * 80
                    side = row >= half
                    at = 2 * 27 * B1R + row - (half if side else 0)
                    lanes = slice(64, 128) if side else slice(0, 64)
                    slab[at : at + 80, lanes] = rows_wide[piece * 80 : piece * 80 + 80, 256:]
                at = 2 * 27 * B1R + half + tap * B2R
                slab[at : at + B2R] = thin[c * STEMS + B1R : (c + 1) * STEMS].astype(bf16)


CONV_ROWS = 2 * 27 * B1R + 27 * B1R // 2 + 27 * B2R


def halved(n):
    return -(-n // (2 * GRANULE)) * GRANULE


def pack_matrix(slab, at, matrix):
    n, lanes = matrix.shape
    blocks, half = lanes // 128, halved(n)
    matrix = matrix.astype(bf16)
    for j in range(blocks):
        slab[at + j * n : at + (j + 1) * n] = matrix[:, j * 128 : (j + 1) * 128]
    at = at + blocks * n
    left, right = matrix[:half, blocks * 128 :], matrix[half:, blocks * 128 :]
    if n < 2 * half:
        right = jnp.concatenate([right, jnp.zeros((2 * half - n, 64), bf16)], axis=0)
    slab[at : at + half] = jnp.concatenate([left, right], axis=1)
    return at + half


def pack_norms(slab, at, gain, bias):
    rows = [row[:, j * 128 : (j + 1) * 128] for row in (gain, bias) for j in range(8)]
    slab[at : at + 16] = jnp.concatenate(rows, axis=0).astype(bf16)


def give_halves(slab, seg, mine, other):
    half = mine.shape[0]
    mine[...] = slab[pl.ds(seg * half, half)]
    other[...] = slab[pl.ds((1 - seg) * half, half)]


def unpack_conv(slab, wide_out, thin_out):
    half = 27 * B1R // 2
    for tap in range(27):
        at = tap * B1R
        wide_out[tap, :, :128] = slab[at : at + B1R].astype(f32)
        wide_out[tap, :, 128:256] = slab[27 * B1R + at : 27 * B1R + at + B1R].astype(f32)
        for piece in range(2):
            row = at + piece * 80
            side = row >= half
            start = 2 * 27 * B1R + row - (half if side else 0)
            part = slab[start : start + 80].astype(f32)
            part = part[:, 64:] if side else part[:, :64]
            wide_out[tap, piece * 80 : piece * 80 + 80, 256:] = part
        at = 2 * 27 * B1R + half + tap * B2R
        thin_out[tap] = slab[at : at + B2R].astype(f32)


def unpack_matrix(slab, at, n, lanes):
    blocks, half = lanes // 128, halved(n)
    parts = [slab[at + j * n : at + (j + 1) * n].astype(f32) for j in range(blocks)]
    at = at + blocks * n
    tail = slab[at : at + half].astype(f32)
    parts.append(jnp.concatenate([tail[:, :64], tail[: n - half, 64:]], axis=0))
    return parts, at + half


def matrix_rows(n, lanes):
    return lanes // 128 * n + halved(n)


def padded_rows(rows):
    unit = GRANULE * lax.axis_size("segment") * lax.axis_size("dp") * lax.axis_size("space")
    return -(-rows // unit) * unit


def split_sum(parts, pieces, row, at):
    rows = parts[0].shape[0] // pieces

    def body(row_ref, *refs):
        ins, outs = refs[: len(parts)], refs[len(parts) :]
        for k, out in enumerate(outs):
            start = (row_ref[at] ^ k) * rows if pieces > 1 else 0
            if pieces > 1:
                start = pl.multiple_of(start, GRANULE)
            total = ins[0][pl.ds(start, rows)].astype(f32)
            for ref in ins[1:]:
                total = total + ref[pl.ds(start, rows)].astype(f32)
            out[...] = total.astype(bf16)

    outs = [((rows, 128), bf16)] * pieces
    return call(body, outs, parts, [row], us=1.0, limit=32)


def joined(parts, row, at):
    rows, pieces = parts[0].shape[0], len(parts)

    def body(row_ref, *refs):
        for k, ref in enumerate(refs[:-1]):
            start = (row_ref[at] ^ k) * rows
            refs[-1][pl.ds(pl.multiple_of(start, GRANULE), rows)] = ref[...]

    outs = [((rows * pieces, 128), bf16)]
    return call(body, outs, parts, [row], us=1.0, limit=32)[0]


def swapped(x):
    return lax.ppermute(x, "segment", [(0, 1), (1, 0)])


class Slab:
    def __init__(self, mine, other, row):
        self.row, self.parts = row, [mine, swapped(other)]

    def to_dp(self):
        self.parts = exchanged(split_sum(self.parts, lax.axis_size("dp"), self.row, DP), "dp")

    def to_dp_again(self):
        pass

    def to_space(self):
        bands = lax.axis_size("space")
        self.parts = exchanged(split_sum(self.parts, bands, self.row, BAND), "space")

    def summed(self):
        self.parts = copies(split_sum(self.parts, 1, self.row, BAND)[0], "space")

    def to_shard(self):
        self.shard = split_sum(self.parts, 1, self.row, BAND)[0]

    def back_dp(self):
        held = copies(joined(self.parts, self.row, BAND), "dp")
        self.parts = held + [swapped(part) for part in held]

    def back_dp_again(self):
        pass

    def place(self, slab, pieces, row_ref):
        rows, peers = pieces[0].shape[0], len(pieces) // 2
        for k, piece in enumerate(pieces):
            side = row_ref[SEG] if k < peers else 1 - row_ref[SEG]
            at = (side * peers + (row_ref[DP] ^ (k % peers))) * rows
            slab[pl.ds(pl.multiple_of(at, GRANULE), rows)] = piece[...]


class CrossSlab(Slab):
    def to_dp(self):
        mine, got = self.parts
        self.quarter = mine.shape[0] // 4
        half, quarter = self.quarter // 2, self.quarter

        def body(row_ref, mine_ref, got_ref, to_x, to_y, keep_a, keep_b):
            y, x = lax.div(row_ref[DP], 2), lax.rem(row_ref[DP], 2)
            for k in range(2):
                to = slice(k * half, (k + 1) * half)
                for out, start in (
                    (to_x, (k * 2 + (1 - x)) * quarter),
                    (keep_a, (k * 2 + x) * quarter),
                    (to_y, ((1 - y) * 2 + k) * quarter + half),
                    (keep_b, (y * 2 + k) * quarter + half),
                ):
                    at = pl.ds(pl.multiple_of(start, GRANULE), half)
                    total = mine_ref[at].astype(f32) + got_ref[at].astype(f32)
                    out[to] = total.astype(out.dtype)

        send, keep = ((2 * half, 128), bf16), ((2 * half, 128), f32)
        to_x, to_y, *self.kept = call(
            body, [send, send, keep, keep], [mine, got], [self.row], us=1.3, limit=32
        )
        self.got = [lax.ppermute(to_x, "dp", pairing(4, 1)), lax.ppermute(to_y, "dp", pairing(4, 2))]

    def to_dp_again(self):
        half = self.quarter // 2

        def body(row_ref, keep_a, keep_b, got_a, got_b, send_a, send_b, next_a, next_b):
            y, x = lax.div(row_ref[DP], 2), lax.rem(row_ref[DP], 2)
            for keep, got, send, own, place in (
                (keep_a, got_a, send_a, next_a, y),
                (keep_b, got_b, send_b, next_b, x),
            ):
                at = pl.ds(pl.multiple_of(place * half, GRANULE), half)
                own[...] = keep[at] + got[at].astype(f32)
                at = pl.ds(pl.multiple_of((1 - place) * half, GRANULE), half)
                send[...] = (keep[at] + got[at].astype(f32)).astype(bf16)

        send, keep = ((half, 128), bf16), ((half, 128), f32)
        to_y, to_x, *self.kept = call(
            body, [send, send, keep, keep], self.kept + self.got, [self.row], us=1.0, limit=32
        )
        self.got = [lax.ppermute(to_y, "dp", pairing(4, 2)), lax.ppermute(to_x, "dp", pairing(4, 1))]

    def to_space(self):
        half, bands = self.quarter // 2, lax.axis_size("space")
        rows = self.quarter // bands

        def body(row_ref, keep_a, keep_b, got_a, got_b, own, *refs):
            outs, whole = refs[:-1], refs[-1]
            whole[:half] = keep_a[...] + got_a[...].astype(f32)
            whole[half:] = keep_b[...] + got_b[...].astype(f32)
            for k, out in enumerate((own,) + outs):
                at = pl.ds(pl.multiple_of((row_ref[BAND] ^ k) * rows, GRANULE), rows)
                out[...] = whole[at].astype(out.dtype)

        outs = [((rows, 128), f32)] + [((rows, 128), bf16)] * (bands - 1)
        scratch = [((self.quarter, 128), f32)]
        parts = call(body, outs, self.kept + self.got, [self.row], scratch, us=1.0, limit=32)
        self.parts = exchanged(parts, "space")

    def back_dp(self):
        half, bands = self.quarter // 2, lax.axis_size("space")
        rows = self.quarter // bands

        def body(row_ref, *refs):
            parts, (out_a, out_b, whole) = refs[:bands], refs[bands:]
            for k, ref in enumerate(parts):
                at = pl.ds(pl.multiple_of((row_ref[BAND] ^ k) * rows, GRANULE), rows)
                whole[at] = ref[...]
            out_a[...] = whole[:half]
            out_b[...] = whole[half:]

        outs, scratch = [((half, 128), bf16)] * 2, [((self.quarter, 128), bf16)]
        a, b = call(body, outs, self.parts, [self.row], scratch, us=1.0, limit=32)
        self.got = [lax.ppermute(a, "dp", pairing(4, 2)), lax.ppermute(b, "dp", pairing(4, 1))]
        self.kept = [a, b]

    def back_dp_again(self):
        half = self.quarter // 2

        def body(row_ref, own_a, own_b, got_a, got_b, pair_a, pair_b, both):
            y, x = lax.div(row_ref[DP], 2), lax.rem(row_ref[DP], 2)
            for own, got, out, place in ((own_a, got_a, pair_a, y), (own_b, got_b, pair_b, x)):
                out[pl.ds(pl.multiple_of(place * half, GRANULE), half)] = own[...]
                out[pl.ds(pl.multiple_of((1 - place) * half, GRANULE), half)] = got[...]
            both[: 2 * half] = pair_a[...]
            both[2 * half :] = pair_b[...]

        outs = [((2 * half, 128), bf16)] * 2 + [((4 * half, 128), bf16)]
        a, b, both = call(body, outs, self.kept + self.got, [self.row], us=1.0, limit=32)
        got = [lax.ppermute(a, "dp", pairing(4, 1)), lax.ppermute(b, "dp", pairing(4, 2))]
        self.parts = [both] + got + [swapped(part) for part in [both] + got]

    def place(self, slab, pieces, row_ref):
        half, quarter = self.quarter // 2, self.quarter
        y, x = lax.div(row_ref[DP], 2), lax.rem(row_ref[DP], 2)
        for turn, side in enumerate((row_ref[SEG], 1 - row_ref[SEG])):
            both, far_a, far_b = pieces[3 * turn : 3 * turn + 3]
            a, b = both.at[: 2 * half], both.at[2 * half :]
            for k in range(2):
                part = slice(k * half, (k + 1) * half)
                for ref, start in (
                    (a, (k * 2 + x) * quarter),
                    (far_a, (k * 2 + (1 - x)) * quarter),
                    (b, (y * 2 + k) * quarter + half),
                    (far_b, ((1 - y) * 2 + k) * quarter + half),
                ):
                    at = pl.multiple_of(side * 4 * quarter + start, GRANULE)
                    slab[pl.ds(at, half)] = ref[part]


class JointSlab(CrossSlab):
    def __init__(self, first, second, row):
        self.first, self.second, self.row = first, second, row

    def summed(self):
        shard, parts, bands = self.first.shard, self.second.parts, lax.axis_size("space")
        self.sizes = [shard.shape[0], parts[0].shape[0]]
        unit = sum(self.sizes)

        def body(first, *refs):
            refs[-1][: self.sizes[0]] = first[...]
            total = functools.reduce(jnp.add, [ref[...].astype(f32) for ref in refs[:-1]])
            refs[-1][self.sizes[0] :] = total.astype(bf16)

        (joint,) = call(body, [((unit, 128), bf16)], [shard] + parts, us=1.0, limit=32)
        self.quarter = unit * bands
        self.parts = copies(joint, "space")

    def place(self, slab, pieces, row_ref):
        bands, unit = lax.axis_size("space"), sum(self.sizes)
        half = self.quarter // 2
        y, x = lax.div(row_ref[DP], 2), lax.rem(row_ref[DP], 2)
        for turn, side in enumerate((row_ref[SEG], 1 - row_ref[SEG])):
            both, far_a, far_b = pieces[3 * turn : 3 * turn + 3]
            for k in range(2):
                for ref, at, quarter, second in (
                    (both, k * half, k * 2 + x, 0),
                    (far_a, k * half, k * 2 + (1 - x), 0),
                    (both, (2 + k) * half, y * 2 + k, 1),
                    (far_b, k * half, (1 - y) * 2 + k, 1),
                ):
                    for band in range(bands // 2):
                        base, start = 0, at + band * unit
                        for size in self.sizes:
                            place = (side * 4 + quarter) * bands + second * (bands // 2) + band
                            to = pl.multiple_of(base + place * size, GRANULE)
                            slab[pl.ds(to, size)] = ref[start : start + size]
                            base, start = base + 8 * bands * size, start + size


def widened(x):
    more = PADDED - x.shape[1]
    return jnp.concatenate([x, jnp.zeros((2, more), f32)], axis=1) if more else x


def pack_lanes(out, at, x):
    cells, channels = x.shape
    for start in range(0, channels, 128):
        part = x[:, start : start + 128]
        if part.shape[1] < 128:
            part = jnp.concatenate([part, jnp.zeros((cells, 128 - part.shape[1]), f32)], axis=1)
        out[at : at + cells] = part.astype(bf16)
        at += cells
    return at


def unpacked_lanes(ref, at, cells, channels):
    parts = []
    for start in range(0, channels, 128):
        parts.append(ref[at : at + cells, : min(128, channels - start)].astype(f32))
        at += cells
    return jnp.concatenate(parts, axis=1)


def shards(
    inputs,
    crop_group,
    in_proj_4f,
    conv_a_4f,
    conv_b_4f,
    gain_4f,
    bias_4f,
    in_proj_5b,
    conv_a_5b,
    conv_b_5b,
    gain_5b,
    bias_5b,
    out_grad,
):
    order.last = []
    segs, dps, bands = (lax.axis_size(axis) for axis in ("segment", "dp", "space"))
    micro, clips, frames, rows, width, channels = inputs.shape
    full_rows, all_clips = rows * bands, clips * dps
    halves = micro // segs
    held = halves * clips
    items = micro * clips
    spread = segs if items == segs * bands else 1
    assert segs == 2 and items == spread * bands and clips % spread == 0
    each = clips // spread
    cells, part_cells = frames * full_rows * width, frames * rows * width
    frames5, rows5, width5 = frames // 2, full_rows // 2, width // 2
    cells5, part_cells5 = cells // 8, part_cells // 8
    band_rows5 = rows // 2

    inward, pooled_in, outward = [], [], []
    for s in range(segs):
        for z in range(bands):
            for item in range(bands):
                inward.append((s * bands + z, s * bands + item, item, z))
    for m in range(micro):
        for c in range(clips):
            if spread > 1:
                holders = [(c // each) * bands + m * each + c % each]
            else:
                holders = [s * bands + m * clips + c for s in range(segs)]
            home, local = m // halves, (m % halves) * clips + c
            for z in range(bands):
                for holder in holders:
                    pooled_in.append((home * bands + z, holder, local, z))
                outward.append((holders[z % len(holders)], home * bands + z, z, local))
    inward, pooled_in, outward = (
        Route(edges, segs * bands) for edges in (inward, pooled_in, outward)
    )
    IN_BLOCK = TABLES
    IN_SLOT = IN_BLOCK + len(inward.rounds)
    POOLED_BLOCK = IN_SLOT + len(inward.rounds)
    POOLED_SLOT = POOLED_BLOCK + len(pooled_in.rounds)
    OUT_BLOCK = POOLED_SLOT + len(pooled_in.rounds)
    OUT_SLOT = OUT_BLOCK + len(outward.rounds)
    table = []
    for s in range(segs):
        for d in range(dps):
            for z in range(bands):
                me = s * bands + z
                first = s * each if spread > 1 else 0
                counted = 1 if spread > 1 or s == 0 else 0
                line = [s, d, z, first, z // each, counted]
                for route in (inward, pooled_in, outward):
                    line = line + route.blocks[me] + route.slots[me]
                table.append(line)
    row = jnp.array(table, i32)[lax.axis_index(("segment", "dp", "space"))]
    numbers = [row, crop_group]

    def group_parts(x):
        if each > 1:
            pairs = [[z * each + k for k in range(each)] for z in range(micro)]
            x = lax.psum(x, "space", axis_index_groups=pairs)
        if spread > 1:
            x = x + swapped(x)
        if dps > 4:
            return [lax.psum(x, "dp")]
        return copies(x, "dp")

    def total_of(refs):
        return functools.reduce(jnp.add, [ref[...] for ref in refs])

    def crop(row_ref, group_ref, scale=1, m=None):
        group = group_ref[row_ref[MY_MICRO] if m is None else m]
        tall, wide = full_rows // scale, width // scale
        height, across = tall - group * (tall // 4), wide - group * (wide // 4)
        count = all_clips * (frames // scale) * height * across
        return height, across, 1.0 / jnp.full((1, 1), count, i32).astype(f32)

    LEAD, OUTER, STEM = slice(0, B0), slice(0, C_MID), slice(C_MID, None)
    RESTS = slice(B0, C_MID)
    wide4, thin4 = conv_a_4f.reshape(27, B1R, B1), conv_b_4f.reshape(27, B2R, B2)
    wide5, thin5 = conv_a_5b.reshape(27, B1R, B1), conv_b_5b.reshape(27, B2R, B2)

    def project_body(row_ref, group_ref, x_ref, p_ref, stat, pool, *outs):
        for k in range(bands):
            item = row_ref[IN_BLOCK + k]
            m, c = lax.div(item, each), row_ref[FIRST_CLIP] + lax.rem(item, each)
            x = x_ref[m, c].reshape(part_cells, channels)
            height, across, _ = crop(row_ref, group_ref, 1, m)
            mask = mask_of(part_cells, rows, width, height, across, row_ref[BAND] * rows)
            z = dot(x, p_ref[:, B0:]) * mask
            stem = z[:, :STEMS]
            outs[k][...] = stem.astype(bf16)
            pool[k] = z[:, STEMS:].astype(bf16)
            stat[item] = sums(stem, stem)

    got = call(
        project_body,
        [((bands, 2, STEMS), f32), ((bands, part_cells, BP), bf16)]
        + [((part_cells, STEMS), bf16)] * bands,
        [inputs, in_proj_4f],
        numbers,
        us=1.5,
    )
    stem_stat, pool_parts, stem_parts = got[0], got[1], got[2:]
    stem_blocks = inward.send(stem_parts)

    def home_crop(row_ref, group_ref, i):
        m = row_ref[SEG] * halves + i // clips
        height, across, inverse = crop(row_ref, group_ref, 1, m)
        first = row_ref[BAND] * rows
        return m, mask_of(part_cells, rows, width, height, across, first), inverse

    lanes5 = -(-C_MID // 128)
    carried = part_cells + lanes5 * part_cells5

    def lead_body(row_ref, group_ref, x_ref, p_ref, stem_stat, pool, upper, *refs):
        lead_out, stem_out, stat, outs = refs[0], refs[1], refs[2], refs[3:]
        for i in range(held):
            m, mask, _ = home_crop(row_ref, group_ref, i)
            x = x_ref[m, i % clips].reshape(part_cells, channels)
            z = dot(x, p_ref[:, :STEM_END]) * mask
            lead = z[:, :B0]
            lead_out[i] = lead
            stem_out[i] = z[:, B0:]
            total = sums(lead, lead)
            j = bands + i // clips
            stat[j] = total if i % clips == 0 else stat[j] + total
        for k in range(bands):
            stat[k] = widened(stem_stat[k])
            item = row_ref[IN_BLOCK + k]
            m, c = lax.div(item, each), row_ref[FIRST_CLIP] + lax.rem(item, each)
            outs[k][:part_cells] = pool[k]
            pack_lanes(outs[k], part_cells, upper[m, c].astype(f32).reshape(part_cells5, C_MID))

    got = call(
        lead_body,
        [
            ((held, part_cells, B0), f32),
            ((held, part_cells, STEMS), f32),
            ((bands + halves, 2, PADDED), f32),
        ]
        + [((carried, 128), bf16)] * bands,
        [inputs, in_proj_4f, stem_stat, pool_parts, out_grad],
        numbers,
        us=2.5,
    )
    lead, home_stem, stat = got[:3]

    def all_parts(x, axis):
        return [lax.psum(x, axis)] if lax.axis_size(axis) > 4 else copies(x, axis)

    def whole_body(*refs):
        refs[-1][...] = total_of(refs[:-1])

    def summed_dp(x):
        parts = all_parts(x, "dp")
        return call(whole_body, [(x.shape, f32)], parts, us=0.8)[0]

    def share_body(row_ref, own, other, *outs):
        for k, out in enumerate(outs):
            item = row_ref[BAND] ^ k
            first = lax.div(item, each) * each
            total = jnp.zeros((2, PADDED), f32)
            for c in range(each):
                total = total + own[first + c]
                if spread > 1:
                    total = total + other[first + c]
            out[0] = total
            for j in range(halves):
                out[1 + j] = own[bands + j]

    stat = summed_dp(stat)
    stat_parts = call(
        share_body,
        [((1 + halves, 2, PADDED), f32)] * bands,
        [stat, swapped(stat)],
        [row],
        us=0.8,
    )
    stat_parts = exchanged(stat_parts, "space")
    carried_blocks = inward.send(got[3:])

    def arrange_body(gain4, bias4, gain5, bias5, p4, p5, affine4, affine5, proj4, proj5):
        for gain, bias, out in ((gain4, bias4, affine4), (gain5, bias5, affine5)):
            for k, ref in enumerate((gain, bias)):
                v = ref[...]
                out[k : k + 1] = jnp.concatenate(
                    [
                        v[:, :B0],
                        v[:, STEM_END:FIRST],
                        v[:, FIRST + B1 :],
                        v[:, FIRST : FIRST + B1],
                        v[:, B0:STEM_END],
                    ],
                    axis=1,
                )
        proj4[:, :B0] = p4[:, :B0]
        proj4[:, B0:] = jnp.concatenate([p4[:, STEM_END:], p4[:, B0:STEM_END]], axis=1)
        for first, last, to in ((0, B0, 0), (STEM_END, FIRST, B0), (B0, STEM_END, B0 + BP)):
            rows_in = p5[first:last]
            proj5[to : to + last - first, :B0] = rows_in[:, :B0]
            proj5[to : to + last - first, B0:] = jnp.concatenate(
                [
                    rows_in[:, B0 + SECOND :],
                    rows_in[:, B0 + B1 : B0 + SECOND],
                    rows_in[:, B0 : B0 + B1],
                ],
                axis=1,
            )

    affine4, affine5, proj4, proj5 = call(
        arrange_body,
        [((2, 1024), f32)] * 2 + [((channels, FIRST), bf16), ((FIRST, C_MID), bf16)],
        [v.reshape(1, -1) for v in (gain_4f, bias_4f, gain_5b, bias_5b)]
        + [in_proj_4f, in_proj_5b.T],
        us=2.0,
    )

    def lead_act(i, lead_ref, stat_ref, affine_ref, inverse):
        mean, scale = moments(stat_ref[i // clips], inverse)
        norm = (lead_ref[i] - mean) * scale
        return norm, scale, norm * affine_ref[0:1, LEAD] + affine_ref[1:2, LEAD]

    def lead_out_body(row_ref, group_ref, lead_ref, affine_ref, *refs):
        parts, stat_ref, outs, kept = refs[:bands], refs[bands], refs[bands + 1 : -1], refs[-1]
        stat_ref[...] = total_of(parts)[1:]
        matrix = pool_matrix(frames, rows, width, False)
        for i in range(held):
            _, mask, inverse = home_crop(row_ref, group_ref, i)
            _, _, active = lead_act(i, lead_ref, stat_ref, affine_ref, inverse)
            kept[i] = dot(matrix, (silu(active) * mask).astype(bf16)).astype(bf16)
        for turn, out in enumerate(outs):
            out[...] = kept[row_ref[POOLED_BLOCK + turn]]

    got = call(
        lead_out_body,
        [((halves, 2, B0), f32)] + [((part_cells5, B0), bf16)] * len(pooled_in.rounds),
        [lead, affine4] + stat_parts,
        numbers,
        [((held, part_cells5, B0), bf16)],
        us=1.8,
    )
    lead_stat = got[0]
    lead_pooled = pooled_in.send(got[1:])

    step = 2 if full_rows * width <= 128 else 1

    def conv_body(row_ref, group_ref, affine_ref, wide_ref, thin_ref, *refs):
        stats, blocks = refs[:bands], refs[bands : 2 * bands]
        second_out, sums_out, norm_out, stat_out, beside, stage, flat = refs[2 * bands :]
        height, across, inverse = crop(row_ref, group_ref)
        totals = functools.reduce(jnp.add, [ref[0] for ref in stats])[:, :STEMS]
        mean, scale = moments(totals, inverse)
        stat_out[...] = totals
        fill_conv_weights(flat, wide_ref, thin_ref)
        slots = [row_ref[IN_SLOT + k] for k in range(bands)]
        place_bands(stage, blocks, slots, frames, rows, width)
        mask = mask_of(cells, full_rows, width, height, across)
        norm = (stage[...].reshape(cells, STEMS) - mean) * scale
        norm_out[...] = norm
        active = norm * affine_ref[0:1, STEM] + affine_ref[1:2, STEM]
        fill_beside(beside, silu(active) * mask, frames, full_rows, width)
        chunk = step * full_rows * width
        total = jnp.zeros((2, SECOND), f32)
        for start in range(0, frames, step):
            got = conv_chunk(beside, flat, start, step, full_rows)
            second_out[start * full_rows * width : start * full_rows * width + chunk] = got
            total = total + sums(got * mask[:chunk], got)
        sums_out[...] = total

    second, second_sums, stem_norm, stem_total, beside = call(
        conv_body,
        [
            ((cells, SECOND), f32),
            ((2, SECOND), f32),
            ((cells, STEMS), f32),
            ((2, STEMS), f32),
            ((frames + 2, full_rows + 2, width, BESIDE), bf16),
        ],
        [affine4, wide4, thin4] + stat_parts + stem_blocks,
        numbers,
        [
            ((frames, full_rows, width, STEMS), f32),
            ((9 * BESIDE, SECOND), bf16),
        ],
        us=9.0,
    )

    def pool_body(row_ref, group_ref, second_sums, *refs):
        blocks, (zp_out, sums_out, stage) = refs[:bands], refs[bands:]
        height, across, _ = crop(row_ref, group_ref)
        slots = [row_ref[IN_SLOT + k] for k in range(bands)]
        place_bands(stage, [ref.at[:part_cells] for ref in blocks], slots, frames, rows, width)
        zp = box_mean(stage[...].reshape(cells, BP), frames, full_rows, width)
        zp_out[...] = zp
        mask = mask_of(cells, full_rows, width, height, across)
        sums_out[...] = jnp.concatenate([sums(zp * mask, zp), second_sums[...]], axis=1)

    zp, rest_sums = call(
        pool_body,
        [((cells, BP), f32), ((2, REST), f32)],
        [second_sums] + carried_blocks,
        numbers,
        [((frames, full_rows, width, BP), f32)],
        us=1.3,
    )
    rest_parts = group_parts(rest_sums)
    n_parts = len(rest_parts)

    span = 2 * full_rows * width

    def rest_of(zp_ref, second_ref, start, affine_ref, mean, scale):
        z = jnp.concatenate(
            [zp_ref[start : start + span], second_ref[start : start + span]], axis=1
        )
        norm = (z - mean) * scale
        return norm, norm * affine_ref[0:1, RESTS] + affine_ref[1:2, RESTS]

    def middle_body(row_ref, group_ref, affine_ref, p_ref, zp_ref, second_ref, *refs):
        parts, leads = refs[:n_parts], refs[n_parts:-6]
        stat_out, pooled, first_out, sums_out, stage, kept = refs[-6:]
        height, across, inverse = crop(row_ref, group_ref)
        mean, scale = moments(total_of(parts), inverse)
        stat_out[...] = jnp.concatenate([mean, scale], axis=0)
        mask = mask_of(span, full_rows, width, height, across)
        matrix = pool_matrix(2, full_rows, width, False)
        slots = [row_ref[POOLED_SLOT + k] for k in range(len(leads))]
        place_bands(stage, leads, slots, frames5, band_rows5, width5)
        pooled[:, :B0] = stage[...].reshape(cells5, B0).astype(bf16)
        for f in range(frames5):
            _, active = rest_of(zp_ref, second_ref, f * span, affine_ref, mean, scale)
            out = dot(matrix, (silu(active) * mask).astype(bf16))
            pooled[f * span // 8 : (f + 1) * span // 8, B0:] = out.astype(bf16)
        z = dot_nt(pooled[...], p_ref[...])
        kept[...] = z
        project = z[:, LEAD.stop : LEAD.stop + BP].astype(bf16).astype(f32)
        kept[:, B0 : B0 + BP] = box_mean(project, frames5, rows5, width5)
        z = kept[...]
        first_out[...] = z
        height, across, _ = crop(row_ref, group_ref, 2)
        sums_out[...] = sums(z * mask_of(cells5, rows5, width5, height, across), z)

    rest_stat, pooled, first5, first5_sums = call(
        middle_body,
        [((2, REST), f32), ((cells5, C_MID), bf16), ((cells5, FIRST), f32), ((2, FIRST), f32)],
        [affine4, proj5, zp, second] + rest_parts + lead_pooled,
        numbers,
        [((frames5, rows5, width5, B0), f32), ((cells5, FIRST), f32)],
    )
    first5_parts = group_parts(first5_sums)

    def conv5_body(row_ref, group_ref, affine_ref, wide_ref, thin_ref, first_ref, *refs):
        parts = refs[:n_parts]
        second_out, sums_out, stat_out, beside, flat = refs[n_parts:]
        height, across, inverse = crop(row_ref, group_ref, 2)
        mean, scale = moments(total_of(parts), inverse)
        stat_out[...] = jnp.concatenate([mean, scale], axis=0)
        fill_conv_weights(flat, wide_ref, thin_ref)
        mask = mask_of(cells5, rows5, width5, height, across)
        stem = slice(B0 + BP, FIRST)
        norm = (first_ref[:, stem] - mean[:, stem]) * scale[:, stem]
        active = norm * affine_ref[0:1, STEM] + affine_ref[1:2, STEM]
        fill_beside(beside, silu(active) * mask, frames5, rows5, width5)
        got = conv_chunk(beside, flat, 0, frames5, rows5)
        second_out[...] = got
        sums_out[...] = sums(got * mask, got)

    second5, second5_sums, first5_stat, beside5 = call(
        conv5_body,
        [
            ((cells5, SECOND), f32),
            ((2, SECOND), f32),
            ((2, FIRST), f32),
            ((frames5 + 2, rows5 + 2, width5, BESIDE), f32),
        ],
        [affine5, wide5, thin5, first5] + first5_parts,
        numbers,
        [((9 * BESIDE, SECOND), bf16)],
    )
    second5_parts = group_parts(second5_sums)

    def out5_body(row_ref, group_ref, affine_ref, first_ref, stat_ref, second_ref, *refs):
        parts, uppers = refs[:n_parts], refs[n_parts : n_parts + bands]
        out, norm_out, slope_out, scale_out, sums_out, stage = refs[n_parts + bands :]
        height, across, inverse = crop(row_ref, group_ref, 2)
        mean2, scale2 = moments(total_of(parts), inverse)
        mask = mask_of(cells5, rows5, width5, height, across)
        outer = slice(0, B0 + BP)
        mean = jnp.concatenate([stat_ref[0:1, outer], mean2], axis=1)
        scale = jnp.concatenate([stat_ref[1:2, outer], scale2], axis=1)
        z = jnp.concatenate([first_ref[:, outer], second_ref[...]], axis=1)
        norm = (z - mean) * scale
        active = norm * affine_ref[0:1, OUTER] + affine_ref[1:2, OUTER]
        act = silu(active) * mask
        natural = [act[:, :B0], act[:, B0 + BP + B2 :], act[:, B0 + BP : B0 + BP + B2]]
        natural = jnp.concatenate(natural + [act[:, B0 : B0 + BP]], axis=1)
        out[...] = natural.reshape(frames5, rows5, width5, C_MID)
        for k, ref in enumerate(uppers):
            part = unpacked_lanes(ref, part_cells, part_cells5, C_MID)
            part = part.reshape(frames5, band_rows5, width5, C_MID)
            stage[:, pl.ds(row_ref[IN_SLOT + k] * band_rows5, band_rows5)] = part
        upper = stage[...].reshape(cells5, C_MID)
        upper = jnp.concatenate(
            [
                upper[:, :B0],
                upper[:, B0 + SECOND :],
                upper[:, B0 + B1 : B0 + SECOND],
                upper[:, B0 : B0 + B1],
            ],
            axis=1,
        )
        slopes = slope(active, upper * mask)
        norm_out[...] = norm
        slope_out[...] = slopes
        scale_out[...] = scale
        sums_out[...] = sums(slopes, norm)

    out5, outer5_norm, outer5_slope, outer5_scale, outer5_sums = call(
        out5_body,
        [
            ((frames5, rows5, width5, C_MID), f32),
            ((cells5, C_MID), f32),
            ((cells5, C_MID), f32),
            ((1, C_MID), f32),
            ((2, C_MID), f32),
        ],
        [affine5, first5, first5_stat, second5] + second5_parts + carried_blocks,
        numbers,
        [((frames5, rows5, width5, C_MID), f32)],
        us=1.4,
    )
    outer5_parts = group_parts(outer5_sums)

    def back5_body(row_ref, group_ref, affine_ref, wide_ref, thin_ref, *refs):
        norm_ref, slope_ref, scale_ref, first_ref, stat_ref = refs[:5]
        parts, refs = refs[5 : 5 + n_parts], refs[5 + n_parts :]
        dz_out, lead_out, project_out, slope_out, sums_out, shifted, flat = refs
        height, across, inverse = crop(row_ref, group_ref, 2)
        mask = mask_of(cells5, rows5, width5, height, across)
        fill_back_weights(flat, wide_ref, thin_ref)
        total = total_of(parts) * inverse
        grad = (mask * (affine_ref[0:1, OUTER] * scale_ref[...])) * (
            slope_ref[...] - total[0:1] - norm_ref[...] * total[1:2]
        )
        lead_out[...] = grad[:, :B0]
        low = grad[:, B0:].astype(bf16)
        dz = low[:, BP:]
        dz_out[...] = dz
        project_out[...] = box_mean(low[:, :BP].astype(f32), frames5, rows5, width5)
        fill_shifted(shifted, dz.astype(f32), frames5, rows5, width5)
        upper = back_chunk(shifted, flat, 0, frames5, rows5)
        stem = slice(B0 + BP, FIRST)
        norm = (first_ref[:, stem] - stat_ref[0:1, stem]) * stat_ref[1:2, stem]
        active = norm * affine_ref[0:1, STEM] + affine_ref[1:2, STEM]
        slopes = slope(active, upper * mask)
        slope_out[...] = slopes
        sums_out[...] = sums(slopes, norm)

    dz5, lead5_grad, project5_grad, stem5_slope, stem5_sums = call(
        back5_body,
        [
            ((cells5, SECOND), bf16),
            ((cells5, B0), f32),
            ((cells5, BP), f32),
            ((cells5, STEMS), f32),
            ((2, STEMS), f32),
        ],
        [affine5, wide5, thin5, outer5_norm, outer5_slope, outer5_scale, first5, first5_stat]
        + outer5_parts,
        numbers,
        [
            ((3, frames5 + 2, rows5 + 2, width5, 512), f32),
            ((STEMS, 27 * 512), bf16),
        ],
    )
    stem5_parts = group_parts(stem5_sums)

    def rest_slope(f, pooled_grad, matrix, mask, zp_ref, second_ref, affine_ref, stat_ref):
        norm, active = rest_of(
            zp_ref, second_ref, f * span, affine_ref, stat_ref[0:1], stat_ref[1:2]
        )
        upper = dot(matrix, pooled_grad[f * span // 8 : (f + 1) * span // 8])
        return norm, slope(active, upper * mask)

    def first5_body(row_ref, group_ref, affine_ref, affine4_ref, p_ref, *refs):
        lead_ref, project_ref, slope_ref, first_ref, stat_ref = refs[:5]
        zp_ref, second_ref, rest_stat = refs[5:8]
        parts, refs = refs[8 : 8 + n_parts], refs[8 + n_parts :]
        lead_out, projected_out, rest_out, sums_out = refs
        height, across, inverse = crop(row_ref, group_ref, 2)
        mask = mask_of(cells5, rows5, width5, height, across)
        total = total_of(parts) * inverse
        stem = slice(B0 + BP, FIRST)
        norm = (first_ref[:, stem] - stat_ref[0:1, stem]) * stat_ref[1:2, stem]
        stem_grad = (mask * (affine_ref[0:1, STEM] * stat_ref[1:2, stem])) * (
            slope_ref[...] - total[0:1] - norm * total[1:2]
        )
        projected = jnp.concatenate([lead_ref[...], project_ref[...], stem_grad], axis=1)
        projected = projected.astype(bf16)
        projected_out[...] = projected
        pooled_grad = dot(projected, p_ref[...]).astype(bf16)
        lead_out[...] = pooled_grad[:, :B0].astype(f32).reshape(frames5, rows5, width5, B0)
        rest_grad = pooled_grad[:, B0:]
        rest_out[...] = rest_grad
        height, across, _ = crop(row_ref, group_ref)
        mask = mask_of(span, full_rows, width, height, across)
        matrix = pool_matrix(2, full_rows, width, True)
        total = jnp.zeros((2, REST), f32)
        for f in range(frames5):
            norm, slopes = rest_slope(
                f, rest_grad, matrix, mask, zp_ref, second_ref, affine4_ref, rest_stat
            )
            total = total + sums(slopes, norm)
        sums_out[...] = total

    lead_grad5, projected5_grad, rest_upper, rest_grad_sums = call(
        first5_body,
        [
            ((frames5, rows5, width5, B0), f32),
            ((cells5, FIRST), bf16),
            ((cells5, REST), bf16),
            ((2, REST), f32),
        ],
        [affine5, affine4, proj5, lead5_grad, project5_grad, stem5_slope, first5, first5_stat]
        + [zp, second, rest_stat]
        + stem5_parts,
        numbers,
        us=2.4,
    )
    rest_grad_parts = group_parts(rest_grad_sums)

    def natural(outer, stem):
        pool, thin, wide = (
            outer[:, B0 : B0 + BP],
            outer[:, B0 + BP : B0 + BP + B2],
            outer[:, B0 + BP + B2 :],
        )
        return jnp.concatenate([outer[:, :B0], stem, pool, wide, thin], axis=1)

    rows_5b = padded_rows(CONV_ROWS + matrix_rows(FIRST, C_MID) + 16)

    def weights5_body(row_ref, beside, dz_ref, pooled_ref, projected_ref, *refs):
        outer_ref, stem_ref, mine, other, slab = refs
        scale = jnp.full((1, 1), row_ref[COUNTED], i32).astype(f32)
        pack_conv(slab, beside, dz_ref[...], frames5, rows5, width5, scale)
        at = pack_matrix(slab, CONV_ROWS, dot_tn(projected_ref[...], pooled_ref[...]) * scale)
        norms = natural(outer_ref[...], stem_ref[...]) * scale
        pack_norms(slab, at, norms[1:2], norms[0:1])
        slab[at + 16 :] = jnp.zeros((rows_5b - at - 16, 128), bf16)
        give_halves(slab, row_ref[SEG], mine, other)

    mine5, other5 = call(
        weights5_body,
        [((rows_5b // 2, 128), bf16)] * 2,
        [beside5, dz5, pooled, projected5_grad, outer5_sums, stem5_sums],
        [row],
        [((rows_5b, 128), bf16)],
        us=3.6,
    )
    slab5 = (CrossSlab if dps == 4 else Slab)(mine5, other5, row)

    slab5.to_dp()
    def back4_body(row_ref, group_ref, affine_ref, zp_ref, second_ref, stat_ref, grad_ref, *refs):
        parts, (out5_ref, lead_ref), refs = refs[:n_parts], refs[n_parts : n_parts + 2], refs[n_parts + 2 :]
        outs, (dz_out, kept) = refs[: len(outward.rounds)], refs[len(outward.rounds) :]
        height, across, inverse = crop(row_ref, group_ref)
        mask = mask_of(span, full_rows, width, height, across)
        total = total_of(parts) * inverse
        matrix = pool_matrix(2, full_rows, width, True)
        factor = affine_ref[0:1, RESTS] * stat_ref[1:2]
        for f in range(frames5):
            norm, slopes = rest_slope(
                f, grad_ref, matrix, mask, zp_ref, second_ref, affine_ref, stat_ref
            )
            grad = (mask * factor) * (slopes - total[0:1] - norm * total[1:2])
            low = grad.astype(bf16)
            dz_out[f * span : (f + 1) * span] = low[:, BP:]
            kept[2 * f : 2 * f + 2] = low[:, :BP].astype(f32).reshape(2, full_rows, width, BP)
        pool = box_mean(kept[...].reshape(cells, BP), frames, full_rows, width)
        kept[...] = pool.reshape(frames, full_rows, width, BP)
        for turn, out in enumerate(outs):
            part = kept[:, pl.ds(row_ref[OUT_BLOCK + turn] * rows, rows)]
            out[:part_cells] = part.reshape(part_cells, BP).astype(bf16)
            start = row_ref[OUT_BLOCK + turn] * band_rows5
            part = lead_ref[:, pl.ds(start, band_rows5)].reshape(part_cells5, B0)
            at = pack_lanes(out, part_cells, part)
            part = out5_ref[:, pl.ds(start, band_rows5)].reshape(part_cells5, C_MID)
            pack_lanes(out, at, part)

    carried_out = carried + B0 // 128 * part_cells5
    got = call(
        back4_body,
        [((carried_out, 128), bf16)] * len(outward.rounds) + [((cells, SECOND), bf16)],
        [affine4, zp, second, rest_stat, rest_upper] + rest_grad_parts + [out5, lead_grad5],
        numbers,
        [((frames, full_rows, width, BP), f32)],
        us=2.6,
    )
    carried_grads = outward.send(got[: len(outward.rounds)])
    dz = got[-1]

    rows_conv = padded_rows(CONV_ROWS)

    def weights4_body(row_ref, beside, dz_ref, mine, other, slab):
        scale = jnp.full((1, 1), row_ref[COUNTED], i32).astype(f32)
        pack_conv(slab, beside, dz_ref[...], frames, full_rows, width, scale)
        slab[CONV_ROWS:] = jnp.zeros((rows_conv - CONV_ROWS, 128), bf16)
        give_halves(slab, row_ref[SEG], mine, other)

    mine4, other4 = call(
        weights4_body,
        [((rows_conv // 2, 128), bf16)] * 2,
        [beside, dz],
        [row],
        [((rows_conv, 128), bf16)],
        us=10.5,
    )
    slab4 = (CrossSlab if dps == 4 else Slab)(mine4, other4, row)

    slab5.to_dp_again()
    def stems4_body(row_ref, group_ref, affine_ref, wide_ref, thin_ref, dz_ref, norm_ref, *refs):
        outs, refs = refs[: len(outward.rounds)], refs[len(outward.rounds) :]
        sums_out, shifted, flat, kept = refs
        height, across, _ = crop(row_ref, group_ref)
        fill_back_weights(flat, wide_ref, thin_ref)
        fill_shifted(shifted, dz_ref[...].astype(f32), frames, full_rows, width)
        chunk = step * full_rows * width
        mask = mask_of(chunk, full_rows, width, height, across)
        total = jnp.zeros((2, STEMS), f32)
        for start in range(0, frames, step):
            upper = back_chunk(shifted, flat, start, step, full_rows)
            at = start * full_rows * width
            norm = norm_ref[at : at + chunk]
            active = norm * affine_ref[0:1, STEM] + affine_ref[1:2, STEM]
            slopes = slope(active, upper * mask)
            kept[start : start + step] = slopes.reshape(step, full_rows, width, STEMS)
            total = total + sums(slopes, norm)
        sums_out[...] = total
        for turn, out in enumerate(outs):
            part = kept[:, pl.ds(row_ref[OUT_BLOCK + turn] * rows, rows)]
            out[...] = part.reshape(part_cells, STEMS).astype(bf16)

    got = call(
        stems4_body,
        [((part_cells, STEMS), bf16)] * len(outward.rounds)
        + [((2, STEMS), f32)],
        [affine4, wide4, thin4, dz, stem_norm],
        numbers,
        [
            ((3, frames + 2, full_rows + 2, width, 512), bf16),
            ((STEMS, 27 * 512), bf16),
            ((frames, full_rows, width, STEMS), f32),
        ],
        us=9.0,
    )
    stem_slopes = outward.send(got[: len(outward.rounds)])
    stem_sums = got[-1]

    def lead_slopes(i, row_ref, group_ref, lead_ref, stat_ref, affine_ref, matrix, kept):
        _, mask, inverse = home_crop(row_ref, group_ref, i)
        norm, scale, active = lead_act(i, lead_ref, stat_ref, affine_ref, inverse)
        upper = dot(matrix, kept[i])
        return mask, inverse, scale, norm, slope(active, upper * mask)

    def lead_back_body(row_ref, group_ref, lead_ref, stat_ref, affine_ref, stem_ref, *refs):
        blocks, (sums_out, kept, out) = refs[:held], refs[held:]
        matrix = pool_matrix(frames, rows, width, True)
        for turn, ref in enumerate(blocks):
            place = row_ref[OUT_SLOT + turn]
            at = part_cells + B0 // 128 * part_cells5
            part = unpacked_lanes(ref, part_cells, part_cells5, B0)
            kept[place] = part.astype(bf16)
            part = unpacked_lanes(ref, at, part_cells5, C_MID)
            out[place] = part.reshape(frames5, band_rows5, width5, C_MID).astype(bf16)
        for i in range(held):
            _, _, _, norm, slopes = lead_slopes(
                i, row_ref, group_ref, lead_ref, stat_ref, affine_ref, matrix, kept
            )
            total = sums(slopes, norm)
            j = 1 + i // clips
            sums_out[j] = total if i % clips == 0 else sums_out[j] + total
        sums_out[0] = widened(stem_ref[...])

    last_sums, lead_upper, block_out = call(
        lead_back_body,
        [
            ((1 + halves, 2, PADDED), f32),
            ((held, part_cells5, B0), bf16),
            ((held, frames5, band_rows5, width5, C_MID), bf16),
        ],
        [lead, lead_stat, affine4, stem_sums] + carried_grads,
        numbers,
        us=2.0,
    )
    block_out = block_out.reshape(halves, clips, frames5, band_rows5, width5, C_MID)

    slab4.to_dp()
    last = summed_dp(last_sums)
    if each > 1:
        pairs = [[z * each + k for k in range(each)] for z in range(micro)]
        last = jnp.concatenate(
            [lax.psum(last[:1], "space", axis_index_groups=pairs), last[1:]], axis=0
        )

    def last_body(own, other, stat, out):
        total = own[0]
        if spread > 1:
            total = total + other[0]
        out[0] = total
        out[1 : 1 + halves] = own[1:]
        out[1 + halves] = widened(stat[...])

    (last,) = call(
        last_body,
        [((2 + halves, 2, PADDED), f32)],
        [last, swapped(last), stem_total],
        us=0.8,
    )
    last_parts = copies(last, "space")

    slab5.to_space()
    slab4.to_dp_again()
    rows_proj = padded_rows(matrix_rows(channels, FIRST) + 16)

    def first4_body(row_ref, group_ref, x_ref, affine_ref, lead_ref, stat_ref, *refs):
        upper_ref, stem_ref, last_sums, rest_sums = refs[:4]
        parts, refs = refs[4 : 4 + bands], refs[4 + bands :]
        slopes_in, pools_in, refs = refs[:held], refs[held : 2 * held], refs[2 * held :]
        projected, mine, other, x_all, slab, late, stem_all = refs
        lead_total = functools.reduce(
            jnp.add, [ref[1 : 1 + halves] for ref in parts]
        )
        matrix = pool_matrix(frames, rows, width, True)
        for turn in range(held):
            place = row_ref[OUT_SLOT + turn]
            late[place, :, :BP] = pools_in[turn][:part_cells].astype(f32)
            late[place, :, BP:] = slopes_in[turn][...].astype(f32)
        for k in range(bands):
            stem_all[k, 0] = parts[k][0]
            stem_all[k, 1] = parts[k][1 + halves]
        for i in range(held):
            mask, inverse, scale, norm, slopes = lead_slopes(
                i, row_ref, group_ref, lead_ref, stat_ref, affine_ref, matrix, upper_ref
            )
            total = lead_total[i // clips] * inverse
            lead_grad = (affine_ref[0:1, LEAD] * scale) * (
                slopes - total[0:1] - norm * total[1:2]
            )
            m = row_ref[SEG] * halves + i // clips
            turn = row_ref[BAND] ^ (m * each)
            mean, scale = moments(stem_all[turn, 1][:, :STEMS], inverse)
            total = stem_all[turn, 0][:, :STEMS] * inverse
            norm = (stem_ref[i] - mean) * scale
            stem_grad = (affine_ref[0:1, STEM] * scale) * (
                late[i, :, BP:] - total[0:1] - norm * total[1:2]
            )
            grad = jnp.concatenate([lead_grad, late[i, :, :BP], stem_grad], axis=1) * mask
            at = i * part_cells
            projected[at : at + part_cells] = grad.astype(bf16)
            x_all[at : at + part_cells] = x_ref[m, i % clips].reshape(part_cells, channels)
        at = pack_matrix(slab, 0, dot_tn(x_all[...], projected[...]))
        counted = jnp.full((1, 1), row_ref[COUNTED], i32).astype(f32)
        own = jnp.sum(last_sums[1:], axis=0)
        rest = rest_sums[...] * counted
        stem = last_sums[0][:, :STEMS] * counted
        norms = natural(jnp.concatenate([own, rest], axis=1), stem)
        pack_norms(slab, at, norms[1:2], norms[0:1])
        slab[at + 16 :] = jnp.zeros((rows_proj - at - 16, 128), bf16)
        give_halves(slab, row_ref[SEG], mine, other)

    projected_grad, mine_proj, other_proj = call(
        first4_body,
        [((held * part_cells, FIRST), bf16)] + [((rows_proj // 2, 128), bf16)] * 2,
        [inputs, affine4, lead, lead_stat, lead_upper, home_stem, last_sums, rest_grad_sums]
        + last_parts
        + stem_slopes
        + carried_grads,
        numbers,
        [
            ((held * part_cells, channels), bf16),
            ((rows_proj, 128), bf16),
            ((held, part_cells, BP + STEMS), f32),
            ((bands, 2, 2, PADDED), f32),
        ],
        us=4.0,
    )
    slab_proj = Slab(mine_proj, other_proj, row)
    joint = JointSlab(slab4, slab_proj, row) if dps == 4 else None

    slab4.to_space()
    slab5.summed()
    def input_body(projected_ref, p_ref, out):
        for i in range(held):
            at = i * part_cells
            got = dot_nt(projected_ref[at : at + part_cells], p_ref[...])
            out[i // clips, i % clips] = got.reshape(frames, rows, width, channels)

    (input_grad,) = call(
        input_body,
        [((halves, clips, frames, rows, width, channels), f32)],
        [projected_grad, proj4],
    )

    slab_proj.to_dp()
    slab5.back_dp()
    slab_proj.to_space()
    if joint is None:
        slab4.summed()
    else:
        slab4.to_shard()
    if joint is None:
        slab_proj.summed()
    else:
        joint.summed()
    slab5.back_dp_again()
    if joint is None:
        slab4.back_dp()
        slab_proj.back_dp()
    else:
        joint.back_dp()
    if joint is not None:
        joint.back_dp_again()
    def unpacked(way, n_rows, body, outs, us):
        pieces = way.parts

        def whole(row_ref, *refs):
            slab = refs[-1]
            way.place(slab, refs[: len(pieces)], row_ref)
            body(slab, *refs[len(pieces) : -1])

        scratch = [((n_rows, 128), bf16)]
        return call(whole, outs, pieces, [row], scratch, us=us, limit=48)

    conv_outs = [((27, B1R, B1), f32), ((27, B2R, B2), f32)]

    def unpack_proj(slab, proj_out, gain_out, bias_out):
        parts, at = unpack_matrix(slab, 0, channels, FIRST)
        proj_out[:, :128] = parts[0]
        proj_out[:, 128:256] = parts[1]
        proj_out[:, 256:] = jnp.concatenate([parts[3], parts[4], parts[2]], axis=1)
        norms = slab[at : at + 16].astype(f32)
        gain_out[...] = norms[:8]
        bias_out[...] = norms[8:]

    def unpack5(slab, wide_out, thin_out, proj5_out, gain_out, bias_out):
        unpack_conv(slab, wide_out, thin_out)
        parts, at = unpack_matrix(slab, CONV_ROWS, FIRST, C_MID)
        lead = parts[:2]
        tail = jnp.concatenate([parts[6], parts[3], parts[2]], axis=1)
        for first, last, place in ((0, B0, 0), (B0, B0 + BP, STEM_END), (B0 + BP, FIRST, B0)):
            to = slice(place, place + last - first)
            proj5_out[to, 0:128] = lead[0][first:last]
            proj5_out[to, 128:256] = lead[1][first:last]
            proj5_out[to, 256:384] = parts[4][first:last]
            proj5_out[to, 384:512] = parts[5][first:last]
            proj5_out[to, 512:] = tail[first:last]
        norms = slab[at : at + 16].astype(f32)
        gain_out[...] = norms[:8]
        bias_out[...] = norms[8:]


    wide5_grad, thin5_grad, proj5_grad, gain5_grad, bias5_grad = unpacked(
        slab5,
        rows_5b,
        unpack5,
        conv_outs + [((FIRST, C_MID), f32)] + [((8, 128), f32)] * 2,
        5.0,
    )

    proj_outs = [((channels, FIRST), f32)] + [((8, 128), f32)] * 2
    if joint is not None:
        wide4_grad, thin4_grad, proj4_grad, gain4_grad, bias4_grad = unpacked(
            joint,
            rows_conv + rows_proj,
            lambda slab, *outs: (
                unpack_conv(slab, *outs[:2]),
                unpack_proj(slab.at[rows_conv:], *outs[2:]),
            ),
            conv_outs + proj_outs,
            5.5,
        )
    else:
        wide4_grad, thin4_grad = unpacked(slab4, rows_conv, unpack_conv, conv_outs, 4.0)
        proj4_grad, gain4_grad, bias4_grad = unpacked(slab_proj, rows_proj, unpack_proj, proj_outs, 2.0)


    return (
        block_out,
        input_grad,
        proj4_grad,
        wide4_grad.reshape(conv_a_4f.shape),
        thin4_grad.reshape(conv_b_4f.shape),
        gain4_grad.reshape(-1),
        bias4_grad.reshape(-1),
        proj5_grad.T,
        wide5_grad.reshape(conv_a_5b.shape),
        thin5_grad.reshape(conv_b_5b.shape),
        gain5_grad.reshape(-1),
        bias5_grad.reshape(-1),
    )


def solution(mesh):
    banded = P(None, "dp", None, "space", None, None)
    halved_specs = P("segment", "dp", None, "space", None, None)
    in_specs = (banded,) + (P(),) * 11 + (banded,)
    out_specs = (halved_specs, halved_specs) + (P(),) * 10
    return jax.shard_map(shards, mesh=mesh, in_specs=in_specs, out_specs=out_specs, check_vma=False)
```

```python
import functools

import jax
import jax.numpy as jnp
from jax import lax
from jax.experimental import pallas as pl
from jax.experimental.pallas import tpu as pltpu
from jax.sharding import PartitionSpec as P

B0 = 256
B1R = 160
B2R = 32
B1 = 320
B2 = 128
BP = 128
FIRST = 576
STEMS = B1R + B2R
STEM_END = B0 + STEMS
SECOND = B1 + B2
REST = SECOND + BP
C_MID = B0 + REST
BESIDE = 640
GRANULE = 16
SCALE = 3.0
PADDED = 256

SEG, DP, BAND, FIRST_CLIP, MY_MICRO, COUNTED, TABLES = range(7)

epsilon = 0.001
bf16 = jnp.bfloat16
f32 = jnp.float32
i32 = jnp.int32


def matching(edges):
    by_sender = {}
    for edge in edges:
        by_sender.setdefault(edge[0], []).append(edge)
    taken = {}

    def place(sender, seen):
        for edge in by_sender[sender]:
            receiver = edge[1]
            if receiver in seen:
                continue
            seen.add(receiver)
            if receiver not in taken or place(taken[receiver][0], seen):
                taken[receiver] = edge
                return True
        return False

    for sender in sorted(by_sender):
        place(sender, set())
    return sorted(taken.values())


class Route:
    def __init__(self, edges, devices):
        left, self.rounds = list(edges), []
        while left:
            chosen = matching(left)
            for edge in chosen:
                left.remove(edge)
            self.rounds.append(chosen)
        self.blocks = [[0] * len(self.rounds) for _ in range(devices)]
        self.slots = [[0] * len(self.rounds) for _ in range(devices)]
        for turn, chosen in enumerate(self.rounds):
            for sender, receiver, block, slot in chosen:
                self.blocks[sender][turn] = block
                self.slots[receiver][turn] = slot

    def send(self, parts):
        got = []
        for part, chosen in zip(parts, self.rounds):
            if all(edge[0] == edge[1] for edge in chosen):
                got.append(part)
            else:
                pairs = [(edge[0], edge[1]) for edge in chosen]
                got.append(lax.ppermute(part, ("segment", "space"), pairs))
        return got


def pairing(peers, step):
    return [(i, i ^ step) for i in range(peers)]


def exchanged(parts, axis):
    peers = lax.axis_size(axis)
    assert peers & (peers - 1) == 0
    return [parts[0]] + [lax.ppermute(parts[k], axis, pairing(peers, k)) for k in range(1, peers)]


def copies(x, axis):
    return exchanged([x] * lax.axis_size(axis), axis)


def sum_over(x, axis):
    if lax.axis_size(axis) > 4:
        return lax.psum(x, axis)
    got = copies(x, axis)
    return functools.reduce(jnp.add, got)


class Order:
    def __init__(self):
        self.last = []


order = Order()


def call(body, outs, ins, numbers=(), scratch=(), us=2.0, limit=40):
    vmem = pl.BlockSpec(memory_space=pltpu.VMEM)
    smem = pl.BlockSpec(memory_space=pltpu.SMEM)
    skipped, after = len(numbers) + len(ins), order.last

    def waited(*refs):
        body(*refs[:skipped], *refs[skipped + len(after) :])

    got = pl.pallas_call(
        waited,
        out_shape=[jax.ShapeDtypeStruct(shape, dtype) for shape, dtype in outs],
        in_specs=[smem] * len(numbers)
        + [vmem] * len(ins)
        + [pl.BlockSpec(memory_space=pl.ANY)] * len(after),
        out_specs=[vmem] * len(outs),
        scratch_shapes=[pltpu.VMEM(shape, dtype) for shape, dtype in scratch],
        cost_estimate=pl.CostEstimate(
            flops=int(us * SCALE * 1.1e9), bytes_accessed=10**6, transcendentals=0
        ),
        compiler_params=pltpu.CompilerParams(vmem_limit_bytes=limit * 2**20),
    )(*numbers, *ins, *after)
    order.last = [got[-1]]
    return got


def dot(a, b):
    return jnp.dot(a, b, preferred_element_type=f32)


def dot_nt(a, b):
    return lax.dot_general(a, b, (((1,), (1,)), ((), ())), preferred_element_type=f32)


def dot_tn(a, b):
    return lax.dot_general(a, b, (((0,), (0,)), ((), ())), preferred_element_type=f32)


def mask_of(cells, rows, width, height, across, first_row=0):
    place = lax.broadcasted_iota(i32, (cells, 1), 0)
    column = lax.rem(place, width)
    row = lax.rem(lax.div(place, width), rows) + first_row
    return jnp.where((row < height) & (column < across), 1.0, 0.0).astype(f32)


def pool_matrix(frames, rows, width, up):
    cells, pooled = frames * rows * width, frames * rows * width // 8
    shape = (cells, pooled) if up else (pooled, cells)
    place = lax.broadcasted_iota(i32, shape, 0 if up else 1)
    target = lax.broadcasted_iota(i32, shape, 1 if up else 0)
    column = lax.rem(place, width) // 2
    row = lax.rem(lax.div(place, width), rows) // 2
    frame = lax.div(place, width * rows) // 2
    home = (frame * (rows // 2) + row) * (width // 2) + column
    return jnp.where(home == target, 0.125, 0.0).astype(bf16)


def moments(totals, inverse):
    mean = totals[0:1] * inverse
    variance = totals[1:2] * inverse - mean * mean
    return mean, lax.rsqrt(variance + epsilon)


def column_shift(x, width, by):
    cells = x.shape[0]
    column = lax.rem(lax.broadcasted_iota(i32, (cells, 1), 0), width)
    edge = 0 if by == 1 else width - 1
    return jnp.where(column == edge, 0.0, pltpu.roll(x, by % cells, 0))


def silu(active):
    return active * jax.nn.sigmoid(active)


def slope(active, upstream):
    sig = jax.nn.sigmoid(active)
    return upstream * sig * (1.0 + active * (1.0 - sig))


def sums(a, b):
    return jnp.concatenate(
        [jnp.sum(a, axis=0, keepdims=True), jnp.sum(a * b, axis=0, keepdims=True)], axis=0
    )


def box_mean(x, frames, rows, width):
    cells, channels = x.shape
    x = x + column_shift(x, width, 1) + column_shift(x, width, -1)
    x = x.reshape(frames, rows, width, channels)
    edge = jnp.zeros((frames, 1, width, channels), f32)
    x = (
        x
        + jnp.concatenate([edge, x[:, : rows - 1]], axis=1)
        + jnp.concatenate([x[:, 1:], edge], axis=1)
    )
    edge = jnp.zeros((1, rows, width, channels), f32)
    x = (
        x
        + jnp.concatenate([edge, x[: frames - 1]], axis=0)
        + jnp.concatenate([x[1:], edge], axis=0)
    )
    return x.reshape(cells, channels) * (1.0 / 27.0)


def place_bands(dst, blocks, slots, frames, rows, width):
    for turn, block in enumerate(blocks):
        part = block[...].astype(dst.dtype).reshape(frames, rows, width, dst.shape[-1])
        dst[:, pl.ds(slots[turn] * rows, rows)] = part


def fill_beside(beside, stems, frames, rows, width):
    beside[...] = jnp.zeros_like(beside)
    three = jnp.concatenate(
        [column_shift(stems, width, 1), stems, column_shift(stems, width, -1)], axis=1
    )
    three = three.astype(beside.dtype).reshape(frames, rows, width, 3 * STEMS)
    beside[1 : frames + 1, 1 : rows + 1, :, : 3 * STEMS] = three


def fill_conv_weights(flat, wide, thin):
    flat[...] = jnp.zeros_like(flat)
    for tap in range(27):
        row = (tap // 3) * BESIDE + (tap % 3) * STEMS
        flat[row : row + B1R, B2:] = wide[tap]
        flat[row + B1R : row + STEMS, :B2] = thin[tap]


def fill_back_weights(flat, wide, thin):
    flat[...] = jnp.zeros_like(flat)
    for tap in range(27):
        start = tap * 512
        flat[:B1R, start + B2 : start + SECOND] = wide[26 - tap]
        flat[B1R:, start : start + B2] = thin[26 - tap]


def fill_shifted(shifted, grad, frames, rows, width):
    shifted[...] = jnp.zeros_like(shifted)
    for dc in range(3):
        moved = grad if dc == 1 else column_shift(grad, width, 1 - dc)
        moved = moved.astype(shifted.dtype).reshape(frames, rows, width, SECOND)
        shifted[dc, 1 : frames + 1, 1 : rows + 1, :, :SECOND] = moved


def window(padded, f, r, frames, rows):
    part = padded[f : f + frames, r : r + rows]
    return part.reshape(frames * rows * part.shape[2], part.shape[3]).astype(bf16)


def conv_chunk(beside, flat, start, step, rows):
    taps = [window(beside, start + f, r, step, rows) for f in range(3) for r in range(3)]
    return dot(jnp.concatenate(taps, axis=1), flat[...])


def back_chunk(shifted, flat, start, step, rows):
    taps = [
        window(shifted.at[dc], start + f, r, step, rows)
        for f in range(3)
        for r in range(3)
        for dc in range(3)
    ]
    return dot_nt(jnp.concatenate(taps, axis=1), flat[...])


def pack_conv(slab, beside, dz, frames, rows, width, scale):
    cells = frames * rows * width
    half = 27 * B1R // 2
    for f in range(3):
        for r in range(3):
            part = window(beside, f, r, frames, rows)
            both = dot_tn(part, dz) * scale
            thin, wide = both[:, :B2], both[:, B2:]
            for c in range(3):
                tap = (f * 3 + r) * 3 + c
                rows_wide = wide[c * STEMS : c * STEMS + B1R].astype(bf16)
                slab[tap * B1R : (tap + 1) * B1R] = rows_wide[:, :128]
                at = 27 * B1R + tap * B1R
                slab[at : at + B1R] = rows_wide[:, 128:256]
                for piece in range(2):
                    row = tap * B1R + piece * 80
                    side = row >= half
                    at = 2 * 27 * B1R + row - (half if side else 0)
                    lanes = slice(64, 128) if side else slice(0, 64)
                    slab[at : at + 80, lanes] = rows_wide[piece * 80 : piece * 80 + 80, 256:]
                at = 2 * 27 * B1R + half + tap * B2R
                slab[at : at + B2R] = thin[c * STEMS + B1R : (c + 1) * STEMS].astype(bf16)


CONV_ROWS = 2 * 27 * B1R + 27 * B1R // 2 + 27 * B2R


def halved(n):
    return -(-n // (2 * GRANULE)) * GRANULE


def pack_matrix(slab, at, matrix):
    n, lanes = matrix.shape
    blocks, half = lanes // 128, halved(n)
    matrix = matrix.astype(bf16)
    for j in range(blocks):
        slab[at + j * n : at + (j + 1) * n] = matrix[:, j * 128 : (j + 1) * 128]
    at = at + blocks * n
    left, right = matrix[:half, blocks * 128 :], matrix[half:, blocks * 128 :]
    if n < 2 * half:
        right = jnp.concatenate([right, jnp.zeros((2 * half - n, 64), bf16)], axis=0)
    slab[at : at + half] = jnp.concatenate([left, right], axis=1)
    return at + half


def pack_norms(slab, at, gain, bias):
    rows = [row[:, j * 128 : (j + 1) * 128] for row in (gain, bias) for j in range(8)]
    slab[at : at + 16] = jnp.concatenate(rows, axis=0).astype(bf16)


def give_halves(slab, seg, mine, other):
    half = mine.shape[0]
    mine[...] = slab[pl.ds(seg * half, half)]
    other[...] = slab[pl.ds((1 - seg) * half, half)]


def unpack_conv(slab, wide_out, thin_out):
    half = 27 * B1R // 2
    for tap in range(27):
        at = tap * B1R
        wide_out[tap, :, :128] = slab[at : at + B1R].astype(f32)
        wide_out[tap, :, 128:256] = slab[27 * B1R + at : 27 * B1R + at + B1R].astype(f32)
        for piece in range(2):
            row = at + piece * 80
            side = row >= half
            start = 2 * 27 * B1R + row - (half if side else 0)
            part = slab[start : start + 80].astype(f32)
            part = part[:, 64:] if side else part[:, :64]
            wide_out[tap, piece * 80 : piece * 80 + 80, 256:] = part
        at = 2 * 27 * B1R + half + tap * B2R
        thin_out[tap] = slab[at : at + B2R].astype(f32)


def unpack_matrix(slab, at, n, lanes):
    blocks, half = lanes // 128, halved(n)
    parts = [slab[at + j * n : at + (j + 1) * n].astype(f32) for j in range(blocks)]
    at = at + blocks * n
    tail = slab[at : at + half].astype(f32)
    parts.append(jnp.concatenate([tail[:, :64], tail[: n - half, 64:]], axis=0))
    return parts, at + half


def matrix_rows(n, lanes):
    return lanes // 128 * n + halved(n)


def padded_rows(rows):
    unit = GRANULE * lax.axis_size("segment") * lax.axis_size("dp") * lax.axis_size("space")
    return -(-rows // unit) * unit


def split_sum(parts, pieces, row, at):
    rows = parts[0].shape[0] // pieces

    def body(row_ref, *refs):
        ins, outs = refs[: len(parts)], refs[len(parts) :]
        for k, out in enumerate(outs):
            start = (row_ref[at] ^ k) * rows if pieces > 1 else 0
            if pieces > 1:
                start = pl.multiple_of(start, GRANULE)
            total = ins[0][pl.ds(start, rows)].astype(f32)
            for ref in ins[1:]:
                total = total + ref[pl.ds(start, rows)].astype(f32)
            out[...] = total.astype(bf16)

    outs = [((rows, 128), bf16)] * pieces
    return call(body, outs, parts, [row], us=1.0, limit=32)


def joined(parts, row, at):
    rows, pieces = parts[0].shape[0], len(parts)

    def body(row_ref, *refs):
        for k, ref in enumerate(refs[:-1]):
            start = (row_ref[at] ^ k) * rows
            refs[-1][pl.ds(pl.multiple_of(start, GRANULE), rows)] = ref[...]

    outs = [((rows * pieces, 128), bf16)]
    return call(body, outs, parts, [row], us=1.0, limit=32)[0]


def swapped(x):
    return lax.ppermute(x, "segment", [(0, 1), (1, 0)])


class Slab:
    def __init__(self, mine, other, row):
        self.row, self.parts = row, [mine, swapped(other)]

    def to_dp(self):
        self.parts = exchanged(split_sum(self.parts, lax.axis_size("dp"), self.row, DP), "dp")

    def to_dp_again(self):
        pass

    def to_space(self):
        bands = lax.axis_size("space")
        self.parts = exchanged(split_sum(self.parts, bands, self.row, BAND), "space")

    def summed(self):
        self.parts = copies(split_sum(self.parts, 1, self.row, BAND)[0], "space")

    def to_shard(self):
        self.shard = split_sum(self.parts, 1, self.row, BAND)[0]

    def back_dp(self):
        held = copies(joined(self.parts, self.row, BAND), "dp")
        self.parts = held + [swapped(part) for part in held]

    def back_dp_again(self):
        pass

    def place(self, slab, pieces, row_ref):
        rows, peers = pieces[0].shape[0], len(pieces) // 2
        for k, piece in enumerate(pieces):
            side = row_ref[SEG] if k < peers else 1 - row_ref[SEG]
            at = (side * peers + (row_ref[DP] ^ (k % peers))) * rows
            slab[pl.ds(pl.multiple_of(at, GRANULE), rows)] = piece[...]


class CrossSlab(Slab):
    def to_dp(self):
        mine, got = self.parts
        self.quarter = mine.shape[0] // 4
        half, quarter = self.quarter // 2, self.quarter

        def body(row_ref, mine_ref, got_ref, to_x, to_y, keep_a, keep_b):
            y, x = lax.div(row_ref[DP], 2), lax.rem(row_ref[DP], 2)
            for k in range(2):
                to = slice(k * half, (k + 1) * half)
                for out, start in (
                    (to_x, (k * 2 + (1 - x)) * quarter),
                    (keep_a, (k * 2 + x) * quarter),
                    (to_y, ((1 - y) * 2 + k) * quarter + half),
                    (keep_b, (y * 2 + k) * quarter + half),
                ):
                    at = pl.ds(pl.multiple_of(start, GRANULE), half)
                    total = mine_ref[at].astype(f32) + got_ref[at].astype(f32)
                    out[to] = total.astype(out.dtype)

        send, keep = ((2 * half, 128), bf16), ((2 * half, 128), f32)
        to_x, to_y, *self.kept = call(
            body, [send, send, keep, keep], [mine, got], [self.row], us=1.3, limit=32
        )
        self.got = [lax.ppermute(to_x, "dp", pairing(4, 1)), lax.ppermute(to_y, "dp", pairing(4, 2))]

    def to_dp_again(self):
        half = self.quarter // 2

        def body(row_ref, keep_a, keep_b, got_a, got_b, send_a, send_b, next_a, next_b):
            y, x = lax.div(row_ref[DP], 2), lax.rem(row_ref[DP], 2)
            for keep, got, send, own, place in (
                (keep_a, got_a, send_a, next_a, y),
                (keep_b, got_b, send_b, next_b, x),
            ):
                at = pl.ds(pl.multiple_of(place * half, GRANULE), half)
                own[...] = keep[at] + got[at].astype(f32)
                at = pl.ds(pl.multiple_of((1 - place) * half, GRANULE), half)
                send[...] = (keep[at] + got[at].astype(f32)).astype(bf16)

        send, keep = ((half, 128), bf16), ((half, 128), f32)
        to_y, to_x, *self.kept = call(
            body, [send, send, keep, keep], self.kept + self.got, [self.row], us=1.0, limit=32
        )
        self.got = [lax.ppermute(to_y, "dp", pairing(4, 2)), lax.ppermute(to_x, "dp", pairing(4, 1))]

    def to_space(self):
        half, bands = self.quarter // 2, lax.axis_size("space")
        rows = self.quarter // bands

        def body(row_ref, keep_a, keep_b, got_a, got_b, own, *refs):
            outs, whole = refs[:-1], refs[-1]
            whole[:half] = keep_a[...] + got_a[...].astype(f32)
            whole[half:] = keep_b[...] + got_b[...].astype(f32)
            for k, out in enumerate((own,) + outs):
                at = pl.ds(pl.multiple_of((row_ref[BAND] ^ k) * rows, GRANULE), rows)
                out[...] = whole[at].astype(out.dtype)

        outs = [((rows, 128), f32)] + [((rows, 128), bf16)] * (bands - 1)
        scratch = [((self.quarter, 128), f32)]
        parts = call(body, outs, self.kept + self.got, [self.row], scratch, us=1.0, limit=32)
        self.parts = exchanged(parts, "space")

    def back_dp(self):
        half, bands = self.quarter // 2, lax.axis_size("space")
        rows = self.quarter // bands

        def body(row_ref, *refs):
            parts, (out_a, out_b, whole) = refs[:bands], refs[bands:]
            for k, ref in enumerate(parts):
                at = pl.ds(pl.multiple_of((row_ref[BAND] ^ k) * rows, GRANULE), rows)
                whole[at] = ref[...]
            out_a[...] = whole[:half]
            out_b[...] = whole[half:]

        outs, scratch = [((half, 128), bf16)] * 2, [((self.quarter, 128), bf16)]
        a, b = call(body, outs, self.parts, [self.row], scratch, us=1.0, limit=32)
        self.got = [lax.ppermute(a, "dp", pairing(4, 2)), lax.ppermute(b, "dp", pairing(4, 1))]
        self.kept = [a, b]

    def back_dp_again(self):
        half = self.quarter // 2

        def body(row_ref, own_a, own_b, got_a, got_b, pair_a, pair_b, both):
            y, x = lax.div(row_ref[DP], 2), lax.rem(row_ref[DP], 2)
            for own, got, out, place in ((own_a, got_a, pair_a, y), (own_b, got_b, pair_b, x)):
                out[pl.ds(pl.multiple_of(place * half, GRANULE), half)] = own[...]
                out[pl.ds(pl.multiple_of((1 - place) * half, GRANULE), half)] = got[...]
            both[: 2 * half] = pair_a[...]
            both[2 * half :] = pair_b[...]

        outs = [((2 * half, 128), bf16)] * 2 + [((4 * half, 128), bf16)]
        a, b, both = call(body, outs, self.kept + self.got, [self.row], us=1.0, limit=32)
        got = [lax.ppermute(a, "dp", pairing(4, 1)), lax.ppermute(b, "dp", pairing(4, 2))]
        self.parts = [both] + got + [swapped(part) for part in [both] + got]

    def place(self, slab, pieces, row_ref):
        half, quarter = self.quarter // 2, self.quarter
        y, x = lax.div(row_ref[DP], 2), lax.rem(row_ref[DP], 2)
        for turn, side in enumerate((row_ref[SEG], 1 - row_ref[SEG])):
            both, far_a, far_b = pieces[3 * turn : 3 * turn + 3]
            a, b = both.at[: 2 * half], both.at[2 * half :]
            for k in range(2):
                part = slice(k * half, (k + 1) * half)
                for ref, start in (
                    (a, (k * 2 + x) * quarter),
                    (far_a, (k * 2 + (1 - x)) * quarter),
                    (b, (y * 2 + k) * quarter + half),
                    (far_b, ((1 - y) * 2 + k) * quarter + half),
                ):
                    at = pl.multiple_of(side * 4 * quarter + start, GRANULE)
                    slab[pl.ds(at, half)] = ref[part]


class JointSlab(CrossSlab):
    def __init__(self, first, second, row):
        self.first, self.second, self.row = first, second, row

    def summed(self):
        shard, parts, bands = self.first.shard, self.second.parts, lax.axis_size("space")
        self.sizes = [shard.shape[0], parts[0].shape[0]]
        unit = sum(self.sizes)

        def body(first, *refs):
            refs[-1][: self.sizes[0]] = first[...]
            total = functools.reduce(jnp.add, [ref[...].astype(f32) for ref in refs[:-1]])
            refs[-1][self.sizes[0] :] = total.astype(bf16)

        (joint,) = call(body, [((unit, 128), bf16)], [shard] + parts, us=1.0, limit=32)
        self.quarter = unit * bands
        self.parts = copies(joint, "space")

    def place(self, slab, pieces, row_ref):
        bands, unit = lax.axis_size("space"), sum(self.sizes)
        half = self.quarter // 2
        y, x = lax.div(row_ref[DP], 2), lax.rem(row_ref[DP], 2)
        for turn, side in enumerate((row_ref[SEG], 1 - row_ref[SEG])):
            both, far_a, far_b = pieces[3 * turn : 3 * turn + 3]
            for k in range(2):
                for ref, at, quarter, second in (
                    (both, k * half, k * 2 + x, 0),
                    (far_a, k * half, k * 2 + (1 - x), 0),
                    (both, (2 + k) * half, y * 2 + k, 1),
                    (far_b, k * half, (1 - y) * 2 + k, 1),
                ):
                    for band in range(bands // 2):
                        base, start = 0, at + band * unit
                        for size in self.sizes:
                            place = (side * 4 + quarter) * bands + second * (bands // 2) + band
                            to = pl.multiple_of(base + place * size, GRANULE)
                            slab[pl.ds(to, size)] = ref[start : start + size]
                            base, start = base + 8 * bands * size, start + size


def widened(x):
    more = PADDED - x.shape[1]
    return jnp.concatenate([x, jnp.zeros((2, more), f32)], axis=1) if more else x


def pack_lanes(out, at, x):
    cells, channels = x.shape
    for start in range(0, channels, 128):
        part = x[:, start : start + 128]
        if part.shape[1] < 128:
            part = jnp.concatenate([part, jnp.zeros((cells, 128 - part.shape[1]), f32)], axis=1)
        out[at : at + cells] = part.astype(bf16)
        at += cells
    return at


def unpacked_lanes(ref, at, cells, channels):
    parts = []
    for start in range(0, channels, 128):
        parts.append(ref[at : at + cells, : min(128, channels - start)].astype(f32))
        at += cells
    return jnp.concatenate(parts, axis=1)


def shards(
    inputs,
    crop_group,
    in_proj_4f,
    conv_a_4f,
    conv_b_4f,
    gain_4f,
    bias_4f,
    in_proj_5b,
    conv_a_5b,
    conv_b_5b,
    gain_5b,
    bias_5b,
    out_grad,
):
    order.last = []
    segs, dps, bands = (lax.axis_size(axis) for axis in ("segment", "dp", "space"))
    micro, clips, frames, rows, width, channels = inputs.shape
    full_rows, all_clips = rows * bands, clips * dps
    halves = micro // segs
    held = halves * clips
    items = micro * clips
    spread = segs if items == segs * bands else 1
    assert segs == 2 and items == spread * bands and clips % spread == 0
    each = clips // spread
    cells, part_cells = frames * full_rows * width, frames * rows * width
    frames5, rows5, width5 = frames // 2, full_rows // 2, width // 2
    cells5, part_cells5 = cells // 8, part_cells // 8
    band_rows5 = rows // 2

    inward, pooled_in, outward = [], [], []
    for s in range(segs):
        for z in range(bands):
            for item in range(bands):
                inward.append((s * bands + z, s * bands + item, item, z))
    for m in range(micro):
        for c in range(clips):
            if spread > 1:
                holders = [(c // each) * bands + m * each + c % each]
            else:
                holders = [s * bands + m * clips + c for s in range(segs)]
            home, local = m // halves, (m % halves) * clips + c
            for z in range(bands):
                for holder in holders:
                    pooled_in.append((home * bands + z, holder, local, z))
                outward.append((holders[z % len(holders)], home * bands + z, z, local))
    inward, pooled_in, outward = (
        Route(edges, segs * bands) for edges in (inward, pooled_in, outward)
    )
    IN_BLOCK = TABLES
    IN_SLOT = IN_BLOCK + len(inward.rounds)
    POOLED_BLOCK = IN_SLOT + len(inward.rounds)
    POOLED_SLOT = POOLED_BLOCK + len(pooled_in.rounds)
    OUT_BLOCK = POOLED_SLOT + len(pooled_in.rounds)
    OUT_SLOT = OUT_BLOCK + len(outward.rounds)
    table = []
    for s in range(segs):
        for d in range(dps):
            for z in range(bands):
                me = s * bands + z
                first = s * each if spread > 1 else 0
                counted = 1 if spread > 1 or s == 0 else 0
                line = [s, d, z, first, z // each, counted]
                for route in (inward, pooled_in, outward):
                    line = line + route.blocks[me] + route.slots[me]
                table.append(line)
    row = jnp.array(table, i32)[lax.axis_index(("segment", "dp", "space"))]
    numbers = [row, crop_group]

    def group_parts(x):
        if each > 1:
            pairs = [[z * each + k for k in range(each)] for z in range(micro)]
            x = lax.psum(x, "space", axis_index_groups=pairs)
        if spread > 1:
            x = x + swapped(x)
        if dps > 4:
            return [lax.psum(x, "dp")]
        return copies(x, "dp")

    def total_of(refs):
        return functools.reduce(jnp.add, [ref[...] for ref in refs])

    def crop(row_ref, group_ref, scale=1, m=None):
        group = group_ref[row_ref[MY_MICRO] if m is None else m]
        tall, wide = full_rows // scale, width // scale
        height, across = tall - group * (tall // 4), wide - group * (wide // 4)
        count = all_clips * (frames // scale) * height * across
        return height, across, 1.0 / jnp.full((1, 1), count, i32).astype(f32)

    LEAD, OUTER, STEM = slice(0, B0), slice(0, C_MID), slice(C_MID, None)
    RESTS = slice(B0, C_MID)
    wide4, thin4 = conv_a_4f.reshape(27, B1R, B1), conv_b_4f.reshape(27, B2R, B2)
    wide5, thin5 = conv_a_5b.reshape(27, B1R, B1), conv_b_5b.reshape(27, B2R, B2)

    def prepared(fill, shape, wide, thin):
        def body(wide_ref, thin_ref, flat):
            fill(flat, wide_ref, thin_ref)

        return call(body, [shape], [wide, thin], us=1.2)[0]

    forward_shape, back_shape = ((9 * BESIDE, SECOND), bf16), ((STEMS, 27 * 512), bf16)

    def project_body(row_ref, group_ref, x_ref, p_ref, stat, pool, *outs):
        for k in range(bands):
            item = row_ref[IN_BLOCK + k]
            m, c = lax.div(item, each), row_ref[FIRST_CLIP] + lax.rem(item, each)
            x = x_ref[m, c].reshape(part_cells, channels)
            height, across, _ = crop(row_ref, group_ref, 1, m)
            mask = mask_of(part_cells, rows, width, height, across, row_ref[BAND] * rows)
            z = dot(x, p_ref[:, B0:]) * mask
            stem = z[:, :STEMS]
            outs[k][...] = stem.astype(bf16)
            pool[k] = z[:, STEMS:].astype(bf16)
            stat[item] = sums(stem, stem)

    got = call(
        project_body,
        [((bands, 2, STEMS), f32), ((bands, part_cells, BP), bf16)]
        + [((part_cells, STEMS), bf16)] * bands,
        [inputs, in_proj_4f],
        numbers,
        us=1.5,
    )
    stem_stat, pool_parts, stem_parts = got[0], got[1], got[2:]
    stem_blocks = inward.send(stem_parts)

    def home_crop(row_ref, group_ref, i):
        m = row_ref[SEG] * halves + i // clips
        height, across, inverse = crop(row_ref, group_ref, 1, m)
        first = row_ref[BAND] * rows
        return m, mask_of(part_cells, rows, width, height, across, first), inverse

    lanes5 = -(-C_MID // 128)
    carried = part_cells + lanes5 * part_cells5

    def lead_body(row_ref, group_ref, x_ref, p_ref, stem_stat, pool, upper, *refs):
        lead_out, stem_out, stat, outs = refs[0], refs[1], refs[2], refs[3:]
        for i in range(held):
            m, mask, _ = home_crop(row_ref, group_ref, i)
            x = x_ref[m, i % clips].reshape(part_cells, channels)
            z = dot(x, p_ref[:, :STEM_END]) * mask
            lead = z[:, :B0]
            lead_out[i] = lead
            stem_out[i] = z[:, B0:]
            total = sums(lead, lead)
            j = bands + i // clips
            stat[j] = total if i % clips == 0 else stat[j] + total
        for k in range(bands):
            stat[k] = widened(stem_stat[k])
            item = row_ref[IN_BLOCK + k]
            m, c = lax.div(item, each), row_ref[FIRST_CLIP] + lax.rem(item, each)
            outs[k][:part_cells] = pool[k]
            pack_lanes(outs[k], part_cells, upper[m, c].astype(f32).reshape(part_cells5, C_MID))

    got = call(
        lead_body,
        [
            ((held, part_cells, B0), f32),
            ((held, part_cells, STEMS), f32),
            ((bands + halves, 2, PADDED), f32),
        ]
        + [((carried, 128), bf16)] * bands,
        [inputs, in_proj_4f, stem_stat, pool_parts, out_grad],
        numbers,
        us=2.5,
    )
    lead, home_stem, stat = got[:3]

    def all_parts(x, axis):
        return [lax.psum(x, axis)] if lax.axis_size(axis) > 4 else copies(x, axis)

    def whole_body(*refs):
        refs[-1][...] = total_of(refs[:-1])

    def summed_dp(x):
        parts = all_parts(x, "dp")
        return call(whole_body, [(x.shape, f32)], parts, us=0.8)[0]

    def share_body(row_ref, own, other, *outs):
        for k, out in enumerate(outs):
            item = row_ref[BAND] ^ k
            first = lax.div(item, each) * each
            total = jnp.zeros((2, PADDED), f32)
            for c in range(each):
                total = total + own[first + c]
                if spread > 1:
                    total = total + other[first + c]
            out[0] = total
            for j in range(halves):
                out[1 + j] = own[bands + j]

    stat = summed_dp(stat)
    stat_parts = call(
        share_body,
        [((1 + halves, 2, PADDED), f32)] * bands,
        [stat, swapped(stat)],
        [row],
        us=0.8,
    )
    stat_parts = exchanged(stat_parts, "space")
    carried_blocks = inward.send(got[3:])

    def arrange_body(gain4, bias4, gain5, bias5, p4, p5, affine4, affine5, proj4, proj5):
        for gain, bias, out in ((gain4, bias4, affine4), (gain5, bias5, affine5)):
            for k, ref in enumerate((gain, bias)):
                v = ref[...]
                out[k : k + 1] = jnp.concatenate(
                    [
                        v[:, :B0],
                        v[:, STEM_END:FIRST],
                        v[:, FIRST + B1 :],
                        v[:, FIRST : FIRST + B1],
                        v[:, B0:STEM_END],
                    ],
                    axis=1,
                )
        proj4[:, :B0] = p4[:, :B0]
        proj4[:, B0:] = jnp.concatenate([p4[:, STEM_END:], p4[:, B0:STEM_END]], axis=1)
        for first, last, to in ((0, B0, 0), (STEM_END, FIRST, B0), (B0, STEM_END, B0 + BP)):
            rows_in = p5[first:last]
            proj5[to : to + last - first, :B0] = rows_in[:, :B0]
            proj5[to : to + last - first, B0:] = jnp.concatenate(
                [
                    rows_in[:, B0 + SECOND :],
                    rows_in[:, B0 + B1 : B0 + SECOND],
                    rows_in[:, B0 : B0 + B1],
                ],
                axis=1,
            )

    affine4, affine5, proj4, proj5 = call(
        arrange_body,
        [((2, 1024), f32)] * 2 + [((channels, FIRST), bf16), ((FIRST, C_MID), bf16)],
        [v.reshape(1, -1) for v in (gain_4f, bias_4f, gain_5b, bias_5b)]
        + [in_proj_4f, in_proj_5b.T],
        us=2.0,
    )

    def lead_act(i, lead_ref, stat_ref, affine_ref, inverse):
        mean, scale = moments(stat_ref[i // clips], inverse)
        norm = (lead_ref[i] - mean) * scale
        return norm, scale, norm * affine_ref[0:1, LEAD] + affine_ref[1:2, LEAD]

    def lead_out_body(row_ref, group_ref, lead_ref, affine_ref, *refs):
        parts, stat_ref, outs, kept = refs[:bands], refs[bands], refs[bands + 1 : -1], refs[-1]
        stat_ref[...] = total_of(parts)[1:]
        matrix = pool_matrix(frames, rows, width, False)
        for i in range(held):
            _, mask, inverse = home_crop(row_ref, group_ref, i)
            _, _, active = lead_act(i, lead_ref, stat_ref, affine_ref, inverse)
            kept[i] = dot(matrix, (silu(active) * mask).astype(bf16)).astype(bf16)
        for turn, out in enumerate(outs):
            out[...] = kept[row_ref[POOLED_BLOCK + turn]]

    got = call(
        lead_out_body,
        [((halves, 2, B0), f32)] + [((part_cells5, B0), bf16)] * len(pooled_in.rounds),
        [lead, affine4] + stat_parts,
        numbers,
        [((held, part_cells5, B0), bf16)],
        us=1.8,
    )
    lead_stat = got[0]
    lead_pooled = pooled_in.send(got[1:])

    step = 2 if full_rows * width <= 128 else 1

    def conv_body(row_ref, group_ref, affine_ref, wide_ref, thin_ref, *refs):
        stats, blocks = refs[:bands], refs[bands : 2 * bands]
        second_out, sums_out, norm_out, stat_out, beside, stage, flat = refs[2 * bands :]
        height, across, inverse = crop(row_ref, group_ref)
        totals = functools.reduce(jnp.add, [ref[0] for ref in stats])[:, :STEMS]
        mean, scale = moments(totals, inverse)
        stat_out[...] = totals
        fill_conv_weights(flat, wide_ref, thin_ref)
        slots = [row_ref[IN_SLOT + k] for k in range(bands)]
        place_bands(stage, blocks, slots, frames, rows, width)
        mask = mask_of(cells, full_rows, width, height, across)
        norm = (stage[...].reshape(cells, STEMS) - mean) * scale
        norm_out[...] = norm
        active = norm * affine_ref[0:1, STEM] + affine_ref[1:2, STEM]
        fill_beside(beside, silu(active) * mask, frames, full_rows, width)
        chunk = step * full_rows * width
        total = jnp.zeros((2, SECOND), f32)
        for start in range(0, frames, step):
            got = conv_chunk(beside, flat, start, step, full_rows)
            second_out[start * full_rows * width : start * full_rows * width + chunk] = got
            total = total + sums(got * mask[:chunk], got)
        sums_out[...] = total

    second, second_sums, stem_norm, stem_total, beside = call(
        conv_body,
        [
            ((cells, SECOND), f32),
            ((2, SECOND), f32),
            ((cells, STEMS), f32),
            ((2, STEMS), f32),
            ((frames + 2, full_rows + 2, width, BESIDE), bf16),
        ],
        [affine4, wide4, thin4] + stat_parts + stem_blocks,
        numbers,
        [
            ((frames, full_rows, width, STEMS), f32),
            ((9 * BESIDE, SECOND), bf16),
        ],
        us=9.0,
    )

    def pool_body(row_ref, group_ref, second_sums, *refs):
        blocks, (zp_out, sums_out, stage) = refs[:bands], refs[bands:]
        height, across, _ = crop(row_ref, group_ref)
        slots = [row_ref[IN_SLOT + k] for k in range(bands)]
        place_bands(stage, [ref.at[:part_cells] for ref in blocks], slots, frames, rows, width)
        zp = box_mean(stage[...].reshape(cells, BP), frames, full_rows, width)
        zp_out[...] = zp
        mask = mask_of(cells, full_rows, width, height, across)
        sums_out[...] = jnp.concatenate([sums(zp * mask, zp), second_sums[...]], axis=1)

    zp, rest_sums = call(
        pool_body,
        [((cells, BP), f32), ((2, REST), f32)],
        [second_sums] + carried_blocks,
        numbers,
        [((frames, full_rows, width, BP), f32)],
        us=1.3,
    )
    rest_parts = group_parts(rest_sums)
    n_parts = len(rest_parts)

    span = 2 * full_rows * width

    def rest_of(zp_ref, second_ref, start, affine_ref, mean, scale):
        z = jnp.concatenate(
            [zp_ref[start : start + span], second_ref[start : start + span]], axis=1
        )
        norm = (z - mean) * scale
        return norm, norm * affine_ref[0:1, RESTS] + affine_ref[1:2, RESTS]

    def middle_body(row_ref, group_ref, affine_ref, p_ref, zp_ref, second_ref, *refs):
        parts, leads = refs[:n_parts], refs[n_parts:-6]
        stat_out, pooled, first_out, sums_out, stage, kept = refs[-6:]
        height, across, inverse = crop(row_ref, group_ref)
        mean, scale = moments(total_of(parts), inverse)
        stat_out[...] = jnp.concatenate([mean, scale], axis=0)
        mask = mask_of(span, full_rows, width, height, across)
        matrix = pool_matrix(2, full_rows, width, False)
        slots = [row_ref[POOLED_SLOT + k] for k in range(len(leads))]
        place_bands(stage, leads, slots, frames5, band_rows5, width5)
        pooled[:, :B0] = stage[...].reshape(cells5, B0).astype(bf16)
        for f in range(frames5):
            _, active = rest_of(zp_ref, second_ref, f * span, affine_ref, mean, scale)
            out = dot(matrix, (silu(active) * mask).astype(bf16))
            pooled[f * span // 8 : (f + 1) * span // 8, B0:] = out.astype(bf16)
        z = dot_nt(pooled[...], p_ref[...])
        kept[...] = z
        project = z[:, LEAD.stop : LEAD.stop + BP].astype(bf16).astype(f32)
        kept[:, B0 : B0 + BP] = box_mean(project, frames5, rows5, width5)
        z = kept[...]
        first_out[...] = z
        height, across, _ = crop(row_ref, group_ref, 2)
        sums_out[...] = sums(z * mask_of(cells5, rows5, width5, height, across), z)

    rest_stat, pooled, first5, first5_sums = call(
        middle_body,
        [((2, REST), f32), ((cells5, C_MID), bf16), ((cells5, FIRST), f32), ((2, FIRST), f32)],
        [affine4, proj5, zp, second] + rest_parts + lead_pooled,
        numbers,
        [((frames5, rows5, width5, B0), f32), ((cells5, FIRST), f32)],
    )
    first5_parts = group_parts(first5_sums)

    flat5 = prepared(fill_conv_weights, forward_shape, wide5, thin5)

    def conv5_body(row_ref, group_ref, affine_ref, flat, first_ref, *refs):
        parts = refs[:n_parts]
        second_out, sums_out, stat_out, beside = refs[n_parts:]
        height, across, inverse = crop(row_ref, group_ref, 2)
        mean, scale = moments(total_of(parts), inverse)
        stat_out[...] = jnp.concatenate([mean, scale], axis=0)
        mask = mask_of(cells5, rows5, width5, height, across)
        stem = slice(B0 + BP, FIRST)
        norm = (first_ref[:, stem] - mean[:, stem]) * scale[:, stem]
        active = norm * affine_ref[0:1, STEM] + affine_ref[1:2, STEM]
        fill_beside(beside, silu(active) * mask, frames5, rows5, width5)
        got = conv_chunk(beside, flat, 0, frames5, rows5)
        second_out[...] = got
        sums_out[...] = sums(got * mask, got)

    second5, second5_sums, first5_stat, beside5 = call(
        conv5_body,
        [
            ((cells5, SECOND), f32),
            ((2, SECOND), f32),
            ((2, FIRST), f32),
            ((frames5 + 2, rows5 + 2, width5, BESIDE), f32),
        ],
        [affine5, flat5, first5] + first5_parts,
        numbers,
    )
    second5_parts = group_parts(second5_sums)

    def out5_body(row_ref, group_ref, affine_ref, first_ref, stat_ref, second_ref, *refs):
        parts, uppers = refs[:n_parts], refs[n_parts : n_parts + bands]
        out, norm_out, slope_out, scale_out, sums_out, stage = refs[n_parts + bands :]
        height, across, inverse = crop(row_ref, group_ref, 2)
        mean2, scale2 = moments(total_of(parts), inverse)
        mask = mask_of(cells5, rows5, width5, height, across)
        outer = slice(0, B0 + BP)
        mean = jnp.concatenate([stat_ref[0:1, outer], mean2], axis=1)
        scale = jnp.concatenate([stat_ref[1:2, outer], scale2], axis=1)
        z = jnp.concatenate([first_ref[:, outer], second_ref[...]], axis=1)
        norm = (z - mean) * scale
        active = norm * affine_ref[0:1, OUTER] + affine_ref[1:2, OUTER]
        act = silu(active) * mask
        natural = [act[:, :B0], act[:, B0 + BP + B2 :], act[:, B0 + BP : B0 + BP + B2]]
        natural = jnp.concatenate(natural + [act[:, B0 : B0 + BP]], axis=1)
        out[...] = natural.reshape(frames5, rows5, width5, C_MID)
        for k, ref in enumerate(uppers):
            part = unpacked_lanes(ref, part_cells, part_cells5, C_MID)
            part = part.reshape(frames5, band_rows5, width5, C_MID)
            stage[:, pl.ds(row_ref[IN_SLOT + k] * band_rows5, band_rows5)] = part
        upper = stage[...].reshape(cells5, C_MID)
        upper = jnp.concatenate(
            [
                upper[:, :B0],
                upper[:, B0 + SECOND :],
                upper[:, B0 + B1 : B0 + SECOND],
                upper[:, B0 : B0 + B1],
            ],
            axis=1,
        )
        slopes = slope(active, upper * mask)
        norm_out[...] = norm
        slope_out[...] = slopes
        scale_out[...] = scale
        sums_out[...] = sums(slopes, norm)

    out5, outer5_norm, outer5_slope, outer5_scale, outer5_sums = call(
        out5_body,
        [
            ((frames5, rows5, width5, C_MID), f32),
            ((cells5, C_MID), f32),
            ((cells5, C_MID), f32),
            ((1, C_MID), f32),
            ((2, C_MID), f32),
        ],
        [affine5, first5, first5_stat, second5] + second5_parts + carried_blocks,
        numbers,
        [((frames5, rows5, width5, C_MID), f32)],
        us=1.4,
    )
    outer5_parts = group_parts(outer5_sums)

    back_flat5 = prepared(fill_back_weights, back_shape, wide5, thin5)

    def back5_body(row_ref, group_ref, affine_ref, flat, *refs):
        norm_ref, slope_ref, scale_ref, first_ref, stat_ref = refs[:5]
        parts, refs = refs[5 : 5 + n_parts], refs[5 + n_parts :]
        dz_out, lead_out, project_out, slope_out, sums_out, shifted = refs
        height, across, inverse = crop(row_ref, group_ref, 2)
        mask = mask_of(cells5, rows5, width5, height, across)
        total = total_of(parts) * inverse
        grad = (mask * (affine_ref[0:1, OUTER] * scale_ref[...])) * (
            slope_ref[...] - total[0:1] - norm_ref[...] * total[1:2]
        )
        lead_out[...] = grad[:, :B0]
        low = grad[:, B0:].astype(bf16)
        dz = low[:, BP:]
        dz_out[...] = dz
        project_out[...] = box_mean(low[:, :BP].astype(f32), frames5, rows5, width5)
        fill_shifted(shifted, dz.astype(f32), frames5, rows5, width5)
        upper = back_chunk(shifted, flat, 0, frames5, rows5)
        stem = slice(B0 + BP, FIRST)
        norm = (first_ref[:, stem] - stat_ref[0:1, stem]) * stat_ref[1:2, stem]
        active = norm * affine_ref[0:1, STEM] + affine_ref[1:2, STEM]
        slopes = slope(active, upper * mask)
        slope_out[...] = slopes
        sums_out[...] = sums(slopes, norm)

    dz5, lead5_grad, project5_grad, stem5_slope, stem5_sums = call(
        back5_body,
        [
            ((cells5, SECOND), bf16),
            ((cells5, B0), f32),
            ((cells5, BP), f32),
            ((cells5, STEMS), f32),
            ((2, STEMS), f32),
        ],
        [affine5, back_flat5, outer5_norm, outer5_slope, outer5_scale, first5, first5_stat]
        + outer5_parts,
        numbers,
        [
            ((3, frames5 + 2, rows5 + 2, width5, 512), f32),
        ],
    )
    back_flat4 = prepared(fill_back_weights, back_shape, wide4, thin4)
    stem5_parts = group_parts(stem5_sums)

    def rest_slope(f, pooled_grad, matrix, mask, zp_ref, second_ref, affine_ref, stat_ref):
        norm, active = rest_of(
            zp_ref, second_ref, f * span, affine_ref, stat_ref[0:1], stat_ref[1:2]
        )
        upper = dot(matrix, pooled_grad[f * span // 8 : (f + 1) * span // 8])
        return norm, slope(active, upper * mask)

    def first5_body(row_ref, group_ref, affine_ref, affine4_ref, p_ref, *refs):
        lead_ref, project_ref, slope_ref, first_ref, stat_ref = refs[:5]
        zp_ref, second_ref, rest_stat = refs[5:8]
        parts, refs = refs[8 : 8 + n_parts], refs[8 + n_parts :]
        lead_out, projected_out, rest_out, sums_out = refs
        height, across, inverse = crop(row_ref, group_ref, 2)
        mask = mask_of(cells5, rows5, width5, height, across)
        total = total_of(parts) * inverse
        stem = slice(B0 + BP, FIRST)
        norm = (first_ref[:, stem] - stat_ref[0:1, stem]) * stat_ref[1:2, stem]
        stem_grad = (mask * (affine_ref[0:1, STEM] * stat_ref[1:2, stem])) * (
            slope_ref[...] - total[0:1] - norm * total[1:2]
        )
        projected = jnp.concatenate([lead_ref[...], project_ref[...], stem_grad], axis=1)
        projected = projected.astype(bf16)
        projected_out[...] = projected
        pooled_grad = dot(projected, p_ref[...]).astype(bf16)
        lead_out[...] = pooled_grad[:, :B0].astype(f32).reshape(frames5, rows5, width5, B0)
        rest_grad = pooled_grad[:, B0:]
        rest_out[...] = rest_grad
        height, across, _ = crop(row_ref, group_ref)
        mask = mask_of(span, full_rows, width, height, across)
        matrix = pool_matrix(2, full_rows, width, True)
        total = jnp.zeros((2, REST), f32)
        for f in range(frames5):
            norm, slopes = rest_slope(
                f, rest_grad, matrix, mask, zp_ref, second_ref, affine4_ref, rest_stat
            )
            total = total + sums(slopes, norm)
        sums_out[...] = total

    lead_grad5, projected5_grad, rest_upper, rest_grad_sums = call(
        first5_body,
        [
            ((frames5, rows5, width5, B0), f32),
            ((cells5, FIRST), bf16),
            ((cells5, REST), bf16),
            ((2, REST), f32),
        ],
        [affine5, affine4, proj5, lead5_grad, project5_grad, stem5_slope, first5, first5_stat]
        + [zp, second, rest_stat]
        + stem5_parts,
        numbers,
        us=2.4,
    )
    rest_grad_parts = group_parts(rest_grad_sums)

    def natural(outer, stem):
        pool, thin, wide = (
            outer[:, B0 : B0 + BP],
            outer[:, B0 + BP : B0 + BP + B2],
            outer[:, B0 + BP + B2 :],
        )
        return jnp.concatenate([outer[:, :B0], stem, pool, wide, thin], axis=1)

    rows_5b = padded_rows(CONV_ROWS + matrix_rows(FIRST, C_MID) + 16)

    def weights5_body(row_ref, beside, dz_ref, pooled_ref, projected_ref, *refs):
        outer_ref, stem_ref, mine, other, slab = refs
        scale = jnp.full((1, 1), row_ref[COUNTED], i32).astype(f32)
        pack_conv(slab, beside, dz_ref[...], frames5, rows5, width5, scale)
        at = pack_matrix(slab, CONV_ROWS, dot_tn(projected_ref[...], pooled_ref[...]) * scale)
        norms = natural(outer_ref[...], stem_ref[...]) * scale
        pack_norms(slab, at, norms[1:2], norms[0:1])
        slab[at + 16 :] = jnp.zeros((rows_5b - at - 16, 128), bf16)
        give_halves(slab, row_ref[SEG], mine, other)

    mine5, other5 = call(
        weights5_body,
        [((rows_5b // 2, 128), bf16)] * 2,
        [beside5, dz5, pooled, projected5_grad, outer5_sums, stem5_sums],
        [row],
        [((rows_5b, 128), bf16)],
        us=3.6,
    )
    slab5 = (CrossSlab if dps == 4 else Slab)(mine5, other5, row)

    slab5.to_dp()
    def back4_body(row_ref, group_ref, affine_ref, zp_ref, second_ref, stat_ref, grad_ref, *refs):
        parts, (out5_ref, lead_ref), refs = refs[:n_parts], refs[n_parts : n_parts + 2], refs[n_parts + 2 :]
        outs, (dz_out, kept) = refs[: len(outward.rounds)], refs[len(outward.rounds) :]
        height, across, inverse = crop(row_ref, group_ref)
        mask = mask_of(span, full_rows, width, height, across)
        total = total_of(parts) * inverse
        matrix = pool_matrix(2, full_rows, width, True)
        factor = affine_ref[0:1, RESTS] * stat_ref[1:2]
        for f in range(frames5):
            norm, slopes = rest_slope(
                f, grad_ref, matrix, mask, zp_ref, second_ref, affine_ref, stat_ref
            )
            grad = (mask * factor) * (slopes - total[0:1] - norm * total[1:2])
            low = grad.astype(bf16)
            dz_out[f * span : (f + 1) * span] = low[:, BP:]
            kept[2 * f : 2 * f + 2] = low[:, :BP].astype(f32).reshape(2, full_rows, width, BP)
        pool = box_mean(kept[...].reshape(cells, BP), frames, full_rows, width)
        kept[...] = pool.reshape(frames, full_rows, width, BP)
        for turn, out in enumerate(outs):
            part = kept[:, pl.ds(row_ref[OUT_BLOCK + turn] * rows, rows)]
            out[:part_cells] = part.reshape(part_cells, BP).astype(bf16)
            start = row_ref[OUT_BLOCK + turn] * band_rows5
            part = lead_ref[:, pl.ds(start, band_rows5)].reshape(part_cells5, B0)
            at = pack_lanes(out, part_cells, part)
            part = out5_ref[:, pl.ds(start, band_rows5)].reshape(part_cells5, C_MID)
            pack_lanes(out, at, part)

    carried_out = carried + B0 // 128 * part_cells5
    got = call(
        back4_body,
        [((carried_out, 128), bf16)] * len(outward.rounds) + [((cells, SECOND), bf16)],
        [affine4, zp, second, rest_stat, rest_upper] + rest_grad_parts + [out5, lead_grad5],
        numbers,
        [((frames, full_rows, width, BP), f32)],
        us=2.6,
    )
    carried_grads = outward.send(got[: len(outward.rounds)])
    dz = got[-1]

    rows_conv = padded_rows(CONV_ROWS)

    def weights4_body(row_ref, beside, dz_ref, mine, other, slab):
        scale = jnp.full((1, 1), row_ref[COUNTED], i32).astype(f32)
        pack_conv(slab, beside, dz_ref[...], frames, full_rows, width, scale)
        slab[CONV_ROWS:] = jnp.zeros((rows_conv - CONV_ROWS, 128), bf16)
        give_halves(slab, row_ref[SEG], mine, other)

    mine4, other4 = call(
        weights4_body,
        [((rows_conv // 2, 128), bf16)] * 2,
        [beside, dz],
        [row],
        [((rows_conv, 128), bf16)],
        us=10.5,
    )
    slab4 = (CrossSlab if dps == 4 else Slab)(mine4, other4, row)

    slab5.to_dp_again()
    def stems4_body(row_ref, group_ref, affine_ref, flat, dz_ref, norm_ref, *refs):
        outs, refs = refs[: len(outward.rounds)], refs[len(outward.rounds) :]
        sums_out, shifted, kept = refs
        height, across, _ = crop(row_ref, group_ref)
        fill_shifted(shifted, dz_ref[...].astype(f32), frames, full_rows, width)
        chunk = step * full_rows * width
        mask = mask_of(chunk, full_rows, width, height, across)
        total = jnp.zeros((2, STEMS), f32)
        for start in range(0, frames, step):
            upper = back_chunk(shifted, flat, start, step, full_rows)
            at = start * full_rows * width
            norm = norm_ref[at : at + chunk]
            active = norm * affine_ref[0:1, STEM] + affine_ref[1:2, STEM]
            slopes = slope(active, upper * mask)
            kept[start : start + step] = slopes.reshape(step, full_rows, width, STEMS)
            total = total + sums(slopes, norm)
        sums_out[...] = total
        for turn, out in enumerate(outs):
            part = kept[:, pl.ds(row_ref[OUT_BLOCK + turn] * rows, rows)]
            out[...] = part.reshape(part_cells, STEMS).astype(bf16)

    got = call(
        stems4_body,
        [((part_cells, STEMS), bf16)] * len(outward.rounds)
        + [((2, STEMS), f32)],
        [affine4, back_flat4, dz, stem_norm],
        numbers,
        [
            ((3, frames + 2, full_rows + 2, width, 512), bf16),
            ((frames, full_rows, width, STEMS), f32),
        ],
        us=9.0,
    )
    stem_slopes = outward.send(got[: len(outward.rounds)])
    stem_sums = got[-1]

    def lead_slopes(i, row_ref, group_ref, lead_ref, stat_ref, affine_ref, matrix, kept):
        _, mask, inverse = home_crop(row_ref, group_ref, i)
        norm, scale, active = lead_act(i, lead_ref, stat_ref, affine_ref, inverse)
        upper = dot(matrix, kept[i])
        return mask, inverse, scale, norm, slope(active, upper * mask)

    def lead_back_body(row_ref, group_ref, lead_ref, stat_ref, affine_ref, stem_ref, *refs):
        blocks, (sums_out, kept, out) = refs[:held], refs[held:]
        matrix = pool_matrix(frames, rows, width, True)
        for turn, ref in enumerate(blocks):
            place = row_ref[OUT_SLOT + turn]
            at = part_cells + B0 // 128 * part_cells5
            part = unpacked_lanes(ref, part_cells, part_cells5, B0)
            kept[place] = part.astype(bf16)
            part = unpacked_lanes(ref, at, part_cells5, C_MID)
            out[place] = part.reshape(frames5, band_rows5, width5, C_MID).astype(bf16)
        for i in range(held):
            _, _, _, norm, slopes = lead_slopes(
                i, row_ref, group_ref, lead_ref, stat_ref, affine_ref, matrix, kept
            )
            total = sums(slopes, norm)
            j = 1 + i // clips
            sums_out[j] = total if i % clips == 0 else sums_out[j] + total
        sums_out[0] = widened(stem_ref[...])

    last_sums, lead_upper, block_out = call(
        lead_back_body,
        [
            ((1 + halves, 2, PADDED), f32),
            ((held, part_cells5, B0), bf16),
            ((held, frames5, band_rows5, width5, C_MID), bf16),
        ],
        [lead, lead_stat, affine4, stem_sums] + carried_grads,
        numbers,
        us=2.0,
    )
    block_out = block_out.reshape(halves, clips, frames5, band_rows5, width5, C_MID)

    slab4.to_dp()
    last = summed_dp(last_sums)
    if each > 1:
        pairs = [[z * each + k for k in range(each)] for z in range(micro)]
        last = jnp.concatenate(
            [lax.psum(last[:1], "space", axis_index_groups=pairs), last[1:]], axis=0
        )

    def last_body(own, other, stat, out):
        total = own[0]
        if spread > 1:
            total = total + other[0]
        out[0] = total
        out[1 : 1 + halves] = own[1:]
        out[1 + halves] = widened(stat[...])

    (last,) = call(
        last_body,
        [((2 + halves, 2, PADDED), f32)],
        [last, swapped(last), stem_total],
        us=0.8,
    )
    last_parts = copies(last, "space")

    slab5.to_space()
    slab4.to_dp_again()
    rows_proj = padded_rows(matrix_rows(channels, FIRST) + 16)

    def first4_body(row_ref, group_ref, x_ref, affine_ref, lead_ref, stat_ref, *refs):
        upper_ref, stem_ref, last_sums, rest_sums = refs[:4]
        parts, refs = refs[4 : 4 + bands], refs[4 + bands :]
        slopes_in, pools_in, refs = refs[:held], refs[held : 2 * held], refs[2 * held :]
        projected, mine, other, x_all, slab, late, stem_all = refs
        lead_total = functools.reduce(
            jnp.add, [ref[1 : 1 + halves] for ref in parts]
        )
        matrix = pool_matrix(frames, rows, width, True)
        for turn in range(held):
            place = row_ref[OUT_SLOT + turn]
            late[place, :, :BP] = pools_in[turn][:part_cells].astype(f32)
            late[place, :, BP:] = slopes_in[turn][...].astype(f32)
        for k in range(bands):
            stem_all[k, 0] = parts[k][0]
            stem_all[k, 1] = parts[k][1 + halves]
        for i in range(held):
            mask, inverse, scale, norm, slopes = lead_slopes(
                i, row_ref, group_ref, lead_ref, stat_ref, affine_ref, matrix, upper_ref
            )
            total = lead_total[i // clips] * inverse
            lead_grad = (affine_ref[0:1, LEAD] * scale) * (
                slopes - total[0:1] - norm * total[1:2]
            )
            m = row_ref[SEG] * halves + i // clips
            turn = row_ref[BAND] ^ (m * each)
            mean, scale = moments(stem_all[turn, 1][:, :STEMS], inverse)
            total = stem_all[turn, 0][:, :STEMS] * inverse
            norm = (stem_ref[i] - mean) * scale
            stem_grad = (affine_ref[0:1, STEM] * scale) * (
                late[i, :, BP:] - total[0:1] - norm * total[1:2]
            )
            grad = jnp.concatenate([lead_grad, late[i, :, :BP], stem_grad], axis=1) * mask
            at = i * part_cells
            projected[at : at + part_cells] = grad.astype(bf16)
            x_all[at : at + part_cells] = x_ref[m, i % clips].reshape(part_cells, channels)
        at = pack_matrix(slab, 0, dot_tn(x_all[...], projected[...]))
        counted = jnp.full((1, 1), row_ref[COUNTED], i32).astype(f32)
        own = jnp.sum(last_sums[1:], axis=0)
        rest = rest_sums[...] * counted
        stem = last_sums[0][:, :STEMS] * counted
        norms = natural(jnp.concatenate([own, rest], axis=1), stem)
        pack_norms(slab, at, norms[1:2], norms[0:1])
        slab[at + 16 :] = jnp.zeros((rows_proj - at - 16, 128), bf16)
        give_halves(slab, row_ref[SEG], mine, other)

    projected_grad, mine_proj, other_proj = call(
        first4_body,
        [((held * part_cells, FIRST), bf16)] + [((rows_proj // 2, 128), bf16)] * 2,
        [inputs, affine4, lead, lead_stat, lead_upper, home_stem, last_sums, rest_grad_sums]
        + last_parts
        + stem_slopes
        + carried_grads,
        numbers,
        [
            ((held * part_cells, channels), bf16),
            ((rows_proj, 128), bf16),
            ((held, part_cells, BP + STEMS), f32),
            ((bands, 2, 2, PADDED), f32),
        ],
        us=4.0,
    )
    slab_proj = Slab(mine_proj, other_proj, row)
    joint = JointSlab(slab4, slab_proj, row) if dps == 4 else None

    slab4.to_space()
    slab5.summed()
    def input_body(projected_ref, p_ref, out):
        for i in range(held):
            at = i * part_cells
            got = dot_nt(projected_ref[at : at + part_cells], p_ref[...])
            out[i // clips, i % clips] = got.reshape(frames, rows, width, channels)

    mark = order.last
    (input_grad,) = call(
        input_body,
        [((halves, clips, frames, rows, width, channels), f32)],
        [projected_grad, proj4],
    )
    order.last = mark

    slab_proj.to_dp()
    slab5.back_dp()
    slab_proj.to_space()
    if joint is None:
        slab4.summed()
    else:
        slab4.to_shard()
    if joint is None:
        slab_proj.summed()
    else:
        joint.summed()
    slab5.back_dp_again()
    if joint is None:
        slab4.back_dp()
        slab_proj.back_dp()
    else:
        joint.back_dp()
    if joint is not None:
        joint.back_dp_again()
    def unpacked(way, n_rows, body, outs, us):
        pieces = way.parts

        def whole(row_ref, *refs):
            slab = refs[-1]
            way.place(slab, refs[: len(pieces)], row_ref)
            body(slab, *refs[len(pieces) : -1])

        scratch = [((n_rows, 128), bf16)]
        return call(whole, outs, pieces, [row], scratch, us=us, limit=48)

    conv_outs = [((27, B1R, B1), f32), ((27, B2R, B2), f32)]

    def unpack_proj(slab, proj_out, gain_out, bias_out):
        parts, at = unpack_matrix(slab, 0, channels, FIRST)
        proj_out[:, :128] = parts[0]
        proj_out[:, 128:256] = parts[1]
        proj_out[:, 256:] = jnp.concatenate([parts[3], parts[4], parts[2]], axis=1)
        norms = slab[at : at + 16].astype(f32)
        gain_out[...] = norms[:8]
        bias_out[...] = norms[8:]

    def unpack5(slab, wide_out, thin_out, proj5_out, gain_out, bias_out):
        unpack_conv(slab, wide_out, thin_out)
        parts, at = unpack_matrix(slab, CONV_ROWS, FIRST, C_MID)
        lead = parts[:2]
        tail = jnp.concatenate([parts[6], parts[3], parts[2]], axis=1)
        for first, last, place in ((0, B0, 0), (B0, B0 + BP, STEM_END), (B0 + BP, FIRST, B0)):
            to = slice(place, place + last - first)
            proj5_out[to, 0:128] = lead[0][first:last]
            proj5_out[to, 128:256] = lead[1][first:last]
            proj5_out[to, 256:384] = parts[4][first:last]
            proj5_out[to, 384:512] = parts[5][first:last]
            proj5_out[to, 512:] = tail[first:last]
        norms = slab[at : at + 16].astype(f32)
        gain_out[...] = norms[:8]
        bias_out[...] = norms[8:]


    wide5_grad, thin5_grad, proj5_grad, gain5_grad, bias5_grad = unpacked(
        slab5,
        rows_5b,
        unpack5,
        conv_outs + [((FIRST, C_MID), f32)] + [((8, 128), f32)] * 2,
        5.0,
    )

    proj_outs = [((channels, FIRST), f32)] + [((8, 128), f32)] * 2
    if joint is not None:
        wide4_grad, thin4_grad, proj4_grad, gain4_grad, bias4_grad = unpacked(
            joint,
            rows_conv + rows_proj,
            lambda slab, *outs: (
                unpack_conv(slab, *outs[:2]),
                unpack_proj(slab.at[rows_conv:], *outs[2:]),
            ),
            conv_outs + proj_outs,
            5.5,
        )
    else:
        wide4_grad, thin4_grad = unpacked(slab4, rows_conv, unpack_conv, conv_outs, 4.0)
        proj4_grad, gain4_grad, bias4_grad = unpacked(slab_proj, rows_proj, unpack_proj, proj_outs, 2.0)


    return (
        block_out,
        input_grad,
        proj4_grad,
        wide4_grad.reshape(conv_a_4f.shape),
        thin4_grad.reshape(conv_b_4f.shape),
        gain4_grad.reshape(-1),
        bias4_grad.reshape(-1),
        proj5_grad.T,
        wide5_grad.reshape(conv_a_5b.shape),
        thin5_grad.reshape(conv_b_5b.shape),
        gain5_grad.reshape(-1),
        bias5_grad.reshape(-1),
    )


def solution(mesh):
    banded = P(None, "dp", None, "space", None, None)
    halved_specs = P("segment", "dp", None, "space", None, None)
    in_specs = (banded,) + (P(),) * 11 + (banded,)
    out_specs = (halved_specs, halved_specs) + (P(),) * 10
    return jax.shard_map(shards, mesh=mesh, in_specs=in_specs, out_specs=out_specs, check_vma=False)
```
